512 devices in a mesh: grp: 8 (over y_lo, x), dev: 64 (over z, y_hi, core).
Axes of the slice: x: 4, y: 4 (y_hi: 2, y_lo: 2; y = y_hi * 2 + y_lo), z: 16, core: 2. Of those that a mesh axis runs over, the one named last changes fastest.
Arguments:
- stream: bfloat16 [2048, 4096], P('grp'), may hold values from -6 to 6
- row_length: int32 [16], P('grp'), may hold values from 1 to 128, as said below
- row_start: int32 [16], P('grp'), may hold values from 0 to 2047
- attn_gain: float32 [4096], replicated, may hold values from 0.1 to 1.9
- w_query: bfloat16 [4096, 4096], P('grp', 'dev'), as said below
- w_key: bfloat16 [4096, 1024], P('grp', 'dev'), may hold values from -0.09375 to 0.09375
- w_value: bfloat16 [4096, 1024], P('grp', 'dev'), may hold values from -0.09375 to 0.09375
- w_out: bfloat16 [4096, 4096], P('grp', 'dev'), may hold values from -0.09375 to 0.09375
- ffn_gain: float32 [4096], replicated, may hold values from 0.1 to 1.9
- w_gate: bfloat16 [4096, 14336], P('grp', 'dev'), may hold values from -0.09375 to 0.09375
- w_up: bfloat16 [4096, 14336], P('grp', 'dev'), may hold values from -0.09375 to 0.09375
- w_down: bfloat16 [4096, 14336], P('grp', 'dev'), may hold values from -0.046875 to 0.046875
Outputs:
- key_cache: bfloat16 [2048, 1024], P('grp', 'dev')
- value_cache: bfloat16 [2048, 1024], P('grp', 'dev')
- next_stream: bfloat16 [2048, 4096], P('grp', 'dev')
The draws below stay inside these ranges and needn't reach their ends.
Inputs may be any that keep to these rules, and one draw needn't show every extreme that they name: `row_length`: in every draw some row holds all 128 slots cached and some row only one. `row_start`: position of each row's first slot. `w_query`: query projection with independent entries.
All inputs are finite; a program needn't handle non-finite values.
Results may differ from the reference program's by a relative error of at most 0.011.
The reference program's roundings to bfloat16 on the way (of `normed`, `probs`, `mixed`, `attended`, `normed2` and `hidden`) count: a program that leaves them out, or rounds other values in their place, can miss the bound.
Values may be sent and summed in bfloat16 or wider, within the bound.
No kernel may reach another device: no remote copies, remote signals or barrier semaphores. Data moves between devices by JAX's collectives and lax.ppermute only.
A program may use at most 64 MiB of HBM per device.

```python
import math
import jax
import jax.numpy as jnp
from jax import lax

D = 4096
FF = 14336
HEADS = 32
KV_HEADS = 8
HEAD_DIM = 128
ROW_LEN = 128
KVD = 1024
ALL_ROWS = 16
TOKENS = 2048


def draw_w_query(key, part):
    key = jax.random.fold_in(key, 11)
    factor = 1.0
    entries = jax.random.normal(key, (D, D), jnp.float32)
    return (entries * (factor / math.sqrt(D))).astype(jnp.bfloat16)


def draw_row_length(key, part):
    key = jax.random.fold_in(key, 23)
    first_key, second_key = jax.random.split(key)
    lengths = jax.random.randint(first_key, (ALL_ROWS,), 1, ROW_LEN + 1)
    order = jax.random.permutation(second_key, ALL_ROWS)
    lengths = lengths.at[order[0]].set(ROW_LEN)
    lengths = lengths.at[order[1]].set(1)
    return lengths.astype(jnp.int32)


def place_ends(result, own_key, least, top_value):
    extent = result.shape
    index_at = [jax.random.randint(jax.random.fold_in(own_key, axis), (), 0, extent[axis]) for axis in range(len(extent))]
    result = result.at[tuple(index_at)].set(least)
    longest = extent.index(max(extent))
    index_at[longest] = (index_at[longest] + 1) % extent[longest]
    return result.at[tuple(index_at)].set(top_value)


def level_of(key, dims, pieces, smallest, high):
    def one(axis_at, shards_of):
        steps = jax.random.uniform(jax.random.fold_in(jax.random.fold_in(key, 6), axis_at), (shards_of,), jnp.float32, smallest / len(pieces), high / len(pieces))
        return jnp.repeat(jnp.exp(steps), dims[axis_at] // shards_of).reshape((-1,) + (1,) * (len(dims) - axis_at - 1))

    loudness = one(*pieces[0])
    for cut in pieces[1:]:
        loudness = loudness * one(*cut)
    return loudness


def gaussian(rng, extent, deviation, most, pieces=(), kind=jnp.bfloat16):
    values = deviation * jax.random.normal(rng, extent, jnp.float32)
    if pieces:
        values = values * level_of(rng, extent, pieces, -0.22, 0.18)
    return jnp.clip(values, -most, most).astype(kind)


def setup_inputs(seed: int = 0) -> dict:
    arg_keys = jax.random.split(jax.random.key(seed), 13)
    stream = gaussian(arg_keys[0], (TOKENS, D), 1.0, 6.0, ((0, 8),))
    row_length = draw_row_length(jax.random.fold_in(arg_keys[12], 71), 0)
    row_start = place_ends(jax.random.randint(arg_keys[2], (ALL_ROWS,), 0, 2048), jax.random.fold_in(arg_keys[2], 1), 0, 2047).astype(jnp.int32)
    attn_gain = jnp.clip(1.0 + 0.18 * jax.random.normal(arg_keys[3], (D,), jnp.float32), 0.1, 1.9)
    w_query = draw_w_query(jax.random.fold_in(arg_keys[12], 71), 0)
    w_key = gaussian(arg_keys[5], (D, KVD), D ** -0.5, 0.09375, ((0, 8), (1, 64)))
    w_value = gaussian(arg_keys[6], (D, KVD), D ** -0.5, 0.09375, ((0, 8), (1, 64)))
    w_out = gaussian(arg_keys[7], (D, D), D ** -0.5, 0.09375, ((0, 8), (1, 64)))
    ffn_gain = jnp.clip(1.0 + 0.18 * jax.random.normal(arg_keys[8], (D,), jnp.float32), 0.1, 1.9)
    w_gate = gaussian(arg_keys[9], (D, FF), D ** -0.5, 0.09375, ((0, 8), (1, 64)))
    w_up = gaussian(arg_keys[10], (D, FF), D ** -0.5, 0.09375, ((0, 8), (1, 64)))
    w_down = gaussian(arg_keys[11], (D, FF), FF ** -0.5, 0.046875, ((0, 8), (1, 64)))
    return {"stream": stream, "row_length": row_length, "row_start": row_start, "attn_gain": attn_gain, "w_query": w_query, "w_key": w_key, "w_value": w_value, "w_out": w_out, "ffn_gain": ffn_gain, "w_gate": w_gate, "w_up": w_up, "w_down": w_down}


rope_base = 500000.0

def norm_rows(values, gain):
    return values * lax.rsqrt(lax.optimization_barrier(jnp.mean(values * values, axis=-1, keepdims=True)) + 1e-05) * gain

def rotate(values, positions, first):
    cols = first + jnp.arange(values.shape[1], dtype=jnp.int32)
    pair = (cols % HEAD_DIM // 2).astype(jnp.float32)
    freq = jnp.exp(-(2.0 * pair / HEAD_DIM) * math.log(rope_base))
    angle = positions.astype(jnp.float32)[:, None] * freq[None, :]
    lead = values.reshape(values.shape[0], -1, 2)
    partner = jnp.stack([-lead[..., 1], lead[..., 0]], axis=-1).reshape(values.shape)
    return values * jnp.cos(angle) + partner * jnp.sin(angle)

def attend_row(packed):
    queries, keys, values, length = packed
    group = HEADS // KV_HEADS
    count = queries.shape[0]
    qh = queries.astype(jnp.float32).reshape(count, KV_HEADS, group, HEAD_DIM)
    kh = keys.astype(jnp.float32).reshape(-1, KV_HEADS, HEAD_DIM)
    vh = values.astype(jnp.float32).reshape(-1, KV_HEADS, HEAD_DIM)
    scores = jnp.einsum('qkgd,jkd->kgqj', qh, kh) / math.sqrt(HEAD_DIM)
    query_pos = jnp.arange(count, dtype=jnp.int32)
    key_pos = jnp.arange(keys.shape[0], dtype=jnp.int32)
    allowed = (key_pos[None, :] <= query_pos[:, None]) & (key_pos[None, :] < length)
    scores = jnp.where(allowed, scores, -jnp.inf)
    top = lax.optimization_barrier(jnp.max(scores, axis=-1, keepdims=True))
    expo = jnp.exp(scores - top)
    probs = (expo / lax.optimization_barrier(jnp.sum(expo, axis=-1, keepdims=True))).astype(jnp.bfloat16)
    mixed = jnp.einsum('kgqj,jkd->qkgd', probs.astype(jnp.float32), vh)
    return mixed.astype(jnp.bfloat16).reshape(count, -1)

def reference(stream, row_length, row_start, attn_gain, w_query, w_key, w_value, w_out, ffn_gain, w_gate, w_up, w_down):
    positions = (row_start[:, None] + jnp.arange(ROW_LEN, dtype=jnp.int32)[None, :]).reshape(-1)
    normed = norm_rows(stream.astype(jnp.float32), attn_gain).astype(jnp.bfloat16)
    queries = rotate(jnp.dot(normed, w_query, preferred_element_type=jnp.float32), positions, 0).astype(jnp.bfloat16)
    keys = rotate(jnp.dot(normed, w_key, preferred_element_type=jnp.float32), positions, 0).astype(jnp.bfloat16)
    values = jnp.dot(normed, w_value, preferred_element_type=jnp.float32).astype(jnp.bfloat16)
    mixed = lax.map(attend_row, (queries.reshape(ALL_ROWS, ROW_LEN, D), keys.reshape(ALL_ROWS, ROW_LEN, KVD), values.reshape(ALL_ROWS, ROW_LEN, KVD), row_length))
    mixed = mixed.reshape(TOKENS, D)
    attended = (stream.astype(jnp.float32) + jnp.dot(mixed, w_out, preferred_element_type=jnp.float32)).astype(jnp.bfloat16)
    normed2 = norm_rows(attended.astype(jnp.float32), ffn_gain).astype(jnp.bfloat16)
    gate = jnp.dot(normed2, w_gate, preferred_element_type=jnp.float32)
    up = jnp.dot(normed2, w_up, preferred_element_type=jnp.float32)
    hidden = (jax.nn.silu(gate) * up).astype(jnp.bfloat16)
    down = lax.dot_general(hidden, w_down, (((1,), (1,)), ((), ())), preferred_element_type=jnp.float32)
    next_stream = (attended.astype(jnp.float32) + down).astype(jnp.bfloat16)
    return (keys, values, next_stream)
```

```python
import functools
import math

import jax
import jax.numpy as jnp
from jax import lax
from jax.experimental import pallas as pl
from jax.experimental.pallas import tpu as pltpu
from jax.sharding import PartitionSpec as P

HEADS = 32
KV_HEADS = 8
HEAD_DIM = 128
ROW_LEN = 128
D = 4096
ROPE_BASE = 500000.0

GROUPS = 8
MEMBERS = 64
DEPTH = 16
HALF = 64
QC = 64
KC = 16
FC = 224
BAND = 256
RUN = 512

COLUMNS = [[4 * z + q for z in range(DEPTH)] for q in range(4)]
QUADS = [[4 * z + q for q in range(4)] for z in range(DEPTH)]
OCTETS = [[8 * z + m for m in range(8)] for z in range(8)]

BF = jnp.bfloat16
F32 = jnp.float32
VMEM = pl.BlockSpec(memory_space=pltpu.VMEM)
SMEM = pl.BlockSpec(memory_space=pltpu.SMEM)


def nt(a, b):
    return lax.dot_general(a, b, (((1,), (1,)), ((), ())), preferred_element_type=F32)


def params(mib):
    return pltpu.CompilerParams(vmem_limit_bytes=mib * 2**20)


def cost(flops, nbytes):
    return pl.CostEstimate(flops=flops, bytes_accessed=nbytes, transcendentals=0)


def project_kernel(at, stream, gain, weights, cos, sin, send, keys, values, own):
    x = stream[...].astype(F32)
    scale = lax.rsqrt(jnp.mean(x * x, axis=-1, keepdims=True) + 1e-05)
    total = jnp.zeros((256, 96), F32)
    for g in range(GROUPS):
        cols = pl.ds(g * RUN, RUN)
        part = stream[:, cols].astype(F32) * scale * gain[:, cols]
        total = total + nt(part.astype(BF), weights[g, 0:96, :])
    total = jnp.concatenate([total, jnp.zeros((256, 32), F32)], axis=1)
    lane = lax.broadcasted_iota(jnp.int32, (256, 128), 1)
    partner = jnp.where(lane % 2 == 0, -pltpu.roll(total, 127, 1), pltpu.roll(total, 1, 1))
    turned = jnp.where(lane < QC + KC, total * cos[...] + partner * sin[...], total)
    turned = turned.astype(BF).astype(F32)
    flipped = turned.T
    keys[...] = flipped[QC : QC + KC, :].astype(BF)
    values[...] = flipped[QC + KC : QC + 2 * KC, :].astype(BF)
    lane = lax.broadcasted_iota(jnp.int32, (HALF, 128), 1)
    for zl in range(2):
        for yhi in range(2):
            for c in range(2):
                first = turned[c * 128 : c * 128 + HALF, :]
                second = turned[c * 128 + HALF : c * 128 + 128, :]
                mine = second if yhi else first
                chunk = jnp.where(lane < QC, mine, jnp.where(lane < 96, first, pltpu.roll(second, 32, 1)))
                send[zl * 4 + yhi * 2 + c] = chunk.astype(BF)
    rows = pl.ds(pl.multiple_of(at[0] * 128 + at[1] * HALF, HALF), HALF)
    own[...] = stream[rows, pl.ds(pl.multiple_of(at[2] * BAND, BAND), BAND)]


def attend_kernel(at, got, out):
    lane = lax.broadcasted_iota(jnp.int32, (HALF, 128), 1)
    pieces = [got[m].astype(F32) for m in range(8)]

    def gather(start):
        full = jnp.zeros((HALF, 128), F32)
        for m in range(8):
            full = jnp.where(lane // KC == m, pltpu.roll(pieces[m], (KC * m - start) % 128, 1), full)
        return full.astype(BF)

    keys = jnp.concatenate([gather(QC), gather(96)], axis=0)
    values = jnp.concatenate([gather(QC + KC), gather(96 + KC)], axis=0)
    slot = lax.broadcasted_iota(jnp.int32, (HALF, 128), 0) + at[1] * HALF
    allowed = (lane <= slot) & (lane < at[4])
    for a in range(2):
        low = got[at[3] * 4 + a * 2].astype(F32)
        high = got[at[3] * 4 + a * 2 + 1].astype(F32)
        queries = jnp.where(lane < QC, low, pltpu.roll(high, QC, 1)).astype(BF)
        scores = nt(queries, keys) / math.sqrt(HEAD_DIM)
        scores = jnp.where(allowed, scores, -jnp.inf)
        expo = jnp.exp(scores - jnp.max(scores, axis=-1, keepdims=True))
        probs = (expo / jnp.sum(expo, axis=-1, keepdims=True)).astype(BF)
        mixed = jnp.dot(probs, values, preferred_element_type=F32).astype(BF)
        for z in range(DEPTH):
            out[z, :, a * 128 : a * 128 + 128] = mixed


def output_kernel(at, got, mine, core, far, cross, own, out):
    parts = []
    for w in (mine, core, far, cross):
        total = jnp.zeros((HALF, QC), F32)
        for g in range(GROUPS):
            total = total + nt(got[2 * g], w[g, :, 0:BAND]) + nt(got[2 * g + 1], w[g, :, BAND:RUN])
        parts.append(total)
    blocks = []
    for j in range(4):
        picked = parts[0]
        for k in range(1, 4):
            picked = jnp.where(jnp.bitwise_xor(at[5], j) == k, parts[k], picked)
        blocks.append(picked)
    projected = jnp.concatenate(blocks, axis=1)
    attended = (own[...].astype(F32) + projected).astype(BF)
    for z in range(DEPTH):
        out[z] = attended


def hidden_kernel(got, gain, mine, core, out, normed, totals):
    g = pl.program_id(0)

    @pl.when(g == 0)
    def _():
        squares = jnp.zeros((HALF, 1), F32)
        for z in range(DEPTH):
            x = got[z].astype(F32)
            squares = squares + jnp.sum(x * x, axis=-1, keepdims=True)
        scale = lax.rsqrt(squares * (1.0 / D) + 1e-05)
        for z in range(DEPTH):
            x = got[z].astype(F32) * scale * gain[:, z * BAND : (z + 1) * BAND]
            normed[z // 2, :, (z % 2) * BAND : (z % 2 + 1) * BAND] = x.astype(BF)
        totals[...] = jnp.zeros_like(totals)

    x = normed[g]
    for i, w in enumerate((mine, core)):
        totals[i, 0] += nt(x, w[0, 0:FC, :])
        totals[i, 1] += nt(x, w[0, FC : 2 * FC, :])

    @pl.when(g == GROUPS - 1)
    def _():
        for i in range(2):
            gate = totals[i, 0]
            out[i] = (gate / (1.0 + jnp.exp(-gate)) * totals[i, 1]).astype(BF)


def down_kernel(hidden, mine, core, out):
    total = jnp.dot(hidden[0], mine[0], preferred_element_type=F32)
    total = total + jnp.dot(hidden[1], core[0], preferred_element_type=F32)
    out[0] = total[:, 0:BAND].astype(out.dtype)
    out[1] = total[:, BAND:RUN].astype(out.dtype)


def finish_kernel(got, attended, out):
    total = got[0].astype(F32)
    for z in range(1, DEPTH):
        total = total + got[z].astype(F32)
    result = (attended[0].astype(F32) + total).T
    for q in range(4):
        out[q] = result[q * QC : (q + 1) * QC, :].astype(BF)


def project(at, stream, gain, weights, cos, sin):
    return pl.pallas_call(
        project_kernel,
        out_shape=(
            jax.ShapeDtypeStruct((8, HALF, 128), BF),
            jax.ShapeDtypeStruct((KC, 256), BF),
            jax.ShapeDtypeStruct((KC, 256), BF),
            jax.ShapeDtypeStruct((HALF, BAND), BF),
        ),
        in_specs=[SMEM] + [VMEM] * 5,
        out_specs=(VMEM,) * 4,
        compiler_params=params(32),
        name="project",
    )(at, stream, gain, weights, cos, sin)


def attend(at, got):
    return pl.pallas_call(
        attend_kernel,
        out_shape=jax.ShapeDtypeStruct((DEPTH, HALF, BAND), BF),
        in_specs=[SMEM, VMEM],
        out_specs=VMEM,
        compiler_params=params(16),
        name="attend",
    )(at, got)


def output(at, got, weights, own):
    return pl.pallas_call(
        output_kernel,
        out_shape=jax.ShapeDtypeStruct((DEPTH, HALF, BAND), BF),
        in_specs=[SMEM] + [VMEM] * 6,
        out_specs=VMEM,
        compiler_params=params(24),
        name="output",
    )(at, got, *weights, own)


def hidden_units(got, gain, mine, core):
    block = pl.BlockSpec((1, 2 * FC, RUN), lambda g: (g, 0, 0))
    return pl.pallas_call(
        hidden_kernel,
        grid=(GROUPS,),
        out_shape=jax.ShapeDtypeStruct((2, HALF, FC), BF),
        in_specs=[
            pl.BlockSpec((DEPTH, HALF, BAND), lambda g: (0, 0, 0)),
            pl.BlockSpec((1, D), lambda g: (0, 0)),
            block,
            block,
        ],
        out_specs=pl.BlockSpec((2, HALF, FC), lambda g: (0, 0, 0)),
        scratch_shapes=[pltpu.VMEM((GROUPS, HALF, RUN), BF), pltpu.VMEM((2, 2, HALF, FC), F32)],
        compiler_params=params(24),
        cost_estimate=cost(2 * HALF * D * 4 * FC, 8 * 2**20),
        name="hidden",
    )(got, gain, mine, core)


def down(hidden, mine, core, dtype):
    block = pl.BlockSpec((1, FC, RUN), lambda g: (g, 0, 0))
    return pl.pallas_call(
        down_kernel,
        grid=(GROUPS,),
        out_shape=jax.ShapeDtypeStruct((DEPTH, HALF, BAND), dtype),
        in_specs=[pl.BlockSpec((2, HALF, FC), lambda g: (0, 0, 0)), block, block],
        out_specs=pl.BlockSpec((2, HALF, BAND), lambda g: (g, 0, 0)),
        compiler_params=params(24),
        cost_estimate=cost(2 * HALF * D * 2 * FC, 5 * 2**20),
        name="down",
    )(hidden, mine, core)


def finish(got, attended):
    return pl.pallas_call(
        finish_kernel,
        out_shape=jax.ShapeDtypeStruct((4, QC, HALF), BF),
        in_specs=[VMEM, VMEM],
        out_specs=VMEM,
        compiler_params=params(16),
        name="finish",
    )(got, attended)


def swap(x, bits):
    return lax.ppermute(x, "dev", [(d, d ^ bits) for d in range(MEMBERS)])


def trade(x, groups):
    return lax.all_to_all(x, "dev", 0, 0, axis_index_groups=groups, tiled=True)


def on_device(
    stream,
    row_length,
    row_start,
    attn_gain,
    w_query,
    w_key,
    w_value,
    w_out,
    ffn_gain,
    w_gate,
    w_up,
    w_down,
):
    member = lax.axis_index("dev")
    core, yhi, z, quad = member % 2, member // 2 % 2, member // 4, member % 4
    length = jnp.where(core == 0, row_length[0], row_length[1])
    at = jnp.stack([core, yhi, z, z % 2, length, quad]).astype(jnp.int32)

    first = jnp.concatenate([w_query.T, w_key.T, w_value.T, w_out.T], axis=0)
    first = lax.all_to_all(jnp.broadcast_to(first[None], (GROUPS, 160, RUN)), "grp", 0, 0, tiled=True)
    out_own = first[:, 96:160, :]
    out_weights = (out_own, swap(out_own, 1), swap(out_own, 2), swap(out_own, 3))

    widen = lax.all_gather(jnp.concatenate([w_gate.T, w_up.T], axis=0), "grp", axis=0)
    narrow = lax.all_gather(w_down.T, "grp", axis=0)
    widen_core = swap(widen, 1)
    narrow_core = swap(narrow, 1)

    lane = jnp.arange(128, dtype=jnp.int32)
    column = jnp.where(lane < QC, member * QC + lane, member * KC + lane - QC)
    pair = (column % HEAD_DIM // 2).astype(F32)
    freq = jnp.exp(-(2.0 * pair / HEAD_DIM) * math.log(ROPE_BASE))
    positions = (row_start[:, None] + jnp.arange(ROW_LEN, dtype=jnp.int32)[None, :]).reshape(-1)
    angle = positions.astype(F32)[:, None] * freq[None, :]

    send, keys, values, own = project(
        at, stream, attn_gain.reshape(1, D), first, jnp.cos(angle), jnp.sin(angle)
    )
    mixed = trade(attend(at, trade(send, OCTETS)), COLUMNS)
    attended = output(at, mixed, out_weights, own)
    full = trade(attended, COLUMNS)
    far = swap(full, 2)
    gain = ffn_gain.reshape(1, D)
    hidden = hidden_units(full, gain, widen, widen_core)
    far_hidden = hidden_units(far, gain, widen, widen_core)
    far_sum = swap(down(far_hidden, narrow, narrow_core, BF), 2)
    total = down(hidden, narrow, narrow_core, F32)
    total = (total + far_sum.astype(F32)).astype(BF)
    blocks = trade(finish(trade(total, COLUMNS), attended), QUADS)
    next_stream = blocks.reshape(2, 2, QC, HALF).transpose(1, 0, 3, 2).reshape(256, QC)
    return (keys.T, values.T, next_stream)


def solution(mesh):
    placed = (
        P("grp", None),
        P("grp"),
        P("grp"),
        P(),
        P("grp", "dev"),
        P("grp", "dev"),
        P("grp", "dev"),
        P("grp", "dev"),
        P(),
        P("grp", "dev"),
        P("grp", "dev"),
        P("grp", "dev"),
    )
    return jax.shard_map(
        on_device,
        mesh=mesh,
        in_specs=placed,
        out_specs=(P("grp", "dev"), P("grp", "dev"), P("grp", "dev")),
        check_vma=False,
    )
```

```python
import math

import jax
import jax.numpy as jnp
from jax import lax
from jax.experimental import pallas as pl
from jax.experimental.pallas import tpu as pltpu
from jax.sharding import PartitionSpec as P

HEADS = 32
KV_HEADS = 8
HEAD_DIM = 128
ROW_LEN = 128
D = 4096
ROPE_BASE = 500000.0

GROUPS = 8
MEMBERS = 64
DEPTH = 16
HALF = 64
QC = 64
KC = 16
FC = 224
BAND = 256
RUN = 512

COLUMNS = [[4 * z + q for z in range(DEPTH)] for q in range(4)]
OCTETS = [[8 * z + m for m in range(8)] for z in range(8)]

BF = jnp.bfloat16
F32 = jnp.float32
VMEM = pl.BlockSpec(memory_space=pltpu.VMEM)
SMEM = pl.BlockSpec(memory_space=pltpu.SMEM)


def nt(a, b):
    return lax.dot_general(a, b, (((1,), (1,)), ((), ())), preferred_element_type=F32)


def params(mib):
    return pltpu.CompilerParams(vmem_limit_bytes=mib * 2**20)


def cost(flops, nbytes):
    return pl.CostEstimate(flops=flops, bytes_accessed=nbytes, transcendentals=0)


def project_kernel(at, stream, gain, weights, cos, sin, send, keys, values, own):
    x = stream[...].astype(F32)
    scale = lax.rsqrt(jnp.mean(x * x, axis=-1, keepdims=True) + 1e-05)
    total = jnp.zeros((256, 96), F32)
    for g in range(GROUPS):
        cols = pl.ds(g * RUN, RUN)
        part = stream[:, cols].astype(F32) * scale * gain[:, cols]
        total = total + nt(part.astype(BF), weights[g, 0:96, :])
    total = jnp.concatenate([total, jnp.zeros((256, 32), F32)], axis=1)
    lane = lax.broadcasted_iota(jnp.int32, (256, 128), 1)
    partner = jnp.where(lane % 2 == 0, -pltpu.roll(total, 127, 1), pltpu.roll(total, 1, 1))
    turned = jnp.where(lane < QC + KC, total * cos[...] + partner * sin[...], total)
    turned = turned.astype(BF).astype(F32)
    flipped = turned.T
    keys[...] = flipped[QC : QC + KC, :].astype(BF)
    values[...] = flipped[QC + KC : QC + 2 * KC, :].astype(BF)
    lane = lax.broadcasted_iota(jnp.int32, (HALF, 128), 1)
    for zl in range(2):
        for yhi in range(2):
            for c in range(2):
                first = turned[c * 128 : c * 128 + HALF, :]
                second = turned[c * 128 + HALF : c * 128 + 128, :]
                mine = second if yhi else first
                chunk = jnp.where(lane < QC, mine, jnp.where(lane < 96, first, pltpu.roll(second, 32, 1)))
                send[zl * 4 + yhi * 2 + c] = chunk.astype(BF)
    rows = pl.ds(pl.multiple_of(at[0] * 128 + at[1] * HALF, HALF), HALF)
    own[...] = stream[rows, pl.ds(pl.multiple_of(at[2] * BAND, BAND), BAND)]


def attend_kernel(at, got, out):
    lane = lax.broadcasted_iota(jnp.int32, (HALF, 128), 1)
    pieces = [got[m].astype(F32) for m in range(8)]

    def gather(start):
        full = jnp.zeros((HALF, 128), F32)
        for m in range(8):
            full = jnp.where(lane // KC == m, pltpu.roll(pieces[m], (KC * m - start) % 128, 1), full)
        return full.astype(BF)

    keys = jnp.concatenate([gather(QC), gather(96)], axis=0)
    values = jnp.concatenate([gather(QC + KC), gather(96 + KC)], axis=0)
    slot = lax.broadcasted_iota(jnp.int32, (HALF, 128), 0) + at[1] * HALF
    allowed = (lane <= slot) & (lane < at[4])
    for a in range(2):
        low = got[at[3] * 4 + a * 2].astype(F32)
        high = got[at[3] * 4 + a * 2 + 1].astype(F32)
        queries = jnp.where(lane < QC, low, pltpu.roll(high, QC, 1)).astype(BF)
        scores = nt(queries, keys) / math.sqrt(HEAD_DIM)
        scores = jnp.where(allowed, scores, -jnp.inf)
        expo = jnp.exp(scores - jnp.max(scores, axis=-1, keepdims=True))
        probs = (expo / jnp.sum(expo, axis=-1, keepdims=True)).astype(BF)
        mixed = jnp.dot(probs, values, preferred_element_type=F32).astype(BF)
        out[:, a * 128 : a * 128 + 128] = mixed


def output_kernel(at, got, mine, core, far, cross, own, out):
    parts = []
    for w in (mine, core, far, cross):
        total = jnp.zeros((HALF, QC), F32)
        for g in range(GROUPS):
            total = total + nt(got[2 * g], w[g, :, 0:BAND]) + nt(got[2 * g + 1], w[g, :, BAND:RUN])
        parts.append(total)
    blocks = []
    for j in range(4):
        picked = parts[0]
        for k in range(1, 4):
            picked = jnp.where(jnp.bitwise_xor(at[5], j) == k, parts[k], picked)
        blocks.append(picked)
    projected = jnp.concatenate(blocks, axis=1)
    attended = (own[...].astype(F32) + projected).astype(BF)
    out[...] = attended


def hidden_kernel(at, got, gain, mine, core, out, kept, normed, totals):
    g = pl.program_id(0)

    @pl.when(g == 0)
    def _():
        squares = jnp.zeros((HALF, 1), F32)
        for z in range(DEPTH):
            x = got[z].astype(F32)
            squares = squares + jnp.sum(x * x, axis=-1, keepdims=True)
        scale = lax.rsqrt(squares * (1.0 / D) + 1e-05)
        for z in range(DEPTH):
            x = got[z].astype(F32) * scale * gain[:, z * BAND : (z + 1) * BAND]
            normed[z // 2, :, (z % 2) * BAND : (z % 2 + 1) * BAND] = x.astype(BF)
        totals[...] = jnp.zeros_like(totals)

    x = normed[g]
    totals[0] += nt(mine[0, 0], x)
    totals[1] += nt(core[0, 0], x)

    @pl.when(g == GROUPS - 1)
    def _():
        for i in range(2):
            gate = totals[i, 0:FC, :]
            units = gate / (1.0 + jnp.exp(-gate)) * totals[i, FC : 2 * FC, :]
            out[i] = units.T.astype(BF)
        kept[...] = got[at[2], :, pl.ds(pl.multiple_of(at[1] * 128, 128), 128)]


def down_kernel(at, near, far, far_near, far_far, mine, core, out, units):
    g = pl.program_id(0)

    @pl.when(g == 0)
    def _():
        own = pl.ds(pl.multiple_of(at[1] * HALF, HALF), HALF)
        other = pl.ds(pl.multiple_of((1 - at[1]) * HALF, HALF), HALF)
        for i in range(2):
            units[i, own, :] = near[i]
            units[i, other, :] = far[i]
            units[2 + i, own, :] = far_far[i]
            units[2 + i, other, :] = far_near[i]

    total = jnp.dot(units[0], mine[0, 0, :, 0:BAND], preferred_element_type=F32)
    total = total + jnp.dot(units[1], core[0, 0, :, 0:BAND], preferred_element_type=F32)
    total = total + jnp.dot(units[2], mine[0, 0, :, BAND:RUN], preferred_element_type=F32)
    total = total + jnp.dot(units[3], core[0, 0, :, BAND:RUN], preferred_element_type=F32)
    out[0] = total[:, 0:128].astype(BF)
    out[1] = total[:, 128:256].astype(BF)


def finish_kernel(at, got, near, far, keep, give):
    total = got[0].astype(F32)
    for z in range(1, DEPTH):
        total = total + got[z].astype(F32)
    low = at[1] == 0
    first = jnp.where(low, near[...].astype(F32), far[...].astype(F32))
    second = jnp.where(low, far[...].astype(F32), near[...].astype(F32))
    result = (jnp.concatenate([first, second], axis=0) + total).T
    head, tail = result[0:QC, :], result[QC : 2 * QC, :]
    keep[...] = jnp.where(at[0] == 0, head, tail).astype(BF)
    give[...] = jnp.where(at[0] == 0, tail, head).astype(BF)


def pack_kernel(query, key, value, out_part, out):
    for g in range(GROUPS):
        out[g, 0:QC, :] = query[...]
        out[g, QC : QC + KC, :] = key[...]
        out[g, QC + KC : QC + 2 * KC, :] = value[...]
        out[g, 96:160, :] = out_part[...]


def pack(*parts):
    return pl.pallas_call(
        pack_kernel,
        out_shape=jax.ShapeDtypeStruct((GROUPS, 160, RUN), BF),
        in_specs=[VMEM] * 4,
        out_specs=VMEM,
        compiler_params=params(16),
        name="pack",
    )(*parts)


def project(at, stream, gain, weights, cos, sin):
    return pl.pallas_call(
        project_kernel,
        out_shape=(
            jax.ShapeDtypeStruct((8, HALF, 128), BF),
            jax.ShapeDtypeStruct((KC, 256), BF),
            jax.ShapeDtypeStruct((KC, 256), BF),
            jax.ShapeDtypeStruct((HALF, BAND), BF),
        ),
        in_specs=[SMEM] + [VMEM] * 5,
        out_specs=(VMEM,) * 4,
        compiler_params=params(32),
        name="project",
    )(at, stream, gain, weights, cos, sin)


def attend(at, got):
    return pl.pallas_call(
        attend_kernel,
        out_shape=jax.ShapeDtypeStruct((HALF, BAND), BF),
        in_specs=[SMEM, VMEM],
        out_specs=VMEM,
        compiler_params=params(16),
        name="attend",
    )(at, got)


def output(at, got, weights, own):
    return pl.pallas_call(
        output_kernel,
        out_shape=jax.ShapeDtypeStruct((HALF, BAND), BF),
        in_specs=[SMEM] + [VMEM] * 6,
        out_specs=VMEM,
        compiler_params=params(24),
        name="output",
    )(at, got, *weights, own)


def weights_at(g, at, part):
    return (g % 4, jnp.bitwise_xor(g // 4, at[6]), part, 0)


def hidden_units(at, got, gain, mine, core):
    block = pl.BlockSpec((1, 1, 2 * FC, RUN), lambda g, at: weights_at(g, at, 0))
    return pl.pallas_call(
        hidden_kernel,
        grid_spec=pltpu.PrefetchScalarGridSpec(
            num_scalar_prefetch=1,
            grid=(GROUPS,),
            in_specs=[
                pl.BlockSpec((DEPTH, HALF, BAND), lambda g, at: (0, 0, 0)),
                pl.BlockSpec((1, D), lambda g, at: (0, 0)),
                block,
                block,
            ],
            out_specs=(
                pl.BlockSpec((2, HALF, FC), lambda g, at: (0, 0, 0)),
                pl.BlockSpec((HALF, 128), lambda g, at: (0, 0)),
            ),
            scratch_shapes=[pltpu.VMEM((GROUPS, HALF, RUN), BF), pltpu.VMEM((2, 2 * FC, HALF), F32)],
        ),
        out_shape=(jax.ShapeDtypeStruct((2, HALF, FC), BF), jax.ShapeDtypeStruct((HALF, 128), BF)),
        compiler_params=params(24),
        cost_estimate=cost(2 * HALF * D * 4 * FC, 8 * 2**20),
        name="hidden",
    )(at, got, gain, mine, core)


def down(at, units, mine, core):
    block = pl.BlockSpec((1, 1, FC, RUN), lambda g, at: weights_at(g, at, 2))
    return pl.pallas_call(
        down_kernel,
        grid_spec=pltpu.PrefetchScalarGridSpec(
            num_scalar_prefetch=1,
            grid=(GROUPS,),
            in_specs=[pl.BlockSpec((2, HALF, FC), lambda g, at: (0, 0, 0))] * 4 + [block, block],
            out_specs=pl.BlockSpec((2, 128, 128), lambda g, at: (g, 0, 0)),
            scratch_shapes=[pltpu.VMEM((4, 128, FC), BF)],
        ),
        out_shape=jax.ShapeDtypeStruct((DEPTH, 128, 128), BF),
        compiler_params=params(24),
        cost_estimate=cost(4 * HALF * D * 2 * FC, 5 * 2**20),
        name="down",
    )(at, *units, mine, core)


def finish(at, got, near, far):
    return pl.pallas_call(
        finish_kernel,
        out_shape=(jax.ShapeDtypeStruct((QC, 128), BF),) * 2,
        in_specs=[SMEM] + [VMEM] * 3,
        out_specs=(VMEM, VMEM),
        compiler_params=params(16),
        name="finish",
    )(at, got, near, far)


def swap(x, bits):
    return lax.ppermute(x, "dev", [(d, d ^ bits) for d in range(MEMBERS)])


def swap_groups(x):
    return lax.ppermute(x, "grp", [(g, g ^ 4) for g in range(GROUPS)])


def trade(x, groups):
    return lax.all_to_all(x, "dev", 0, 0, axis_index_groups=groups, tiled=True)


def collect(x):
    return lax.all_gather(x, "dev", axis=0, axis_index_groups=COLUMNS)


def after(x, other):
    return lax.optimization_barrier((x, other))[0]


def on_device(
    stream,
    row_length,
    row_start,
    attn_gain,
    w_query,
    w_key,
    w_value,
    w_out,
    ffn_gain,
    w_gate,
    w_up,
    w_down,
):
    member = lax.axis_index("dev")
    core, yhi, z, quad = member % 2, member // 2 % 2, member // 4, member % 4
    ylo = lax.axis_index("grp") // 4
    length = jnp.where(core == 0, row_length[0], row_length[1])
    at = jnp.stack([core, yhi, z, z % 2, length, quad, ylo]).astype(jnp.int32)

    first = pack(w_query.T, w_key.T, w_value.T, w_out.T)
    first = lax.all_to_all(first, "grp", 0, 0, tiled=True)

    bands = w_down.T.reshape(FC, 2, 2, 128)
    low, high = bands[:, :, 0].reshape(FC, BAND), bands[:, :, 1].reshape(FC, BAND)
    kept = jnp.where(yhi == 0, low, high)
    given = swap(jnp.where(yhi == 0, high, low), 2)
    narrow = jnp.concatenate([kept, given], axis=1)
    wide = jnp.concatenate([w_gate.T, w_up.T], axis=0)
    ff = jnp.stack(
        [jnp.concatenate([wide, narrow], axis=0), jnp.concatenate([swap_groups(wide), swap_groups(narrow)], axis=0)]
    )
    ff = lax.all_gather(ff, "grp", axis=0, axis_index_groups=[[0, 1, 2, 3], [4, 5, 6, 7]])
    ff_core = swap(ff, 1)

    lane = jnp.arange(128, dtype=jnp.int32)
    column = jnp.where(lane < QC, member * QC + lane, member * KC + lane - QC)
    pair = (column % HEAD_DIM // 2).astype(F32)
    freq = jnp.exp(-(2.0 * pair / HEAD_DIM) * math.log(ROPE_BASE))
    positions = (row_start[:, None] + jnp.arange(ROW_LEN, dtype=jnp.int32)[None, :]).reshape(-1)
    angle = positions.astype(F32)[:, None] * freq[None, :]

    send, keys, values, own = project(
        at, stream, attn_gain.reshape(1, D), first, jnp.cos(angle), jnp.sin(angle)
    )
    got = trade(send, OCTETS)
    out_own = after(first, got)[:, 96:160, :]
    out_weights = (out_own, swap(out_own, 1), swap(out_own, 2), swap(out_own, 3))
    mixed = collect(attend(at, got))
    attended = output(at, mixed, out_weights, own)
    full = collect(attended)
    far_full = swap(full, 2)
    gain = ffn_gain.reshape(1, D)
    near, near_kept = hidden_units(at, full, gain, ff, ff_core)
    far_near = swap(near, 2)
    far, far_kept = hidden_units(at, far_full, gain, ff, ff_core)
    far_far = swap(far, 2)
    sums = trade(down(at, (near, far, far_near, far_far), ff, ff_core), COLUMNS)
    keep, give = finish(at, sums, near_kept, far_kept)
    give = swap(give, 1)
    rows = jnp.where(core == 0, jnp.concatenate([keep, give], axis=1), jnp.concatenate([give, keep], axis=1))
    return (keys.T, values.T, rows.T)


def solution(mesh):
    placed = (
        P("grp", None),
        P("grp"),
        P("grp"),
        P(),
        P("grp", "dev"),
        P("grp", "dev"),
        P("grp", "dev"),
        P("grp", "dev"),
        P(),
        P("grp", "dev"),
        P("grp", "dev"),
        P("grp", "dev"),
    )
    return jax.shard_map(
        on_device,
        mesh=mesh,
        in_specs=placed,
        out_specs=(P("grp", "dev"), P("grp", "dev"), P("grp", "dev")),
        check_vma=False,
    )
```

```python
import math

import jax
import jax.numpy as jnp
from jax import lax
from jax.experimental import pallas as pl
from jax.experimental.pallas import tpu as pltpu
from jax.sharding import PartitionSpec as P

HEADS = 32
KV_HEADS = 8
HEAD_DIM = 128
ROW_LEN = 128
D = 4096
ROPE_BASE = 500000.0

GROUPS = 8
MEMBERS = 64
DEPTH = 16
HALF = 64
QC = 64
KC = 16
FC = 224
BAND = 256
RUN = 512

COLUMNS = [[4 * z + q for z in range(DEPTH)] for q in range(4)]
OCTETS = [[8 * z + m for m in range(8)] for z in range(8)]

BF = jnp.bfloat16
F32 = jnp.float32
VMEM = pl.BlockSpec(memory_space=pltpu.VMEM)
HBM = pl.BlockSpec(memory_space=pltpu.HBM)
ANY = pl.BlockSpec(memory_space=pl.ANY)
SMEM = pl.BlockSpec(memory_space=pltpu.SMEM)


def nt(a, b):
    return lax.dot_general(a, b, (((1,), (1,)), ((), ())), preferred_element_type=F32)


def whole(*shape):
    return pl.BlockSpec(shape, lambda i: (0,) * len(shape))


def params(mib):
    return pltpu.CompilerParams(vmem_limit_bytes=mib * 2**20)


def cost(flops, nbytes):
    return pl.CostEstimate(flops=flops, bytes_accessed=nbytes, transcendentals=0)


def project_kernel(after, normed, weights, cos, sin, send, keys, values):
    total = jnp.zeros((256, 96), F32)
    for g in range(GROUPS):
        total = total + nt(normed[g], weights[g, 0:96, :])
    total = jnp.concatenate([total, jnp.zeros((256, 32), F32)], axis=1)
    lane = lax.broadcasted_iota(jnp.int32, (256, 128), 1)
    partner = jnp.where(lane % 2 == 0, -pltpu.roll(total, 127, 1), pltpu.roll(total, 1, 1))
    turned = jnp.where(lane < QC + KC, total * cos[...] + partner * sin[...], total)
    turned = turned.astype(BF).astype(F32)
    flipped = turned.T
    keys[...] = flipped[QC : QC + KC, :].astype(BF)
    values[...] = flipped[QC + KC : QC + 2 * KC, :].astype(BF)
    lane = lax.broadcasted_iota(jnp.int32, (HALF, 128), 1)
    for zl in range(2):
        for yhi in range(2):
            for c in range(2):
                first = turned[c * 128 : c * 128 + HALF, :]
                second = turned[c * 128 + HALF : c * 128 + 128, :]
                mine = second if yhi else first
                chunk = jnp.where(lane < QC, mine, jnp.where(lane < 96, first, pltpu.roll(second, 32, 1)))
                send[zl * 4 + yhi * 2 + c] = chunk.astype(BF)


def attend_kernel(at, lengths, got, out):
    lane = lax.broadcasted_iota(jnp.int32, (HALF, 128), 1)
    pieces = [got[m].astype(F32) for m in range(8)]

    def gather(start):
        full = jnp.zeros((HALF, 128), F32)
        for m in range(8):
            full = jnp.where(lane // KC == m, pltpu.roll(pieces[m], (KC * m - start) % 128, 1), full)
        return full.astype(BF)

    keys = jnp.concatenate([gather(QC), gather(96)], axis=0)
    values = jnp.concatenate([gather(QC + KC), gather(96 + KC)], axis=0)
    slot = lax.broadcasted_iota(jnp.int32, (HALF, 128), 0) + at[1] * HALF
    allowed = (lane <= slot) & (lane < lengths[at[0]])
    for a in range(2):
        low = got[at[3] * 4 + a * 2].astype(F32)
        high = got[at[3] * 4 + a * 2 + 1].astype(F32)
        queries = jnp.where(lane < QC, low, pltpu.roll(high, QC, 1)).astype(BF)
        scores = nt(queries, keys) / math.sqrt(HEAD_DIM)
        scores = jnp.where(allowed, scores, -jnp.inf)
        expo = jnp.exp(scores - jnp.max(scores, axis=-1, keepdims=True))
        probs = (expo / jnp.sum(expo, axis=-1, keepdims=True)).astype(BF)
        mixed = jnp.dot(probs, values, preferred_element_type=F32).astype(BF)
        out[:, a * 128 : a * 128 + 128] = mixed


def output_kernel(at, got, mine, core, far, cross, own, out):
    parts = []
    for w in (mine, core, far, cross):
        total = jnp.zeros((HALF, QC), F32)
        for g in range(GROUPS):
            total = total + nt(got[2 * g], w[g, :, 0:BAND]) + nt(got[2 * g + 1], w[g, :, BAND:RUN])
        parts.append(total)
    blocks = []
    for j in range(4):
        picked = parts[0]
        for k in range(1, 4):
            picked = jnp.where(jnp.bitwise_xor(at[5], j) == k, parts[k], picked)
        blocks.append(picked)
    projected = jnp.concatenate(blocks, axis=1)
    attended = (own[...].astype(F32) + projected).astype(BF)
    out[...] = attended


def hidden_kernel(at, after, got, gain, mine, core, out, kept):
    squares = jnp.zeros((HALF, 1), F32)
    for z in range(DEPTH):
        x = got[z].astype(F32)
        squares = squares + jnp.sum(x * x, axis=-1, keepdims=True)
    scale = lax.rsqrt(squares * (1.0 / D) + 1e-05)
    kept[...] = got[at[2], :, pl.ds(pl.multiple_of(at[1] * 128, 128), 128)]
    totals = [jnp.zeros((HALF, FC), F32) for _ in range(4)]
    for g in range(GROUPS):
        parts = []
        for z in (2 * g, 2 * g + 1):
            part = got[z].astype(F32) * scale * gain[:, z * BAND : (z + 1) * BAND]
            parts.append(part.astype(BF))
        x = jnp.concatenate(parts, axis=1)
        side = jnp.bitwise_xor(g // 4, at[6])
        for i, w in enumerate((mine, core)):
            totals[2 * i] = totals[2 * i] + nt(x, w[g % 4, side, 0:FC, :])
            totals[2 * i + 1] = totals[2 * i + 1] + nt(x, w[g % 4, side, FC : 2 * FC, :])
    for i in range(2):
        gate = totals[2 * i]
        out[i] = (gate / (1.0 + jnp.exp(-gate)) * totals[2 * i + 1]).astype(BF)


def down_kernel(at, near, far, far_near, far_far, mine, core, out, units):
    own = pl.ds(pl.multiple_of(at[1] * HALF, HALF), HALF)
    other = pl.ds(pl.multiple_of((1 - at[1]) * HALF, HALF), HALF)
    for i in range(2):
        units[i, own, :] = near[i]
        units[i, other, :] = far[i]
        units[2 + i, own, :] = far_far[i]
        units[2 + i, other, :] = far_near[i]
    for g in range(GROUPS):
        side = jnp.bitwise_xor(g // 4, at[6])
        total = jnp.zeros((128, BAND), F32)
        for i, w in enumerate((mine, core)):
            total = total + jnp.dot(units[i], w[g % 4, side, 2 * FC : 3 * FC, 0:BAND], preferred_element_type=F32)
            total = total + jnp.dot(units[2 + i], w[g % 4, side, 2 * FC : 3 * FC, BAND:RUN], preferred_element_type=F32)
        out[2 * g] = total[:, 0:128].astype(BF)
        out[2 * g + 1] = total[:, 128:256].astype(BF)


def finish_kernel(at, got, near, far, keep, give):
    total = got[0].astype(F32)
    for z in range(1, DEPTH):
        total = total + got[z].astype(F32)
    low = at[1] == 0
    first = jnp.where(low, near[...].astype(F32), far[...].astype(F32))
    second = jnp.where(low, far[...].astype(F32), near[...].astype(F32))
    result = (jnp.concatenate([first, second], axis=0) + total).T
    head, tail = result[0:QC, :], result[QC : 2 * QC, :]
    keep[...] = jnp.where(at[0] == 0, head, tail).astype(BF)
    give[...] = jnp.where(at[0] == 0, tail, head).astype(BF)


def pack_kernel(query, key, value, out_part, out, token, held, sems):
    token[...] = jnp.zeros_like(token)
    spans = ((query, 0, QC), (key, QC, KC), (value, QC + KC, KC), (out_part, 96, QC))
    reads = [
        pltpu.make_async_copy(ref, held.at[pl.ds(start, rows), :], sems.at[i])
        for i, (ref, start, rows) in enumerate(spans)
    ]
    for copy in reads:
        copy.start()
    for copy in reads:
        copy.wait()
    writes = [pltpu.make_async_copy(held, out.at[g], sems.at[4 + g]) for g in range(GROUPS)]
    for copy in writes:
        copy.start()
    for copy in writes:
        copy.wait()


def prepare_kernel(at, after, tables, gate, up, narrow, stream, gain, wide, keep, give, normed, own):
    wide[0:FC, :] = gate[...]
    wide[FC : 2 * FC, :] = up[...]
    low = at[1] == 0
    for i in range(2):
        even = narrow[:, 2 * i * 128 : (2 * i + 1) * 128]
        odd = narrow[:, (2 * i + 1) * 128 : (2 * i + 2) * 128]
        keep[:, i * 128 : (i + 1) * 128] = jnp.where(low, even, odd)
        give[:, i * 128 : (i + 1) * 128] = jnp.where(low, odd, even)
    x = stream[...].astype(F32)
    scale = lax.rsqrt(jnp.mean(x * x, axis=-1, keepdims=True) + 1e-05)
    for g in range(GROUPS):
        cols = pl.ds(g * RUN, RUN)
        normed[g] = (stream[:, cols].astype(F32) * scale * gain[:, cols]).astype(BF)
    rows = pl.ds(pl.multiple_of(at[0] * 128 + at[1] * HALF, HALF), HALF)
    own[...] = stream[rows, pl.ds(pl.multiple_of(at[2] * BAND, BAND), BAND)]


def prepare(at, after, tables, gate, up, narrow, stream, gain):
    half = jax.ShapeDtypeStruct((FC, BAND), BF)
    return pl.pallas_call(
        prepare_kernel,
        out_shape=(
            jax.ShapeDtypeStruct((2 * FC, RUN), BF),
            half,
            half,
            jax.ShapeDtypeStruct((GROUPS, 256, RUN), BF),
            jax.ShapeDtypeStruct((HALF, BAND), BF),
        ),
        in_specs=[SMEM, ANY, ANY] + [VMEM] * 5,
        out_specs=(VMEM,) * 5,
        compiler_params=params(24),
        name="prepare",
    )(at, after, tables, gate, up, narrow, stream, gain)


def join_kernel(after, wide, keep, got, wide_lo, keep_lo, got_lo, out, token, sems):
    token[...] = jnp.zeros_like(token)
    copies = []
    for i, parts in enumerate(((wide, keep, got), (wide_lo, keep_lo, got_lo))):
        spans = (
            out.at[i, pl.ds(0, 2 * FC), :],
            out.at[i, pl.ds(2 * FC, FC), pl.ds(0, BAND)],
            out.at[i, pl.ds(2 * FC, FC), pl.ds(BAND, BAND)],
        )
        for k, (part, span) in enumerate(zip(parts, spans)):
            copies.append(pltpu.make_async_copy(part, span, sems.at[3 * i + k]))
    for copy in copies:
        copy.start()
    for copy in copies:
        copy.wait()


def join(after, *parts):
    return pl.pallas_call(
        join_kernel,
        out_shape=(jax.ShapeDtypeStruct((2, 3 * FC, RUN), BF), jax.ShapeDtypeStruct((8, 128), F32)),
        in_specs=[ANY] + [HBM] * 6,
        out_specs=(HBM, VMEM),
        scratch_shapes=[pltpu.SemaphoreType.DMA((6,))],
        compiler_params=params(57),
        name="join",
    )(after, *parts)


def pack(*parts):
    return pl.pallas_call(
        pack_kernel,
        out_shape=(jax.ShapeDtypeStruct((GROUPS, 160, RUN), BF), jax.ShapeDtypeStruct((8, 128), F32)),
        in_specs=[HBM] * 4,
        out_specs=(HBM, VMEM),
        scratch_shapes=[pltpu.VMEM((160, RUN), BF), pltpu.SemaphoreType.DMA((4 + GROUPS,))],
        compiler_params=params(60),
        name="pack",
    )(*parts)


def project(after, normed, weights, cos, sin):
    return pl.pallas_call(
        project_kernel,
        out_shape=(
            jax.ShapeDtypeStruct((8, HALF, 128), BF),
            jax.ShapeDtypeStruct((KC, 256), BF),
            jax.ShapeDtypeStruct((KC, 256), BF),
        ),
        in_specs=[ANY] + [VMEM] * 4,
        out_specs=(VMEM,) * 3,
        compiler_params=params(24),
        name="project",
    )(after, normed, weights, cos, sin)


def attend(at, lengths, got):
    return pl.pallas_call(
        attend_kernel,
        out_shape=jax.ShapeDtypeStruct((HALF, BAND), BF),
        in_specs=[SMEM, SMEM, VMEM],
        out_specs=VMEM,
        compiler_params=params(16),
        name="attend",
    )(at, lengths, got)


def output(at, got, weights, own):
    return pl.pallas_call(
        output_kernel,
        out_shape=jax.ShapeDtypeStruct((HALF, BAND), BF),
        in_specs=[SMEM] + [VMEM] * 6,
        out_specs=VMEM,
        compiler_params=params(24),
        name="output",
    )(at, got, *weights, own)


def hidden_units(at, after, got, gain, mine, core):
    return pl.pallas_call(
        hidden_kernel,
        out_shape=(jax.ShapeDtypeStruct((2, HALF, FC), BF), jax.ShapeDtypeStruct((HALF, 128), BF)),
        in_specs=[SMEM, ANY] + [VMEM] * 4,
        out_specs=(VMEM, VMEM),
        compiler_params=params(16),
        cost_estimate=cost(2 * HALF * D * 4 * FC, 8 * 2**20),
        name="hidden",
    )(at, after, got, gain, mine, core)


def down(at, units, mine, core):
    return pl.pallas_call(
        down_kernel,
        out_shape=jax.ShapeDtypeStruct((DEPTH, 128, 128), BF),
        in_specs=[SMEM] + [VMEM] * 6,
        out_specs=VMEM,
        scratch_shapes=[pltpu.VMEM((4, 128, FC), BF)],
        compiler_params=params(16),
        cost_estimate=cost(4 * HALF * D * 2 * FC, 5 * 2**20),
        name="down",
    )(at, *units, mine, core)


def finish(at, got, near, far):
    return pl.pallas_call(
        finish_kernel,
        out_shape=(jax.ShapeDtypeStruct((QC, 128), BF),) * 2,
        in_specs=[SMEM] + [VMEM] * 3,
        out_specs=(VMEM, VMEM),
        compiler_params=params(16),
        name="finish",
    )(at, got, near, far)


def swap(x, bits):
    return lax.ppermute(x, "dev", [(d, d ^ bits) for d in range(MEMBERS)])


def swap_groups(x):
    return lax.ppermute(x, "grp", [(g, g ^ 4) for g in range(GROUPS)])


def swap_both(x):
    pairs = [(g * MEMBERS + d, (g ^ 4) * MEMBERS + (d ^ 2)) for g in range(GROUPS) for d in range(MEMBERS)]
    return lax.ppermute(x, ("grp", "dev"), pairs)


def trade(x, groups):
    return lax.all_to_all(x, "dev", 0, 0, axis_index_groups=groups, tiled=True)


def collect(x):
    return lax.all_gather(x, "dev", axis=0, axis_index_groups=COLUMNS)


def after(x, other):
    return lax.optimization_barrier((x, other))[0]


def on_device(
    stream,
    row_length,
    row_start,
    attn_gain,
    w_query,
    w_key,
    w_value,
    w_out,
    ffn_gain,
    w_gate,
    w_up,
    w_down,
):
    member = lax.axis_index("dev")
    core, yhi, z, quad = member % 2, member // 2 % 2, member // 4, member % 4
    ylo = lax.axis_index("grp") // 4
    at = jnp.stack([core, yhi, z, z % 2, z // 2, quad, ylo]).astype(jnp.int32)

    packed, token = pack(w_query.T, w_key.T, w_value.T, w_out.T)
    first = lax.all_to_all(packed, "grp", 0, 0, tiled=True)

    lane = jnp.arange(128, dtype=jnp.int32)
    column = jnp.where(lane < QC, member * QC + lane, member * KC + lane - QC)
    pair = (column % HEAD_DIM // 2).astype(F32)
    freq = jnp.exp(-(2.0 * pair / HEAD_DIM) * math.log(ROPE_BASE))
    positions = (row_start[:, None] + jnp.arange(ROW_LEN, dtype=jnp.int32)[None, :]).reshape(-1)
    angle = positions.astype(F32)[:, None] * freq[None, :]
    cos, sin = jnp.cos(angle), jnp.sin(angle)

    wide, keep, give, normed, own = prepare(
        at, token, cos, w_gate.T, w_up.T, w_down.T, stream, attn_gain.reshape(1, D)
    )
    ff, token = join(first, wide, keep, swap(give, 2), swap_groups(wide), swap_groups(keep), swap_both(give))
    ff_all = lax.all_gather(ff, "grp", axis=0, axis_index_groups=[[0, 1, 2, 3], [4, 5, 6, 7]])

    send, keys, values = project(token, normed, first, cos, sin)
    got = trade(send, OCTETS)
    out_own = after(first, got)[:, 96:160, :]
    out_weights = (out_own, swap(out_own, 1), swap(out_own, 2), swap(out_own, 3))
    mixed = collect(attend(at, row_length, got))
    attended = output(at, mixed, out_weights, own)
    ff = after(ff_all, attended)
    ff_core = swap(ff, 1)
    full = collect(attended)
    far_full = swap(full, 2)
    gain = ffn_gain.reshape(1, D)
    near, near_kept = hidden_units(at, at, full, gain, ff, ff_core)
    far_near = swap(near, 2)
    far, far_kept = hidden_units(at, far_near, far_full, gain, ff, ff_core)
    far_far = swap(far, 2)
    sums = trade(down(at, (near, far, far_near, far_far), ff, ff_core), COLUMNS)
    keep, give = finish(at, sums, near_kept, far_kept)
    give = swap(give, 1)
    rows = jnp.where(core == 0, jnp.concatenate([keep, give], axis=1), jnp.concatenate([give, keep], axis=1))
    return (keys.T, values.T, rows.T)


def solution(mesh):
    placed = (
        P("grp", None),
        P("grp"),
        P("grp"),
        P(),
        P("grp", "dev"),
        P("grp", "dev"),
        P("grp", "dev"),
        P("grp", "dev"),
        P(),
        P("grp", "dev"),
        P("grp", "dev"),
        P("grp", "dev"),
    )
    return jax.shard_map(
        on_device,
        mesh=mesh,
        in_specs=placed,
        out_specs=(P("grp", "dev"), P("grp", "dev"), P("grp", "dev")),
        check_vma=False,
    )
```

```python
import math

import jax
import jax.numpy as jnp
from jax import lax
from jax.experimental import pallas as pl
from jax.experimental.pallas import tpu as pltpu
from jax.sharding import PartitionSpec as P

HEADS = 32
KV_HEADS = 8
HEAD_DIM = 128
ROW_LEN = 128
D = 4096
ROPE_BASE = 500000.0

GROUPS = 8
MEMBERS = 64
DEPTH = 16
HALF = 64
QC = 64
KC = 16
FC = 224
BAND = 256
RUN = 512

COLUMNS = [[4 * z + q for z in range(DEPTH)] for q in range(4)]
OCTETS = [[8 * z + m for m in range(8)] for z in range(8)]

BF = jnp.bfloat16
F32 = jnp.float32
VMEM = pl.BlockSpec(memory_space=pltpu.VMEM)
HBM = pl.BlockSpec(memory_space=pltpu.HBM)
ANY = pl.BlockSpec(memory_space=pl.ANY)
SMEM = pl.BlockSpec(memory_space=pltpu.SMEM)


def nt(a, b):
    return lax.dot_general(a, b, (((1,), (1,)), ((), ())), preferred_element_type=F32)


def whole(*shape):
    return pl.BlockSpec(shape, lambda i: (0,) * len(shape))


def params(mib):
    return pltpu.CompilerParams(vmem_limit_bytes=mib * 2**20)


def cost(flops, nbytes):
    return pl.CostEstimate(flops=flops, bytes_accessed=nbytes, transcendentals=0)


def project_kernel(normed, weights, cos, sin, send, keys, values):
    total = jnp.zeros((256, 96), F32)
    for g in range(GROUPS):
        total = total + nt(normed[g], weights[g, 0:96, :])
    total = jnp.concatenate([total, jnp.zeros((256, 32), F32)], axis=1)
    lane = lax.broadcasted_iota(jnp.int32, (256, 128), 1)
    partner = jnp.where(lane % 2 == 0, -pltpu.roll(total, 127, 1), pltpu.roll(total, 1, 1))
    turned = jnp.where(lane < QC + KC, total * cos[...] + partner * sin[...], total)
    turned = turned.astype(BF).astype(F32)
    flipped = turned.T
    keys[...] = flipped[QC : QC + KC, :].astype(BF)
    values[...] = flipped[QC + KC : QC + 2 * KC, :].astype(BF)
    lane = lax.broadcasted_iota(jnp.int32, (HALF, 128), 1)
    for zl in range(2):
        for yhi in range(2):
            for c in range(2):
                first = turned[c * 128 : c * 128 + HALF, :]
                second = turned[c * 128 + HALF : c * 128 + 128, :]
                mine = second if yhi else first
                chunk = jnp.where(lane < QC, mine, jnp.where(lane < 96, first, pltpu.roll(second, 32, 1)))
                send[zl * 4 + yhi * 2 + c] = chunk.astype(BF)


def attend_kernel(at, lengths, got, out):
    lane = lax.broadcasted_iota(jnp.int32, (HALF, 128), 1)
    pieces = [got[m].astype(F32) for m in range(8)]

    def gather(start):
        full = jnp.zeros((HALF, 128), F32)
        for m in range(8):
            full = jnp.where(lane // KC == m, pltpu.roll(pieces[m], (KC * m - start) % 128, 1), full)
        return full.astype(BF)

    keys = jnp.concatenate([gather(QC), gather(96)], axis=0)
    values = jnp.concatenate([gather(QC + KC), gather(96 + KC)], axis=0)
    slot = lax.broadcasted_iota(jnp.int32, (HALF, 128), 0) + at[1] * HALF
    allowed = (lane <= slot) & (lane < lengths[at[0]])
    for a in range(2):
        low = got[at[3] * 4 + a * 2].astype(F32)
        high = got[at[3] * 4 + a * 2 + 1].astype(F32)
        queries = jnp.where(lane < QC, low, pltpu.roll(high, QC, 1)).astype(BF)
        scores = nt(queries, keys) / math.sqrt(HEAD_DIM)
        scores = jnp.where(allowed, scores, -jnp.inf)
        expo = jnp.exp(scores - jnp.max(scores, axis=-1, keepdims=True))
        probs = (expo / jnp.sum(expo, axis=-1, keepdims=True)).astype(BF)
        mixed = jnp.dot(probs, values, preferred_element_type=F32).astype(BF)
        out[:, a * 128 : a * 128 + 128] = mixed


def output_kernel(at, got, mine, core, far, cross, own, out):
    parts = []
    for w in (mine, core, far, cross):
        total = jnp.zeros((HALF, QC), F32)
        for g in range(GROUPS):
            total = total + nt(got[2 * g], w[g, :, 0:BAND]) + nt(got[2 * g + 1], w[g, :, BAND:RUN])
        parts.append(total)
    blocks = []
    for j in range(4):
        picked = parts[0]
        for k in range(1, 4):
            picked = jnp.where(jnp.bitwise_xor(at[5], j) == k, parts[k], picked)
        blocks.append(picked)
    projected = jnp.concatenate(blocks, axis=1)
    attended = (own[...].astype(F32) + projected).astype(BF)
    out[...] = attended


def hidden_kernel(at, near, far, gain, mine, core, out, kept):
    low = at[1] == 0
    lanes = pl.ds(pl.multiple_of(at[1] * 128, 128), 128)
    near_kept, far_kept = near[at[2], :, lanes], far[at[2], :, lanes]
    kept[0:HALF, :] = jnp.where(low, near_kept, far_kept)
    kept[HALF : 2 * HALF, :] = jnp.where(low, far_kept, near_kept)
    scales = []
    for got in (near, far):
        squares = jnp.zeros((HALF, 1), F32)
        for z in range(DEPTH):
            x = got[z].astype(F32)
            squares = squares + jnp.sum(x * x, axis=-1, keepdims=True)
        scales.append(lax.rsqrt(squares * (1.0 / D) + 1e-05))
    totals = [jnp.zeros((2 * HALF, FC), F32) for _ in range(4)]
    for g in range(GROUPS):
        rows = []
        for got, scale in zip((near, far), scales):
            parts = []
            for z in (2 * g, 2 * g + 1):
                part = got[z].astype(F32) * scale * gain[:, z * BAND : (z + 1) * BAND]
                parts.append(part.astype(BF))
            rows.append(jnp.concatenate(parts, axis=1))
        x = jnp.concatenate(rows, axis=0)
        side = jnp.bitwise_xor(g // 4, at[6])
        for i, w in enumerate((mine, core)):
            totals[2 * i] = totals[2 * i] + nt(x, w[g % 4, side, 0:FC, :])
            totals[2 * i + 1] = totals[2 * i + 1] + nt(x, w[g % 4, side, FC : 2 * FC, :])
    for i in range(2):
        gate = totals[2 * i]
        units = (gate / (1.0 + jnp.exp(-gate)) * totals[2 * i + 1]).astype(BF)
        first, second = units[0:HALF, :], units[HALF : 2 * HALF, :]
        out[i, 0:HALF, :] = jnp.where(low, first, second)
        out[i, HALF : 2 * HALF, :] = jnp.where(low, second, first)


def down_kernel(at, units, far_units, mine, core, out):
    for g in range(GROUPS):
        side = jnp.bitwise_xor(g // 4, at[6])
        total = jnp.zeros((128, BAND), F32)
        for i, w in enumerate((mine, core)):
            total = total + jnp.dot(units[i], w[g % 4, side, 2 * FC : 3 * FC, 0:BAND], preferred_element_type=F32)
            total = total + jnp.dot(far_units[i], w[g % 4, side, 2 * FC : 3 * FC, BAND:RUN], preferred_element_type=F32)
        out[2 * g] = total[:, 0:128].astype(BF)
        out[2 * g + 1] = total[:, 128:256].astype(BF)


def finish_kernel(at, got, kept, keep, give):
    total = kept[...].astype(F32)
    for z in range(DEPTH):
        total = total + got[z].astype(F32)
    result = total.T
    head, tail = result[0:QC, :], result[QC : 2 * QC, :]
    keep[...] = jnp.where(at[0] == 0, head, tail).astype(BF)
    give[...] = jnp.where(at[0] == 0, tail, head).astype(BF)


def pack_kernel(query, key, value, out_part, out, token, held, sems):
    token[...] = jnp.zeros_like(token)
    spans = ((query, 0, QC), (key, QC, KC), (value, QC + KC, KC), (out_part, 96, QC))
    reads = [
        pltpu.make_async_copy(ref, held.at[pl.ds(start, rows), :], sems.at[i])
        for i, (ref, start, rows) in enumerate(spans)
    ]
    for copy in reads:
        copy.start()
    for copy in reads:
        copy.wait()
    writes = [pltpu.make_async_copy(held, out.at[g], sems.at[4 + g]) for g in range(GROUPS)]
    for copy in writes:
        copy.start()
    for copy in writes:
        copy.wait()


def prepare_kernel(at, after, tables, gate, up, narrow, stream, gain, wide, give, normed, own):
    wide[0:FC, :] = gate[...]
    wide[FC : 2 * FC, :] = up[...]
    low = at[1] == 0
    for i in range(2):
        even = narrow[:, 2 * i * 128 : (2 * i + 1) * 128]
        odd = narrow[:, (2 * i + 1) * 128 : (2 * i + 2) * 128]
        keep = jnp.where(low, even, odd)
        for k in range(2):
            lanes = slice(k * BAND + i * 128, k * BAND + (i + 1) * 128)
            wide[2 * FC : 5 * FC // 2, lanes] = keep[k * FC // 2 : (k + 1) * FC // 2, :]
        give[:, i * 128 : (i + 1) * 128] = jnp.where(low, odd, even)
    x = stream[...].astype(F32)
    scale = lax.rsqrt(jnp.mean(x * x, axis=-1, keepdims=True) + 1e-05)
    for g in range(GROUPS):
        cols = pl.ds(g * RUN, RUN)
        normed[g] = (stream[:, cols].astype(F32) * scale * gain[:, cols]).astype(BF)
    rows = pl.ds(pl.multiple_of(at[0] * 128 + at[1] * HALF, HALF), HALF)
    own[...] = stream[rows, pl.ds(pl.multiple_of(at[2] * BAND, BAND), BAND)]


def prepare(at, after, tables, gate, up, narrow, stream, gain):
    half = jax.ShapeDtypeStruct((FC, BAND), BF)
    return pl.pallas_call(
        prepare_kernel,
        out_shape=(
            jax.ShapeDtypeStruct((5 * FC // 2, RUN), BF),
            half,
            jax.ShapeDtypeStruct((GROUPS, 256, RUN), BF),
            jax.ShapeDtypeStruct((HALF, BAND), BF),
        ),
        in_specs=[SMEM, ANY, ANY] + [VMEM] * 5,
        out_specs=(VMEM,) * 4,
        compiler_params=params(24),
        name="prepare",
    )(at, after, tables, gate, up, narrow, stream, gain)


def join_kernel(after, wide, got, wide_lo, got_lo, out):
    for i, (kept, given) in enumerate(((wide, got), (wide_lo, got_lo))):
        out[i, 0 : 2 * FC, :] = kept[0 : 2 * FC, :]
        for k in range(2):
            rows = slice(2 * FC + k * FC // 2, 2 * FC + (k + 1) * FC // 2)
            out[i, rows, 0:BAND] = kept[2 * FC : 5 * FC // 2, k * BAND : (k + 1) * BAND]
        out[i, 2 * FC : 3 * FC, BAND:RUN] = given[...]


def join(after, *parts):
    return pl.pallas_call(
        join_kernel,
        out_shape=jax.ShapeDtypeStruct((2, 3 * FC, RUN), BF),
        in_specs=[ANY] + [VMEM] * 4,
        out_specs=VMEM,
        compiler_params=params(16),
        name="join",
    )(after, *parts)


def pack(*parts):
    return pl.pallas_call(
        pack_kernel,
        out_shape=(jax.ShapeDtypeStruct((GROUPS, 160, RUN), BF), jax.ShapeDtypeStruct((8, 128), F32)),
        in_specs=[HBM] * 4,
        out_specs=(HBM, VMEM),
        scratch_shapes=[pltpu.VMEM((160, RUN), BF), pltpu.SemaphoreType.DMA((4 + GROUPS,))],
        compiler_params=params(60),
        name="pack",
    )(*parts)


def project(normed, weights, cos, sin):
    return pl.pallas_call(
        project_kernel,
        out_shape=(
            jax.ShapeDtypeStruct((8, HALF, 128), BF),
            jax.ShapeDtypeStruct((KC, 256), BF),
            jax.ShapeDtypeStruct((KC, 256), BF),
        ),
        in_specs=[VMEM] * 4,
        out_specs=(VMEM,) * 3,
        compiler_params=params(24),
        name="project",
    )(normed, weights, cos, sin)


def attend(at, lengths, got):
    return pl.pallas_call(
        attend_kernel,
        out_shape=jax.ShapeDtypeStruct((HALF, BAND), BF),
        in_specs=[SMEM, SMEM, VMEM],
        out_specs=VMEM,
        compiler_params=params(16),
        name="attend",
    )(at, lengths, got)


def output(at, got, weights, own):
    return pl.pallas_call(
        output_kernel,
        out_shape=jax.ShapeDtypeStruct((HALF, BAND), BF),
        in_specs=[SMEM] + [VMEM] * 6,
        out_specs=VMEM,
        compiler_params=params(24),
        name="output",
    )(at, got, *weights, own)


def hidden_units(at, near, far, gain, mine, core):
    return pl.pallas_call(
        hidden_kernel,
        out_shape=(jax.ShapeDtypeStruct((2, 128, FC), BF), jax.ShapeDtypeStruct((128, 128), BF)),
        in_specs=[SMEM] + [VMEM] * 5,
        out_specs=(VMEM, VMEM),
        compiler_params=params(16),
        cost_estimate=cost(4 * HALF * D * 4 * FC, 8 * 2**20),
        name="hidden",
    )(at, near, far, gain, mine, core)


def down(at, units, far_units, mine, core):
    return pl.pallas_call(
        down_kernel,
        out_shape=jax.ShapeDtypeStruct((DEPTH, 128, 128), BF),
        in_specs=[SMEM] + [VMEM] * 4,
        out_specs=VMEM,
        compiler_params=params(16),
        cost_estimate=cost(4 * HALF * D * 2 * FC, 5 * 2**20),
        name="down",
    )(at, units, far_units, mine, core)


def finish(at, got, kept):
    return pl.pallas_call(
        finish_kernel,
        out_shape=(jax.ShapeDtypeStruct((QC, 128), BF),) * 2,
        in_specs=[SMEM] + [VMEM] * 2,
        out_specs=(VMEM, VMEM),
        compiler_params=params(16),
        name="finish",
    )(at, got, kept)


def swap(x, bits):
    return lax.ppermute(x, "dev", [(d, d ^ bits) for d in range(MEMBERS)])


def swap_groups(x):
    return lax.ppermute(x, "grp", [(g, g ^ 4) for g in range(GROUPS)])


def swap_both(x):
    pairs = [(g * MEMBERS + d, (g ^ 4) * MEMBERS + (d ^ 2)) for g in range(GROUPS) for d in range(MEMBERS)]
    return lax.ppermute(x, ("grp", "dev"), pairs)


def trade(x, groups):
    return lax.all_to_all(x, "dev", 0, 0, axis_index_groups=groups, tiled=True)


def collect(x):
    return lax.all_gather(x, "dev", axis=0, axis_index_groups=COLUMNS)


def after(x, other):
    return lax.optimization_barrier((x, other))[0]


def on_device(
    stream,
    row_length,
    row_start,
    attn_gain,
    w_query,
    w_key,
    w_value,
    w_out,
    ffn_gain,
    w_gate,
    w_up,
    w_down,
):
    member = lax.axis_index("dev")
    core, yhi, z, quad = member % 2, member // 2 % 2, member // 4, member % 4
    ylo = lax.axis_index("grp") // 4
    at = jnp.stack([core, yhi, z, z % 2, z // 2, quad, ylo]).astype(jnp.int32)

    packed, token = pack(w_query.T, w_key.T, w_value.T, w_out.T)
    first = lax.all_to_all(packed, "grp", 0, 0, tiled=True)

    lane = jnp.arange(128, dtype=jnp.int32)
    column = jnp.where(lane < QC, member * QC + lane, member * KC + lane - QC)
    pair = (column % HEAD_DIM // 2).astype(F32)
    freq = jnp.exp(-(2.0 * pair / HEAD_DIM) * math.log(ROPE_BASE))
    positions = (row_start[:, None] + jnp.arange(ROW_LEN, dtype=jnp.int32)[None, :]).reshape(-1)
    angle = positions.astype(F32)[:, None] * freq[None, :]
    cos, sin = jnp.cos(angle), jnp.sin(angle)

    wide, give, normed, own = prepare(
        at, token, cos, w_gate.T, w_up.T, w_down.T, stream, attn_gain.reshape(1, D)
    )
    trades = (swap(give, 2), swap_groups(wide), swap_both(give))
    send, keys, values = project(normed, first, cos, sin)
    got = trade(send, OCTETS)
    ff = join(got, wide, *trades)
    ff_all = lax.all_gather(ff, "grp", axis=0, axis_index_groups=[[0, 1, 2, 3], [4, 5, 6, 7]])
    out_own = first[:, 96:160, :]
    out_weights = (out_own, swap(out_own, 1), swap(out_own, 2), swap(out_own, 3))
    mixed = collect(attend(at, row_length, got))
    attended = output(at, mixed, out_weights, own)
    ff = after(ff_all, attended)
    ff_core = swap(ff, 1)
    full = collect(attended)
    far_full = swap(full, 2)
    gain = ffn_gain.reshape(1, D)
    units, kept = hidden_units(at, full, far_full, gain, ff, ff_core)
    sums = trade(down(at, units, swap(units, 2), ff, ff_core), COLUMNS)
    keep, give = finish(at, sums, kept)
    give = swap(give, 1)
    rows = jnp.where(core == 0, jnp.concatenate([keep, give], axis=1), jnp.concatenate([give, keep], axis=1))
    return (keys.T, values.T, rows.T)


def solution(mesh):
    placed = (
        P("grp", None),
        P("grp"),
        P("grp"),
        P(),
        P("grp", "dev"),
        P("grp", "dev"),
        P("grp", "dev"),
        P("grp", "dev"),
        P(),
        P("grp", "dev"),
        P("grp", "dev"),
        P("grp", "dev"),
    )
    return jax.shard_map(
        on_device,
        mesh=mesh,
        in_specs=placed,
        out_specs=(P("grp", "dev"), P("grp", "dev"), P("grp", "dev")),
        check_vma=False,
    )
```

```python
import math

import jax
import jax.numpy as jnp
from jax import lax
from jax.experimental import pallas as pl
from jax.experimental.pallas import tpu as pltpu
from jax.sharding import PartitionSpec as P

HEADS = 32
KV_HEADS = 8
HEAD_DIM = 128
ROW_LEN = 128
D = 4096
ROPE_BASE = 500000.0

GROUPS = 8
MEMBERS = 64
DEPTH = 16
HALF = 64
QC = 64
KC = 16
FC = 224
BAND = 256
RUN = 512

COLUMNS = [[4 * z + q for z in range(DEPTH)] for q in range(4)]
OCTETS = [[8 * z + m for m in range(8)] for z in range(8)]

BF = jnp.bfloat16
F32 = jnp.float32
VMEM = pl.BlockSpec(memory_space=pltpu.VMEM)
HBM = pl.BlockSpec(memory_space=pltpu.HBM)
ANY = pl.BlockSpec(memory_space=pl.ANY)
SMEM = pl.BlockSpec(memory_space=pltpu.SMEM)


def nt(a, b):
    return lax.dot_general(a, b, (((1,), (1,)), ((), ())), preferred_element_type=F32)


def whole(*shape):
    return pl.BlockSpec(shape, lambda i: (0,) * len(shape))


def params(mib):
    return pltpu.CompilerParams(vmem_limit_bytes=mib * 2**20)


def cost(flops, nbytes):
    return pl.CostEstimate(flops=flops, bytes_accessed=nbytes, transcendentals=0)


def project_kernel(normed, weights, cos, sin, send, keys, values):
    total = jnp.zeros((256, 96), F32)
    for g in range(GROUPS):
        total = total + nt(normed[g], weights[g, 0:96, :])
    total = jnp.concatenate([total, jnp.zeros((256, 32), F32)], axis=1)
    lane = lax.broadcasted_iota(jnp.int32, (256, 128), 1)
    partner = jnp.where(lane % 2 == 0, -pltpu.roll(total, 127, 1), pltpu.roll(total, 1, 1))
    turned = jnp.where(lane < QC + KC, total * cos[...] + partner * sin[...], total)
    turned = turned.astype(BF).astype(F32)
    flipped = turned.T
    keys[...] = flipped[QC : QC + KC, :].astype(BF)
    values[...] = flipped[QC + KC : QC + 2 * KC, :].astype(BF)
    lane = lax.broadcasted_iota(jnp.int32, (HALF, 128), 1)
    for zl in range(2):
        for yhi in range(2):
            for c in range(2):
                first = turned[c * 128 : c * 128 + HALF, :]
                second = turned[c * 128 + HALF : c * 128 + 128, :]
                mine = second if yhi else first
                chunk = jnp.where(lane < QC, mine, jnp.where(lane < 96, first, pltpu.roll(second, 32, 1)))
                send[zl * 4 + yhi * 2 + c] = chunk.astype(BF)


def attend_kernel(at, lengths, got, out):
    lane = lax.broadcasted_iota(jnp.int32, (HALF, 128), 1)
    pieces = [got[m].astype(F32) for m in range(8)]

    def gather(start):
        full = jnp.zeros((HALF, 128), F32)
        for m in range(8):
            full = jnp.where(lane // KC == m, pltpu.roll(pieces[m], (KC * m - start) % 128, 1), full)
        return full.astype(BF)

    keys = jnp.concatenate([gather(QC), gather(96)], axis=0)
    values = jnp.concatenate([gather(QC + KC), gather(96 + KC)], axis=0)
    slot = lax.broadcasted_iota(jnp.int32, (HALF, 128), 0) + at[1] * HALF
    allowed = (lane <= slot) & (lane < lengths[at[0]])
    for a in range(2):
        low = got[at[3] * 4 + a * 2].astype(F32)
        high = got[at[3] * 4 + a * 2 + 1].astype(F32)
        queries = jnp.where(lane < QC, low, pltpu.roll(high, QC, 1)).astype(BF)
        scores = nt(queries, keys) / math.sqrt(HEAD_DIM)
        scores = jnp.where(allowed, scores, -jnp.inf)
        expo = jnp.exp(scores - jnp.max(scores, axis=-1, keepdims=True))
        probs = (expo / jnp.sum(expo, axis=-1, keepdims=True)).astype(BF)
        mixed = jnp.dot(probs, values, preferred_element_type=F32).astype(BF)
        out[:, a * 128 : a * 128 + 128] = mixed


def output_kernel(at, got, mine, core, far, cross, own, out):
    parts = []
    for w in (mine, core, far, cross):
        total = jnp.zeros((HALF, QC), F32)
        for g in range(GROUPS):
            total = total + nt(got[2 * g], w[g, :, 0:BAND]) + nt(got[2 * g + 1], w[g, :, BAND:RUN])
        parts.append(total)
    blocks = []
    for j in range(4):
        picked = parts[0]
        for k in range(1, 4):
            picked = jnp.where(jnp.bitwise_xor(at[5], j) == k, parts[k], picked)
        blocks.append(picked)
    projected = jnp.concatenate(blocks, axis=1)
    attended = (own[...].astype(F32) + projected).astype(BF)
    out[...] = attended


def renorm(got, gain, out):
    squares = jnp.zeros((HALF, 1), F32)
    for z in range(DEPTH):
        x = got[z].astype(F32)
        squares = squares + jnp.sum(x * x, axis=-1, keepdims=True)
    scale = lax.rsqrt(squares * (1.0 / D) + 1e-05)
    for z in range(DEPTH):
        x = got[z].astype(F32) * scale * gain[:, z * BAND : (z + 1) * BAND]
        out[z // 2, :, (z % 2) * BAND : (z % 2 + 1) * BAND] = x.astype(BF)


def near_kernel(got, gain, mine, mine_lo, out):
    renorm(got, gain, out)


def hidden_kernel(at, near, full, far, gain, mine, mine_lo, core, core_lo, out, kept, normed):
    low = at[1] == 0
    lanes = pl.ds(pl.multiple_of(at[1] * 128, 128), 128)
    near_kept, far_kept = full[at[2], :, lanes], far[at[2], :, lanes]
    kept[0:HALF, :] = jnp.where(low, near_kept, far_kept)
    kept[HALF : 2 * HALF, :] = jnp.where(low, far_kept, near_kept)
    renorm(far, gain, normed)
    totals = [jnp.zeros((2 * HALF, FC), F32) for _ in range(4)]
    for x in range(4):
        for side, pair in enumerate(((mine, core), (mine_lo, core_lo))):
            g = jnp.bitwise_xor(at[6], side) * 4 + x
            rows = jnp.concatenate([near[g], normed[g]], axis=0)
            for i, w in enumerate(pair):
                totals[2 * i] = totals[2 * i] + nt(rows, w[x, 0:FC, :])
                totals[2 * i + 1] = totals[2 * i + 1] + nt(rows, w[x, FC : 2 * FC, :])
    for i in range(2):
        gate = totals[2 * i]
        units = (gate / (1.0 + jnp.exp(-gate)) * totals[2 * i + 1]).astype(BF)
        first, second = units[0:HALF, :], units[HALF : 2 * HALF, :]
        out[i, 0:HALF, :] = jnp.where(low, first, second)
        out[i, HALF : 2 * HALF, :] = jnp.where(low, second, first)


def down_kernel(at, units, far_units, mine, mine_lo, core, core_lo, out):
    for x in range(4):
        for side, pair in enumerate(((mine, core), (mine_lo, core_lo))):
            total = jnp.zeros((128, BAND), F32)
            for i, w in enumerate(pair):
                total = total + jnp.dot(units[i], w[x, 2 * FC : 3 * FC, 0:BAND], preferred_element_type=F32)
                total = total + jnp.dot(far_units[i], w[x, 2 * FC : 3 * FC, BAND:RUN], preferred_element_type=F32)
            z = (jnp.bitwise_xor(at[6], side) * 4 + x) * 2
            out[z] = total[:, 0:128].astype(BF)
            out[z + 1] = total[:, 128:256].astype(BF)


def finish_kernel(at, got, kept, keep, give):
    total = kept[...].astype(F32)
    for z in range(DEPTH):
        total = total + got[z].astype(F32)
    result = total.T
    head, tail = result[0:QC, :], result[QC : 2 * QC, :]
    keep[...] = jnp.where(at[0] == 0, head, tail).astype(BF)
    give[...] = jnp.where(at[0] == 0, tail, head).astype(BF)


def pack_kernel(query, key, value, out_part, out, token, held, sems):
    token[...] = jnp.zeros_like(token)
    spans = ((query, 0, QC), (key, QC, KC), (value, QC + KC, KC), (out_part, 96, QC))
    reads = [
        pltpu.make_async_copy(ref, held.at[pl.ds(start, rows), :], sems.at[i])
        for i, (ref, start, rows) in enumerate(spans)
    ]
    for copy in reads:
        copy.start()
    for copy in reads:
        copy.wait()
    writes = [pltpu.make_async_copy(held, out.at[g], sems.at[4 + g]) for g in range(GROUPS)]
    for copy in writes:
        copy.start()
    for copy in writes:
        copy.wait()


def divide_kernel(at, after, narrow, keep, give, held, sem):
    copy = pltpu.make_async_copy(narrow, held, sem.at[0])
    copy.start()
    copy.wait()
    low = at[1] == 0
    for i in range(2):
        even = held[:, 2 * i * 128 : (2 * i + 1) * 128]
        odd = held[:, (2 * i + 1) * 128 : (2 * i + 2) * 128]
        keep[:, i * 128 : (i + 1) * 128] = jnp.where(low, even, odd)
        give[:, i * 128 : (i + 1) * 128] = jnp.where(low, odd, even)


def divide(at, after, narrow):
    half = jax.ShapeDtypeStruct((FC, BAND), BF)
    return pl.pallas_call(
        divide_kernel,
        out_shape=(half, half),
        in_specs=[SMEM, ANY, HBM],
        out_specs=(VMEM,) * 2,
        scratch_shapes=[pltpu.VMEM((FC, RUN), BF), pltpu.SemaphoreType.DMA((1,))],
        compiler_params=params(57),
        name="divide",
    )(at, after, narrow)


def norm_kernel(at, after, tables, stream, gain, normed, own, held, gains, sems):
    copies = [
        pltpu.make_async_copy(stream, held, sems.at[0]),
        pltpu.make_async_copy(gain, gains, sems.at[1]),
    ]
    for copy in copies:
        copy.start()
    for copy in copies:
        copy.wait()
    x = held[...].astype(F32)
    scale = lax.rsqrt(jnp.mean(x * x, axis=-1, keepdims=True) + 1e-05)
    for g in range(GROUPS):
        cols = pl.ds(g * RUN, RUN)
        normed[g] = (held[:, cols].astype(F32) * scale * gains[:, cols]).astype(BF)
    rows = pl.ds(pl.multiple_of(at[0] * 128 + at[1] * HALF, HALF), HALF)
    own[...] = held[rows, pl.ds(pl.multiple_of(at[2] * BAND, BAND), BAND)]


def norm(at, after, tables, stream, gain):
    return pl.pallas_call(
        norm_kernel,
        out_shape=(jax.ShapeDtypeStruct((GROUPS, 256, RUN), BF), jax.ShapeDtypeStruct((HALF, BAND), BF)),
        in_specs=[SMEM, ANY, ANY, HBM, HBM],
        out_specs=(VMEM,) * 2,
        scratch_shapes=[pltpu.VMEM((256, D), BF), pltpu.VMEM((1, D), F32), pltpu.SemaphoreType.DMA((2,))],
        compiler_params=params(50),
        name="norm",
    )(at, after, tables, stream, gain)


def join_kernel(after, gate, up, keep, got, out, sems):
    copies = [
        pltpu.make_async_copy(gate, out.at[pl.ds(0, FC), :], sems.at[0]),
        pltpu.make_async_copy(up, out.at[pl.ds(FC, FC), :], sems.at[1]),
    ]
    for copy in copies:
        copy.start()
    out[2 * FC : 3 * FC, 0:BAND] = keep[...]
    out[2 * FC : 3 * FC, BAND:RUN] = got[...]
    for copy in copies:
        copy.wait()


def join(after, gate, up, keep, got):
    return pl.pallas_call(
        join_kernel,
        out_shape=jax.ShapeDtypeStruct((3 * FC, RUN), BF),
        in_specs=[ANY, HBM, HBM, VMEM, VMEM],
        out_specs=VMEM,
        scratch_shapes=[pltpu.SemaphoreType.DMA((2,))],
        compiler_params=params(16),
        name="join",
    )(after, gate, up, keep, got)


def pack(*parts):
    return pl.pallas_call(
        pack_kernel,
        out_shape=(jax.ShapeDtypeStruct((GROUPS, 160, RUN), BF), jax.ShapeDtypeStruct((8, 128), F32)),
        in_specs=[HBM] * 4,
        out_specs=(HBM, VMEM),
        scratch_shapes=[pltpu.VMEM((160, RUN), BF), pltpu.SemaphoreType.DMA((4 + GROUPS,))],
        compiler_params=params(60),
        name="pack",
    )(*parts)


def project(normed, weights, cos, sin):
    return pl.pallas_call(
        project_kernel,
        out_shape=(
            jax.ShapeDtypeStruct((8, HALF, 128), BF),
            jax.ShapeDtypeStruct((KC, 256), BF),
            jax.ShapeDtypeStruct((KC, 256), BF),
        ),
        in_specs=[VMEM] * 4,
        out_specs=(VMEM,) * 3,
        compiler_params=params(24),
        name="project",
    )(normed, weights, cos, sin)


def attend(at, lengths, got):
    return pl.pallas_call(
        attend_kernel,
        out_shape=jax.ShapeDtypeStruct((HALF, BAND), BF),
        in_specs=[SMEM, SMEM, VMEM],
        out_specs=VMEM,
        compiler_params=params(16),
        name="attend",
    )(at, lengths, got)


def output(at, got, weights, own):
    return pl.pallas_call(
        output_kernel,
        out_shape=jax.ShapeDtypeStruct((HALF, BAND), BF),
        in_specs=[SMEM] + [VMEM] * 6,
        out_specs=VMEM,
        compiler_params=params(24),
        name="output",
    )(at, got, *weights, own)


def near_half(got, gain, mine, mine_lo):
    return pl.pallas_call(
        near_kernel,
        out_shape=jax.ShapeDtypeStruct((GROUPS, HALF, RUN), BF),
        in_specs=[VMEM] * 4,
        out_specs=VMEM,
        compiler_params=params(16),
        name="near_half",
    )(got, gain, mine, mine_lo)


def hidden_units(at, near, full, far, gain, weights):
    return pl.pallas_call(
        hidden_kernel,
        out_shape=(jax.ShapeDtypeStruct((2, 128, FC), BF), jax.ShapeDtypeStruct((128, 128), BF)),
        in_specs=[SMEM] + [VMEM] * 8,
        out_specs=(VMEM, VMEM),
        scratch_shapes=[pltpu.VMEM((GROUPS, HALF, RUN), BF)],
        compiler_params=params(16),
        cost_estimate=cost(4 * HALF * D * 4 * FC, 8 * 2**20),
        name="hidden",
    )(at, near, full, far, gain, *weights)


def down(at, units, far_units, weights):
    return pl.pallas_call(
        down_kernel,
        out_shape=jax.ShapeDtypeStruct((DEPTH, 128, 128), BF),
        in_specs=[SMEM] + [VMEM] * 6,
        out_specs=VMEM,
        compiler_params=params(16),
        cost_estimate=cost(4 * HALF * D * 2 * FC, 5 * 2**20),
        name="down",
    )(at, units, far_units, *weights)


def finish(at, got, kept):
    return pl.pallas_call(
        finish_kernel,
        out_shape=(jax.ShapeDtypeStruct((QC, 128), BF),) * 2,
        in_specs=[SMEM] + [VMEM] * 2,
        out_specs=(VMEM, VMEM),
        compiler_params=params(16),
        name="finish",
    )(at, got, kept)


def swap(x, bits):
    return lax.ppermute(x, "dev", [(d, d ^ bits) for d in range(MEMBERS)])


def swap_groups(x):
    return lax.ppermute(x, "grp", [(g, g ^ 4) for g in range(GROUPS)])


def collect_x(x):
    return lax.all_gather(x, "grp", axis=0, axis_index_groups=[[0, 1, 2, 3], [4, 5, 6, 7]])


def trade(x, groups):
    return lax.all_to_all(x, "dev", 0, 0, axis_index_groups=groups, tiled=True)


def collect(x):
    return lax.all_gather(x, "dev", axis=0, axis_index_groups=COLUMNS)


def after(x, other):
    return lax.optimization_barrier((x, other))[0]


def on_device(
    stream,
    row_length,
    row_start,
    attn_gain,
    w_query,
    w_key,
    w_value,
    w_out,
    ffn_gain,
    w_gate,
    w_up,
    w_down,
):
    member = lax.axis_index("dev")
    core, yhi, z, quad = member % 2, member // 2 % 2, member // 4, member % 4
    ylo = lax.axis_index("grp") // 4
    at = jnp.stack([core, yhi, z, z % 2, z // 2, quad, ylo]).astype(jnp.int32)

    packed, token = pack(w_query.T, w_key.T, w_value.T, w_out.T)
    first = lax.all_to_all(packed, "grp", 0, 0, tiled=True)

    lane = jnp.arange(128, dtype=jnp.int32)
    column = jnp.where(lane < QC, member * QC + lane, member * KC + lane - QC)
    pair = (column % HEAD_DIM // 2).astype(F32)
    freq = jnp.exp(-(2.0 * pair / HEAD_DIM) * math.log(ROPE_BASE))
    positions = (row_start[:, None] + jnp.arange(ROW_LEN, dtype=jnp.int32)[None, :]).reshape(-1)
    angle = positions.astype(F32)[:, None] * freq[None, :]
    cos, sin = jnp.cos(angle), jnp.sin(angle)

    keep, give = divide(at, token, w_down.T)
    other = swap(give, 2)
    normed, own = norm(at, give, cos, stream, attn_gain.reshape(1, D))
    send, keys, values = project(normed, first, cos, sin)
    got = trade(send, OCTETS)
    mine = join(send, w_gate.T, w_up.T, keep, other)
    own_mixed = attend(at, row_length, got)
    mine_lo = after(swap_groups(mine), own_mixed)
    mine, mine_lo = collect_x(mine), collect_x(mine_lo)
    out_own = first[:, 96:160, :]
    out_weights = (out_own, swap(out_own, 1), swap(out_own, 2), swap(out_own, 3))
    mixed = collect(own_mixed)
    attended = output(at, mixed, out_weights, own)
    full = collect(attended)
    far = swap(full, 2)
    mine, mine_lo = after((mine, mine_lo), full)
    weights = (mine, mine_lo, swap(mine, 1), swap(mine_lo, 1))
    gain = ffn_gain.reshape(1, D)
    near = near_half(full, gain, mine, mine_lo)
    units, kept = hidden_units(at, near, full, far, gain, weights)
    sums = trade(down(at, units, swap(units, 2), weights), COLUMNS)
    keep, give = finish(at, sums, kept)
    give = swap(give, 1)
    rows = jnp.where(core == 0, jnp.concatenate([keep, give], axis=1), jnp.concatenate([give, keep], axis=1))
    return (keys.T, values.T, rows.T)


def solution(mesh):
    placed = (
        P("grp", None),
        P("grp"),
        P("grp"),
        P(),
        P("grp", "dev"),
        P("grp", "dev"),
        P("grp", "dev"),
        P("grp", "dev"),
        P(),
        P("grp", "dev"),
        P("grp", "dev"),
        P("grp", "dev"),
    )
    return jax.shard_map(
        on_device,
        mesh=mesh,
        in_specs=placed,
        out_specs=(P("grp", "dev"), P("grp", "dev"), P("grp", "dev")),
        check_vma=False,
    )
```

```python
import math

import jax
import jax.numpy as jnp
from jax import lax
from jax.experimental import pallas as pl
from jax.experimental.pallas import tpu as pltpu
from jax.sharding import PartitionSpec as P

HEADS = 32
KV_HEADS = 8
HEAD_DIM = 128
ROW_LEN = 128
D = 4096
ROPE_BASE = 500000.0

GROUPS = 8
MEMBERS = 64
DEPTH = 16
HALF = 64
QC = 64
KC = 16
FC = 224
BAND = 256
RUN = 512

COLUMNS = [[4 * z + q for z in range(DEPTH)] for q in range(4)]
OCTETS = [[8 * z + m for m in range(8)] for z in range(8)]

BF = jnp.bfloat16
F32 = jnp.float32
VMEM = pl.BlockSpec(memory_space=pltpu.VMEM)
HBM = pl.BlockSpec(memory_space=pltpu.HBM)
ANY = pl.BlockSpec(memory_space=pl.ANY)
SMEM = pl.BlockSpec(memory_space=pltpu.SMEM)


def nt(a, b):
    return lax.dot_general(a, b, (((1,), (1,)), ((), ())), preferred_element_type=F32)


def whole(*shape):
    return pl.BlockSpec(shape, lambda i: (0,) * len(shape))


def params(mib):
    return pltpu.CompilerParams(vmem_limit_bytes=mib * 2**20)


def cost(flops, nbytes):
    return pl.CostEstimate(flops=flops, bytes_accessed=nbytes, transcendentals=0)


def project_kernel(normed, weights, cos, sin, send, keys, values):
    total = jnp.zeros((256, 96), F32)
    for g in range(GROUPS):
        total = total + nt(normed[g], weights[g, 0:96, :])
    total = jnp.concatenate([total, jnp.zeros((256, 32), F32)], axis=1)
    lane = lax.broadcasted_iota(jnp.int32, (256, 128), 1)
    partner = jnp.where(lane % 2 == 0, -pltpu.roll(total, 127, 1), pltpu.roll(total, 1, 1))
    turned = jnp.where(lane < QC + KC, total * cos[...] + partner * sin[...], total)
    turned = turned.astype(BF).astype(F32)
    flipped = turned.T
    keys[...] = flipped[QC : QC + KC, :].astype(BF)
    values[...] = flipped[QC + KC : QC + 2 * KC, :].astype(BF)
    lane = lax.broadcasted_iota(jnp.int32, (HALF, 128), 1)
    for zl in range(2):
        for yhi in range(2):
            for c in range(2):
                first = turned[c * 128 : c * 128 + HALF, :]
                second = turned[c * 128 + HALF : c * 128 + 128, :]
                mine = second if yhi else first
                chunk = jnp.where(lane < QC, mine, jnp.where(lane < 96, first, pltpu.roll(second, 32, 1)))
                send[zl * 4 + yhi * 2 + c] = chunk.astype(BF)


def attend_kernel(at, lengths, got, out):
    lane = lax.broadcasted_iota(jnp.int32, (HALF, 128), 1)
    pieces = [got[m].astype(F32) for m in range(8)]

    def gather(start):
        full = jnp.zeros((HALF, 128), F32)
        for m in range(8):
            full = jnp.where(lane // KC == m, pltpu.roll(pieces[m], (KC * m - start) % 128, 1), full)
        return full.astype(BF)

    keys = jnp.concatenate([gather(QC), gather(96)], axis=0)
    values = jnp.concatenate([gather(QC + KC), gather(96 + KC)], axis=0)
    slot = lax.broadcasted_iota(jnp.int32, (HALF, 128), 0) + at[1] * HALF
    allowed = (lane <= slot) & (lane < lengths[at[0]])
    for a in range(2):
        low = got[at[3] * 4 + a * 2].astype(F32)
        high = got[at[3] * 4 + a * 2 + 1].astype(F32)
        queries = jnp.where(lane < QC, low, pltpu.roll(high, QC, 1)).astype(BF)
        scores = nt(queries, keys) / math.sqrt(HEAD_DIM)
        scores = jnp.where(allowed, scores, -jnp.inf)
        expo = jnp.exp(scores - jnp.max(scores, axis=-1, keepdims=True))
        probs = (expo / jnp.sum(expo, axis=-1, keepdims=True)).astype(BF)
        mixed = jnp.dot(probs, values, preferred_element_type=F32).astype(BF)
        out[:, a * 128 : a * 128 + 128] = mixed


def output_kernel(at, got, mine, core, far, cross, own, out):
    parts = []
    for w in (mine, core, far, cross):
        total = jnp.zeros((HALF, QC), F32)
        for g in range(GROUPS):
            total = total + nt(got[2 * g], w[g, :, 0:BAND]) + nt(got[2 * g + 1], w[g, :, BAND:RUN])
        parts.append(total)
    blocks = []
    for j in range(4):
        picked = parts[0]
        for k in range(1, 4):
            picked = jnp.where(jnp.bitwise_xor(at[5], j) == k, parts[k], picked)
        blocks.append(picked)
    projected = jnp.concatenate(blocks, axis=1)
    attended = (own[...].astype(F32) + projected).astype(BF)
    out[...] = attended


def renorm(got, gain, out):
    squares = jnp.zeros((HALF, 1), F32)
    for z in range(DEPTH):
        x = got[z].astype(F32)
        squares = squares + jnp.sum(x * x, axis=-1, keepdims=True)
    scale = lax.rsqrt(squares * (1.0 / D) + 1e-05)
    for z in range(DEPTH):
        x = got[z].astype(F32) * scale * gain[:, z * BAND : (z + 1) * BAND]
        out[z // 2, :, (z % 2) * BAND : (z % 2 + 1) * BAND] = x.astype(BF)


def near_kernel(got, gain, out):
    renorm(got, gain, out)


def hidden_kernel(at, near, full, far, gain, mine, mine_lo, core, core_lo, out, kept, normed):
    low = at[1] == 0
    lanes = pl.ds(pl.multiple_of(at[1] * 128, 128), 128)
    near_kept, far_kept = full[at[2], :, lanes], far[at[2], :, lanes]
    kept[0:HALF, :] = jnp.where(low, near_kept, far_kept)
    kept[HALF : 2 * HALF, :] = jnp.where(low, far_kept, near_kept)
    renorm(far, gain, normed)
    totals = [jnp.zeros((2 * HALF, FC), F32) for _ in range(4)]
    for x in range(4):
        for side, pair in enumerate(((mine, core), (mine_lo, core_lo))):
            g = jnp.bitwise_xor(at[6], side) * 4 + x
            rows = jnp.concatenate([near[g], normed[g]], axis=0)
            for i, w in enumerate(pair):
                totals[2 * i] = totals[2 * i] + nt(rows, w[x, 0:FC, :])
                totals[2 * i + 1] = totals[2 * i + 1] + nt(rows, w[x, FC : 2 * FC, :])
    for i in range(2):
        gate = totals[2 * i]
        units = (gate / (1.0 + jnp.exp(-gate)) * totals[2 * i + 1]).astype(BF)
        first, second = units[0:HALF, :], units[HALF : 2 * HALF, :]
        out[i, 0:HALF, :] = jnp.where(low, first, second)
        out[i, HALF : 2 * HALF, :] = jnp.where(low, second, first)


def down_kernel(at, units, far_units, mine, mine_lo, core, core_lo, out):
    for x in range(4):
        for side, pair in enumerate(((mine, core), (mine_lo, core_lo))):
            total = jnp.zeros((128, BAND), F32)
            for i, w in enumerate(pair):
                total = total + jnp.dot(units[i], w[x, 2 * FC : 3 * FC, 0:BAND], preferred_element_type=F32)
                total = total + jnp.dot(far_units[i], w[x, 2 * FC : 3 * FC, BAND:RUN], preferred_element_type=F32)
            z = (jnp.bitwise_xor(at[6], side) * 4 + x) * 2
            out[z] = total[:, 0:128].astype(BF)
            out[z + 1] = total[:, 128:256].astype(BF)


def finish_kernel(at, got, kept, keep, give):
    total = kept[...].astype(F32)
    for z in range(DEPTH):
        total = total + got[z].astype(F32)
    result = total.T
    head, tail = result[0:QC, :], result[QC : 2 * QC, :]
    keep[...] = jnp.where(at[0] == 0, head, tail).astype(BF)
    give[...] = jnp.where(at[0] == 0, tail, head).astype(BF)


def pack_kernel(query, key, value, out_part, out, token, held, sems):
    token[...] = jnp.zeros_like(token)
    spans = ((query, 0, QC), (key, QC, KC), (value, QC + KC, KC), (out_part, 96, QC))
    reads = [
        pltpu.make_async_copy(ref, held.at[pl.ds(start, rows), :], sems.at[i])
        for i, (ref, start, rows) in enumerate(spans)
    ]
    for copy in reads:
        copy.start()
    for copy in reads:
        copy.wait()
    writes = [pltpu.make_async_copy(held, out.at[g], sems.at[4 + g]) for g in range(GROUPS)]
    for copy in writes:
        copy.start()
    for copy in writes:
        copy.wait()


def norm_kernel(at, after, tables, stream, gain, normed, own, held, gains, sems):
    copies = [
        pltpu.make_async_copy(stream, held, sems.at[0]),
        pltpu.make_async_copy(gain, gains, sems.at[1]),
    ]
    for copy in copies:
        copy.start()
    for copy in copies:
        copy.wait()
    x = held[...].astype(F32)
    scale = lax.rsqrt(jnp.mean(x * x, axis=-1, keepdims=True) + 1e-05)
    for g in range(GROUPS):
        cols = pl.ds(g * RUN, RUN)
        normed[g] = (held[:, cols].astype(F32) * scale * gains[:, cols]).astype(BF)
    rows = pl.ds(pl.multiple_of(at[0] * 128 + at[1] * HALF, HALF), HALF)
    own[...] = held[rows, pl.ds(pl.multiple_of(at[2] * BAND, BAND), BAND)]


def norm(at, after, tables, stream, gain):
    return pl.pallas_call(
        norm_kernel,
        out_shape=(jax.ShapeDtypeStruct((GROUPS, 256, RUN), BF), jax.ShapeDtypeStruct((HALF, BAND), BF)),
        in_specs=[SMEM, ANY, ANY, HBM, HBM],
        out_specs=(VMEM,) * 2,
        scratch_shapes=[pltpu.VMEM((256, D), BF), pltpu.VMEM((1, D), F32), pltpu.SemaphoreType.DMA((2,))],
        compiler_params=params(50),
        name="norm",
    )(at, after, tables, stream, gain)


def join_kernel(at, after, gate, up, narrow, got, out, held, sems):
    copies = [
        pltpu.make_async_copy(narrow, held, sems.at[0]),
        pltpu.make_async_copy(gate, out.at[pl.ds(0, FC), :], sems.at[1]),
        pltpu.make_async_copy(up, out.at[pl.ds(FC, FC), :], sems.at[2]),
    ]
    for copy in copies:
        copy.start()
    low = at[1] == 0
    for k, source in ((1, got), (0, held)):
        if k == 0:
            copies[0].wait()
        for i in range(2):
            even = source[:, 2 * i * 128 : (2 * i + 1) * 128]
            odd = source[:, (2 * i + 1) * 128 : (2 * i + 2) * 128]
            out[2 * FC : 3 * FC, k * BAND + i * 128 : k * BAND + (i + 1) * 128] = jnp.where(low, even, odd)
    copies[1].wait()
    copies[2].wait()


def join(at, after, gate, up, narrow, got):
    return pl.pallas_call(
        join_kernel,
        out_shape=jax.ShapeDtypeStruct((3 * FC, RUN), BF),
        in_specs=[SMEM, ANY, HBM, HBM, HBM, VMEM],
        out_specs=VMEM,
        scratch_shapes=[pltpu.VMEM((FC, RUN), BF), pltpu.SemaphoreType.DMA((3,))],
        compiler_params=params(48),
        name="join",
    )(at, after, gate, up, narrow, got)


def pack(*parts):
    return pl.pallas_call(
        pack_kernel,
        out_shape=(jax.ShapeDtypeStruct((GROUPS, 160, RUN), BF), jax.ShapeDtypeStruct((8, 128), F32)),
        in_specs=[HBM] * 4,
        out_specs=(HBM, VMEM),
        scratch_shapes=[pltpu.VMEM((160, RUN), BF), pltpu.SemaphoreType.DMA((4 + GROUPS,))],
        compiler_params=params(60),
        name="pack",
    )(*parts)


def project(normed, weights, cos, sin):
    return pl.pallas_call(
        project_kernel,
        out_shape=(
            jax.ShapeDtypeStruct((8, HALF, 128), BF),
            jax.ShapeDtypeStruct((KC, 256), BF),
            jax.ShapeDtypeStruct((KC, 256), BF),
        ),
        in_specs=[VMEM] * 4,
        out_specs=(VMEM,) * 3,
        compiler_params=params(24),
        name="project",
    )(normed, weights, cos, sin)


def attend(at, lengths, got):
    return pl.pallas_call(
        attend_kernel,
        out_shape=jax.ShapeDtypeStruct((HALF, BAND), BF),
        in_specs=[SMEM, SMEM, VMEM],
        out_specs=VMEM,
        compiler_params=params(16),
        name="attend",
    )(at, lengths, got)


def output(at, got, weights, own):
    return pl.pallas_call(
        output_kernel,
        out_shape=jax.ShapeDtypeStruct((HALF, BAND), BF),
        in_specs=[SMEM] + [VMEM] * 6,
        out_specs=VMEM,
        compiler_params=params(24),
        name="output",
    )(at, got, *weights, own)


def near_half(got, gain):
    return pl.pallas_call(
        near_kernel,
        out_shape=jax.ShapeDtypeStruct((GROUPS, HALF, RUN), BF),
        in_specs=[VMEM] * 2,
        out_specs=VMEM,
        compiler_params=params(16),
        name="near_half",
    )(got, gain)


def hidden_units(at, near, full, far, gain, weights):
    return pl.pallas_call(
        hidden_kernel,
        out_shape=(jax.ShapeDtypeStruct((2, 128, FC), BF), jax.ShapeDtypeStruct((128, 128), BF)),
        in_specs=[SMEM] + [VMEM] * 8,
        out_specs=(VMEM, VMEM),
        scratch_shapes=[pltpu.VMEM((GROUPS, HALF, RUN), BF)],
        compiler_params=params(16),
        cost_estimate=cost(4 * HALF * D * 4 * FC, 8 * 2**20),
        name="hidden",
    )(at, near, full, far, gain, *weights)


def down(at, units, far_units, weights):
    return pl.pallas_call(
        down_kernel,
        out_shape=jax.ShapeDtypeStruct((DEPTH, 128, 128), BF),
        in_specs=[SMEM] + [VMEM] * 6,
        out_specs=VMEM,
        compiler_params=params(16),
        cost_estimate=cost(4 * HALF * D * 2 * FC, 5 * 2**20),
        name="down",
    )(at, units, far_units, *weights)


def finish(at, got, kept):
    return pl.pallas_call(
        finish_kernel,
        out_shape=(jax.ShapeDtypeStruct((QC, 128), BF),) * 2,
        in_specs=[SMEM] + [VMEM] * 2,
        out_specs=(VMEM, VMEM),
        compiler_params=params(16),
        name="finish",
    )(at, got, kept)


def swap(x, bits):
    return lax.ppermute(x, "dev", [(d, d ^ bits) for d in range(MEMBERS)])


def swap_groups(x):
    return lax.ppermute(x, "grp", [(g, g ^ 4) for g in range(GROUPS)])


def collect_x(x):
    return lax.all_gather(x, "grp", axis=0, axis_index_groups=[[0, 1, 2, 3], [4, 5, 6, 7]])


def trade(x, groups):
    return lax.all_to_all(x, "dev", 0, 0, axis_index_groups=groups, tiled=True)


def collect(x):
    return lax.all_gather(x, "dev", axis=0, axis_index_groups=COLUMNS)


def after(x, other):
    return lax.optimization_barrier((x, other))[0]


def on_device(
    stream,
    row_length,
    row_start,
    attn_gain,
    w_query,
    w_key,
    w_value,
    w_out,
    ffn_gain,
    w_gate,
    w_up,
    w_down,
):
    member = lax.axis_index("dev")
    core, yhi, z, quad = member % 2, member // 2 % 2, member // 4, member % 4
    ylo = lax.axis_index("grp") // 4
    at = jnp.stack([core, yhi, z, z % 2, z // 2, quad, ylo]).astype(jnp.int32)

    packed, token = pack(w_query.T, w_key.T, w_value.T, w_out.T)
    first = lax.all_to_all(packed, "grp", 0, 0, tiled=True)

    lane = jnp.arange(128, dtype=jnp.int32)
    column = jnp.where(lane < QC, member * QC + lane, member * KC + lane - QC)
    pair = (column % HEAD_DIM // 2).astype(F32)
    freq = jnp.exp(-(2.0 * pair / HEAD_DIM) * math.log(ROPE_BASE))
    positions = (row_start[:, None] + jnp.arange(ROW_LEN, dtype=jnp.int32)[None, :]).reshape(-1)
    angle = positions.astype(F32)[:, None] * freq[None, :]
    cos, sin = jnp.cos(angle), jnp.sin(angle)

    normed, own = norm(at, token, cos, stream, attn_gain.reshape(1, D))
    narrow = after(w_down.T, token)
    other = swap(narrow, 2)

    send, keys, values = project(normed, first, cos, sin)
    got = trade(send, OCTETS)
    mine = join(at, send, w_gate.T, w_up.T, narrow, other)
    mine_lo = swap_groups(after(mine, got))
    out_own = first[:, 96:160, :]
    out_weights = (out_own, swap(out_own, 1), swap(out_own, 2), swap(out_own, 3))
    mixed = collect(attend(at, row_length, got))
    attended = output(at, mixed, out_weights, own)
    mine, mine_lo = collect_x(mine), collect_x(after(mine_lo, attended))
    mine = after(mine, attended)
    core_mine = swap(mine, 1)
    full = collect(attended)
    far = swap(full, 2)
    mine_lo = after(mine_lo, far)
    weights = (mine, mine_lo, core_mine, swap(mine_lo, 1))
    gain = ffn_gain.reshape(1, D)
    near = near_half(full, gain)
    units, kept = hidden_units(at, near, full, far, gain, weights)
    sums = trade(down(at, units, swap(units, 2), weights), COLUMNS)
    keep, give = finish(at, sums, kept)
    give = swap(give, 1)
    rows = jnp.where(core == 0, jnp.concatenate([keep, give], axis=1), jnp.concatenate([give, keep], axis=1))
    return (keys.T, values.T, rows.T)


def solution(mesh):
    placed = (
        P("grp", None),
        P("grp"),
        P("grp"),
        P(),
        P("grp", "dev"),
        P("grp", "dev"),
        P("grp", "dev"),
        P("grp", "dev"),
        P(),
        P("grp", "dev"),
        P("grp", "dev"),
        P("grp", "dev"),
    )
    return jax.shard_map(
        on_device,
        mesh=mesh,
        in_specs=placed,
        out_specs=(P("grp", "dev"), P("grp", "dev"), P("grp", "dev")),
        check_vma=False,
    )
```

```python
import math

import jax
import jax.numpy as jnp
from jax import lax
from jax.experimental import pallas as pl
from jax.experimental.pallas import tpu as pltpu
from jax.sharding import PartitionSpec as P

HEADS = 32
KV_HEADS = 8
HEAD_DIM = 128
ROW_LEN = 128
D = 4096
ROPE_BASE = 500000.0

GROUPS = 8
MEMBERS = 64
DEPTH = 16
HALF = 64
QC = 64
KC = 16
FC = 224
BAND = 256
RUN = 512

COLUMNS = [[4 * z + q for z in range(DEPTH)] for q in range(4)]
OCTETS = [[8 * z + m for m in range(8)] for z in range(8)]

BF = jnp.bfloat16
F32 = jnp.float32
VMEM = pl.BlockSpec(memory_space=pltpu.VMEM)
HBM = pl.BlockSpec(memory_space=pltpu.HBM)
ANY = pl.BlockSpec(memory_space=pl.ANY)
SMEM = pl.BlockSpec(memory_space=pltpu.SMEM)


def nt(a, b):
    return lax.dot_general(a, b, (((1,), (1,)), ((), ())), preferred_element_type=F32)


def whole(*shape):
    return pl.BlockSpec(shape, lambda i: (0,) * len(shape))


def params(mib):
    return pltpu.CompilerParams(vmem_limit_bytes=mib * 2**20)


def cost(flops, nbytes):
    return pl.CostEstimate(flops=flops, bytes_accessed=nbytes, transcendentals=0)


def project_kernel(normed, weights, cos, sin, send, keys, values):
    total = jnp.zeros((256, 96), F32)
    for g in range(GROUPS):
        total = total + nt(normed[g], weights[g, 0:96, :])
    total = jnp.concatenate([total, jnp.zeros((256, 32), F32)], axis=1)
    lane = lax.broadcasted_iota(jnp.int32, (256, 128), 1)
    partner = jnp.where(lane % 2 == 0, -pltpu.roll(total, 127, 1), pltpu.roll(total, 1, 1))
    turned = jnp.where(lane < QC + KC, total * cos[...] + partner * sin[...], total)
    turned = turned.astype(BF).astype(F32)
    flipped = turned.T
    keys[...] = flipped[QC : QC + KC, :].astype(BF)
    values[...] = flipped[QC + KC : QC + 2 * KC, :].astype(BF)
    lane = lax.broadcasted_iota(jnp.int32, (HALF, 128), 1)
    for zl in range(2):
        for yhi in range(2):
            for c in range(2):
                first = turned[c * 128 : c * 128 + HALF, :]
                second = turned[c * 128 + HALF : c * 128 + 128, :]
                mine = second if yhi else first
                chunk = jnp.where(lane < QC, mine, jnp.where(lane < 96, first, pltpu.roll(second, 32, 1)))
                send[zl * 4 + yhi * 2 + c] = chunk.astype(BF)


def attend_kernel(at, lengths, got, out):
    lane = lax.broadcasted_iota(jnp.int32, (HALF, 128), 1)
    pieces = [got[m].astype(F32) for m in range(8)]

    def gather(start):
        full = jnp.zeros((HALF, 128), F32)
        for m in range(8):
            full = jnp.where(lane // KC == m, pltpu.roll(pieces[m], (KC * m - start) % 128, 1), full)
        return full.astype(BF)

    keys = jnp.concatenate([gather(QC), gather(96)], axis=0)
    values = jnp.concatenate([gather(QC + KC), gather(96 + KC)], axis=0)
    slot = lax.broadcasted_iota(jnp.int32, (HALF, 128), 0) + at[1] * HALF
    allowed = (lane <= slot) & (lane < lengths[at[0]])
    for a in range(2):
        low = got[at[3] * 4 + a * 2].astype(F32)
        high = got[at[3] * 4 + a * 2 + 1].astype(F32)
        queries = jnp.where(lane < QC, low, pltpu.roll(high, QC, 1)).astype(BF)
        scores = nt(queries, keys) / math.sqrt(HEAD_DIM)
        scores = jnp.where(allowed, scores, -jnp.inf)
        expo = jnp.exp(scores - jnp.max(scores, axis=-1, keepdims=True))
        probs = (expo / jnp.sum(expo, axis=-1, keepdims=True)).astype(BF)
        mixed = jnp.dot(probs, values, preferred_element_type=F32).astype(BF)
        out[:, a * 128 : a * 128 + 128] = mixed


def output_kernel(at, got, mine, core, far, cross, own, out):
    parts = []
    for w in (mine, core, far, cross):
        total = jnp.zeros((HALF, QC), F32)
        for g in range(GROUPS):
            total = total + nt(got[2 * g], w[g, :, 0:BAND]) + nt(got[2 * g + 1], w[g, :, BAND:RUN])
        parts.append(total)
    blocks = []
    for j in range(4):
        picked = parts[0]
        for k in range(1, 4):
            picked = jnp.where(jnp.bitwise_xor(at[5], j) == k, parts[k], picked)
        blocks.append(picked)
    projected = jnp.concatenate(blocks, axis=1)
    attended = (own[...].astype(F32) + projected).astype(BF)
    out[...] = attended


def renorm(got, gain, out):
    squares = jnp.zeros((HALF, 1), F32)
    for z in range(DEPTH):
        x = got[z].astype(F32)
        squares = squares + jnp.sum(x * x, axis=-1, keepdims=True)
    scale = lax.rsqrt(squares * (1.0 / D) + 1e-05)
    for z in range(DEPTH):
        x = got[z].astype(F32) * scale * gain[:, z * BAND : (z + 1) * BAND]
        out[z // 2, :, (z % 2) * BAND : (z % 2 + 1) * BAND] = x.astype(BF)


def near_kernel(got, gain, out):
    renorm(got, gain, out)


def multiply(at, near, far, pair, side, totals):
    for x in range(4):
        g = jnp.bitwise_xor(at[6], side) * 4 + x
        rows = jnp.concatenate([near[g], far[g]], axis=0)
        for i, w in enumerate(pair):
            totals[2 * i] = totals[2 * i] + nt(rows, w[x, 0:FC, :])
            totals[2 * i + 1] = totals[2 * i + 1] + nt(rows, w[x, FC : 2 * FC, :])


def own_rows_kernel(at, near, full, far, gain, mine, core, out, kept, normed):
    low = at[1] == 0
    lanes = pl.ds(pl.multiple_of(at[1] * 128, 128), 128)
    near_kept, far_kept = full[at[2], :, lanes], far[at[2], :, lanes]
    kept[0:HALF, :] = jnp.where(low, near_kept, far_kept)
    kept[HALF : 2 * HALF, :] = jnp.where(low, far_kept, near_kept)
    renorm(far, gain, normed)
    totals = [jnp.zeros((2 * HALF, FC), F32) for _ in range(4)]
    multiply(at, near, normed, (mine, core), 0, totals)
    for i in range(4):
        out[i] = totals[i]


def partner_rows_kernel(at, near, far, before, mine, core, out):
    totals = [before[i] for i in range(4)]
    multiply(at, near, far, (mine, core), 1, totals)
    low = at[1] == 0
    for i in range(2):
        gate = totals[2 * i]
        units = (gate / (1.0 + jnp.exp(-gate)) * totals[2 * i + 1]).astype(BF)
        first, second = units[0:HALF, :], units[HALF : 2 * HALF, :]
        out[i, 0:HALF, :] = jnp.where(low, first, second)
        out[i, HALF : 2 * HALF, :] = jnp.where(low, second, first)


def down_kernel(at, units, far_units, mine, mine_lo, core, core_lo, out):
    for x in range(4):
        for side, pair in enumerate(((mine, core), (mine_lo, core_lo))):
            total = jnp.zeros((128, BAND), F32)
            for i, w in enumerate(pair):
                total = total + jnp.dot(units[i], w[x, 2 * FC : 3 * FC, 0:BAND], preferred_element_type=F32)
                total = total + jnp.dot(far_units[i], w[x, 2 * FC : 3 * FC, BAND:RUN], preferred_element_type=F32)
            z = (jnp.bitwise_xor(at[6], side) * 4 + x) * 2
            out[z] = total[:, 0:128].astype(BF)
            out[z + 1] = total[:, 128:256].astype(BF)


def finish_kernel(at, got, kept, keep, give):
    total = kept[...].astype(F32)
    for z in range(DEPTH):
        total = total + got[z].astype(F32)
    result = total.T
    head, tail = result[0:QC, :], result[QC : 2 * QC, :]
    keep[...] = jnp.where(at[0] == 0, head, tail).astype(BF)
    give[...] = jnp.where(at[0] == 0, tail, head).astype(BF)


def pack_kernel(query, key, value, out_part, out, token, held, sems):
    token[...] = jnp.zeros_like(token)
    spans = ((query, 0, QC), (key, QC, KC), (value, QC + KC, KC), (out_part, 96, QC))
    reads = [
        pltpu.make_async_copy(ref, held.at[pl.ds(start, rows), :], sems.at[i])
        for i, (ref, start, rows) in enumerate(spans)
    ]
    for copy in reads:
        copy.start()
    for copy in reads:
        copy.wait()
    writes = [pltpu.make_async_copy(held, out.at[g], sems.at[4 + g]) for g in range(GROUPS)]
    for copy in writes:
        copy.start()
    for copy in writes:
        copy.wait()


def norm_kernel(at, after, tables, stream, gain, normed, own, held, gains, sems):
    copies = [
        pltpu.make_async_copy(stream, held, sems.at[0]),
        pltpu.make_async_copy(gain, gains, sems.at[1]),
    ]
    for copy in copies:
        copy.start()
    for copy in copies:
        copy.wait()
    x = held[...].astype(F32)
    scale = lax.rsqrt(jnp.mean(x * x, axis=-1, keepdims=True) + 1e-05)
    for g in range(GROUPS):
        cols = pl.ds(g * RUN, RUN)
        normed[g] = (held[:, cols].astype(F32) * scale * gains[:, cols]).astype(BF)
    rows = pl.ds(pl.multiple_of(at[0] * 128 + at[1] * HALF, HALF), HALF)
    own[...] = held[rows, pl.ds(pl.multiple_of(at[2] * BAND, BAND), BAND)]


def norm(at, after, tables, stream, gain):
    return pl.pallas_call(
        norm_kernel,
        out_shape=(jax.ShapeDtypeStruct((GROUPS, 256, RUN), BF), jax.ShapeDtypeStruct((HALF, BAND), BF)),
        in_specs=[SMEM, ANY, ANY, HBM, HBM],
        out_specs=(VMEM,) * 2,
        scratch_shapes=[pltpu.VMEM((256, D), BF), pltpu.VMEM((1, D), F32), pltpu.SemaphoreType.DMA((2,))],
        compiler_params=params(50),
        name="norm",
    )(at, after, tables, stream, gain)


def join_kernel(at, after, gate, up, narrow, got, out, held, sems):
    copies = [
        pltpu.make_async_copy(narrow, held, sems.at[0]),
        pltpu.make_async_copy(gate, out.at[pl.ds(0, FC), :], sems.at[1]),
        pltpu.make_async_copy(up, out.at[pl.ds(FC, FC), :], sems.at[2]),
    ]
    for copy in copies:
        copy.start()
    low = at[1] == 0
    for k, source in ((1, got), (0, held)):
        if k == 0:
            copies[0].wait()
        for i in range(2):
            even = source[:, 2 * i * 128 : (2 * i + 1) * 128]
            odd = source[:, (2 * i + 1) * 128 : (2 * i + 2) * 128]
            out[2 * FC : 3 * FC, k * BAND + i * 128 : k * BAND + (i + 1) * 128] = jnp.where(low, even, odd)
    copies[1].wait()
    copies[2].wait()


def join(at, after, gate, up, narrow, got):
    return pl.pallas_call(
        join_kernel,
        out_shape=jax.ShapeDtypeStruct((3 * FC, RUN), BF),
        in_specs=[SMEM, ANY, HBM, HBM, HBM, VMEM],
        out_specs=VMEM,
        scratch_shapes=[pltpu.VMEM((FC, RUN), BF), pltpu.SemaphoreType.DMA((3,))],
        compiler_params=params(48),
        name="join",
    )(at, after, gate, up, narrow, got)


def pack(*parts):
    return pl.pallas_call(
        pack_kernel,
        out_shape=(jax.ShapeDtypeStruct((GROUPS, 160, RUN), BF), jax.ShapeDtypeStruct((8, 128), F32)),
        in_specs=[HBM] * 4,
        out_specs=(HBM, VMEM),
        scratch_shapes=[pltpu.VMEM((160, RUN), BF), pltpu.SemaphoreType.DMA((4 + GROUPS,))],
        compiler_params=params(60),
        name="pack",
    )(*parts)


def project(normed, weights, cos, sin):
    return pl.pallas_call(
        project_kernel,
        out_shape=(
            jax.ShapeDtypeStruct((8, HALF, 128), BF),
            jax.ShapeDtypeStruct((KC, 256), BF),
            jax.ShapeDtypeStruct((KC, 256), BF),
        ),
        in_specs=[VMEM] * 4,
        out_specs=(VMEM,) * 3,
        compiler_params=params(24),
        name="project",
    )(normed, weights, cos, sin)


def attend(at, lengths, got):
    return pl.pallas_call(
        attend_kernel,
        out_shape=jax.ShapeDtypeStruct((HALF, BAND), BF),
        in_specs=[SMEM, SMEM, VMEM],
        out_specs=VMEM,
        compiler_params=params(16),
        name="attend",
    )(at, lengths, got)


def output(at, got, weights, own):
    return pl.pallas_call(
        output_kernel,
        out_shape=jax.ShapeDtypeStruct((HALF, BAND), BF),
        in_specs=[SMEM] + [VMEM] * 6,
        out_specs=VMEM,
        compiler_params=params(24),
        name="output",
    )(at, got, *weights, own)


def near_half(got, gain):
    return pl.pallas_call(
        near_kernel,
        out_shape=jax.ShapeDtypeStruct((GROUPS, HALF, RUN), BF),
        in_specs=[VMEM] * 2,
        out_specs=VMEM,
        compiler_params=params(16),
        name="near_half",
    )(got, gain)


def own_rows(at, near, full, far, gain, mine, core):
    return pl.pallas_call(
        own_rows_kernel,
        out_shape=(
            jax.ShapeDtypeStruct((4, 128, FC), F32),
            jax.ShapeDtypeStruct((128, 128), BF),
            jax.ShapeDtypeStruct((GROUPS, HALF, RUN), BF),
        ),
        in_specs=[SMEM] + [VMEM] * 6,
        out_specs=(VMEM,) * 3,
        compiler_params=params(16),
        cost_estimate=cost(2 * HALF * D * 4 * FC, 4 * 2**20),
        name="own_rows",
    )(at, near, full, far, gain, mine, core)


def partner_rows(at, near, far, before, mine, core):
    return pl.pallas_call(
        partner_rows_kernel,
        out_shape=jax.ShapeDtypeStruct((2, 128, FC), BF),
        in_specs=[SMEM] + [VMEM] * 5,
        out_specs=VMEM,
        compiler_params=params(16),
        cost_estimate=cost(2 * HALF * D * 4 * FC, 4 * 2**20),
        name="partner_rows",
    )(at, near, far, before, mine, core)


def down(at, units, far_units, weights):
    return pl.pallas_call(
        down_kernel,
        out_shape=jax.ShapeDtypeStruct((DEPTH, 128, 128), BF),
        in_specs=[SMEM] + [VMEM] * 6,
        out_specs=VMEM,
        compiler_params=params(16),
        cost_estimate=cost(4 * HALF * D * 2 * FC, 5 * 2**20),
        name="down",
    )(at, units, far_units, *weights)


def finish(at, got, kept):
    return pl.pallas_call(
        finish_kernel,
        out_shape=(jax.ShapeDtypeStruct((QC, 128), BF),) * 2,
        in_specs=[SMEM] + [VMEM] * 2,
        out_specs=(VMEM, VMEM),
        compiler_params=params(16),
        name="finish",
    )(at, got, kept)


def swap(x, bits):
    return lax.ppermute(x, "dev", [(d, d ^ bits) for d in range(MEMBERS)])


def swap_groups(x):
    return lax.ppermute(x, "grp", [(g, g ^ 4) for g in range(GROUPS)])


def collect_x(x):
    return lax.all_gather(x, "grp", axis=0, axis_index_groups=[[0, 1, 2, 3], [4, 5, 6, 7]])


def trade(x, groups):
    return lax.all_to_all(x, "dev", 0, 0, axis_index_groups=groups, tiled=True)


def collect(x):
    return lax.all_gather(x, "dev", axis=0, axis_index_groups=COLUMNS)


def after(x, other):
    return lax.optimization_barrier((x, other))[0]


def on_device(
    stream,
    row_length,
    row_start,
    attn_gain,
    w_query,
    w_key,
    w_value,
    w_out,
    ffn_gain,
    w_gate,
    w_up,
    w_down,
):
    member = lax.axis_index("dev")
    core, yhi, z, quad = member % 2, member // 2 % 2, member // 4, member % 4
    ylo = lax.axis_index("grp") // 4
    at = jnp.stack([core, yhi, z, z % 2, z // 2, quad, ylo]).astype(jnp.int32)

    packed, token = pack(w_query.T, w_key.T, w_value.T, w_out.T)
    first = lax.all_to_all(packed, "grp", 0, 0, tiled=True)

    lane = jnp.arange(128, dtype=jnp.int32)
    column = jnp.where(lane < QC, member * QC + lane, member * KC + lane - QC)
    pair = (column % HEAD_DIM // 2).astype(F32)
    freq = jnp.exp(-(2.0 * pair / HEAD_DIM) * math.log(ROPE_BASE))
    positions = (row_start[:, None] + jnp.arange(ROW_LEN, dtype=jnp.int32)[None, :]).reshape(-1)
    angle = positions.astype(F32)[:, None] * freq[None, :]
    cos, sin = jnp.cos(angle), jnp.sin(angle)

    normed, own = norm(at, token, cos, stream, attn_gain.reshape(1, D))
    narrow = after(w_down.T, token)
    other = swap(narrow, 2)

    send, keys, values = project(normed, first, cos, sin)
    got = trade(send, OCTETS)
    mine = join(at, send, w_gate.T, w_up.T, narrow, other)
    mine_lo = swap_groups(after(mine, got))
    out_own = first[:, 96:160, :]
    out_weights = (out_own, swap(out_own, 1), swap(out_own, 2), swap(out_own, 3))
    mixed = collect(attend(at, row_length, got))
    attended = output(at, mixed, out_weights, own)
    mine, mine_lo = collect_x(mine), collect_x(after(mine_lo, attended))
    mine = after(mine, attended)
    core_mine = swap(mine, 1)
    full = collect(attended)
    far = swap(full, 2)
    gain = ffn_gain.reshape(1, D)
    near = near_half(full, gain)
    mine_lo = after(mine_lo, (far, near))
    core_lo = swap(mine_lo, 1)
    totals, kept, far_normed = own_rows(at, near, full, far, gain, mine, core_mine)
    units = partner_rows(at, near, far_normed, totals, mine_lo, core_lo)
    weights = (mine, mine_lo, core_mine, core_lo)
    sums = trade(down(at, units, swap(units, 2), weights), COLUMNS)
    keep, give = finish(at, sums, kept)
    give = swap(give, 1)
    rows = jnp.where(core == 0, jnp.concatenate([keep, give], axis=1), jnp.concatenate([give, keep], axis=1))
    return (keys.T, values.T, rows.T)


def solution(mesh):
    placed = (
        P("grp", None),
        P("grp"),
        P("grp"),
        P(),
        P("grp", "dev"),
        P("grp", "dev"),
        P("grp", "dev"),
        P("grp", "dev"),
        P(),
        P("grp", "dev"),
        P("grp", "dev"),
        P("grp", "dev"),
    )
    return jax.shard_map(
        on_device,
        mesh=mesh,
        in_specs=placed,
        out_specs=(P("grp", "dev"), P("grp", "dev"), P("grp", "dev")),
        check_vma=False,
    )
```

```python
import math

import jax
import jax.numpy as jnp
from jax import lax
from jax.experimental import pallas as pl
from jax.experimental.pallas import tpu as pltpu
from jax.sharding import PartitionSpec as P

HEADS = 32
KV_HEADS = 8
HEAD_DIM = 128
ROW_LEN = 128
D = 4096
ROPE_BASE = 500000.0

GROUPS = 8
MEMBERS = 64
DEPTH = 16
HALF = 64
QC = 64
KC = 16
FC = 224
BAND = 256
RUN = 512

COLUMNS = [[4 * z + q for z in range(DEPTH)] for q in range(4)]
PARITIES = [[4 * (2 * i + p) + q for i in range(8)] for p in range(2) for q in range(4)]
OCTETS = [[8 * z + m for m in range(8)] for z in range(8)]

BF = jnp.bfloat16
F32 = jnp.float32
VMEM = pl.BlockSpec(memory_space=pltpu.VMEM)
HBM = pl.BlockSpec(memory_space=pltpu.HBM)
ANY = pl.BlockSpec(memory_space=pl.ANY)
SMEM = pl.BlockSpec(memory_space=pltpu.SMEM)


def nt(a, b):
    return lax.dot_general(a, b, (((1,), (1,)), ((), ())), preferred_element_type=F32)


def whole(*shape):
    return pl.BlockSpec(shape, lambda i: (0,) * len(shape))


def params(mib):
    return pltpu.CompilerParams(vmem_limit_bytes=mib * 2**20)


def cost(flops, nbytes):
    return pl.CostEstimate(flops=flops, bytes_accessed=nbytes, transcendentals=0)


def project_kernel(normed, weights, cos, sin, send, keys, values):
    total = jnp.zeros((256, 96), F32)
    for g in range(GROUPS):
        total = total + nt(normed[g], weights[g, 0:96, :])
    total = jnp.concatenate([total, jnp.zeros((256, 32), F32)], axis=1)
    lane = lax.broadcasted_iota(jnp.int32, (256, 128), 1)
    partner = jnp.where(lane % 2 == 0, -pltpu.roll(total, 127, 1), pltpu.roll(total, 1, 1))
    turned = jnp.where(lane < QC + KC, total * cos[...] + partner * sin[...], total)
    turned = turned.astype(BF).astype(F32)
    flipped = turned.T
    keys[...] = flipped[QC : QC + KC, :].astype(BF)
    values[...] = flipped[QC + KC : QC + 2 * KC, :].astype(BF)
    lane = lax.broadcasted_iota(jnp.int32, (HALF, 128), 1)
    for zl in range(2):
        for yhi in range(2):
            for c in range(2):
                first = turned[c * 128 : c * 128 + HALF, :]
                second = turned[c * 128 + HALF : c * 128 + 128, :]
                mine = second if yhi else first
                chunk = jnp.where(lane < QC, mine, jnp.where(lane < 96, first, pltpu.roll(second, 32, 1)))
                send[zl * 4 + yhi * 2 + c] = chunk.astype(BF)


def attend_kernel(at, lengths, got, out):
    lane = lax.broadcasted_iota(jnp.int32, (HALF, 128), 1)
    pieces = [got[m].astype(F32) for m in range(8)]

    def gather(start):
        full = jnp.zeros((HALF, 128), F32)
        for m in range(8):
            full = jnp.where(lane // KC == m, pltpu.roll(pieces[m], (KC * m - start) % 128, 1), full)
        return full.astype(BF)

    keys = jnp.concatenate([gather(QC), gather(96)], axis=0)
    values = jnp.concatenate([gather(QC + KC), gather(96 + KC)], axis=0)
    slot = lax.broadcasted_iota(jnp.int32, (HALF, 128), 0) + at[1] * HALF
    allowed = (lane <= slot) & (lane < lengths[at[0]])
    for a in range(2):
        low = got[at[3] * 4 + a * 2].astype(F32)
        high = got[at[3] * 4 + a * 2 + 1].astype(F32)
        queries = jnp.where(lane < QC, low, pltpu.roll(high, QC, 1)).astype(BF)
        scores = nt(queries, keys) / math.sqrt(HEAD_DIM)
        scores = jnp.where(allowed, scores, -jnp.inf)
        expo = jnp.exp(scores - jnp.max(scores, axis=-1, keepdims=True))
        probs = (expo / jnp.sum(expo, axis=-1, keepdims=True)).astype(BF)
        mixed = jnp.dot(probs, values, preferred_element_type=F32).astype(BF)
        out[:, a * 128 : a * 128 + 128] = mixed


def output_kernel(at, got, mine, core, far, cross, own, out):
    parts = []
    for w in (mine, core, far, cross):
        total = jnp.zeros((HALF, QC), F32)
        for g in range(GROUPS):
            total = total + nt(got[2 * g], w[g, :, 0:BAND]) + nt(got[2 * g + 1], w[g, :, BAND:RUN])
        parts.append(total)
    blocks = []
    for j in range(4):
        picked = parts[0]
        for k in range(1, 4):
            picked = jnp.where(jnp.bitwise_xor(at[5], j) == k, parts[k], picked)
        blocks.append(picked)
    projected = jnp.concatenate(blocks, axis=1)
    attended = (own[...].astype(F32) + projected).astype(BF)
    for i in range(8):
        out[i] = attended


def renorm(at, same, other, gain, out):
    low = at[3] == 0
    squares = jnp.zeros((HALF, 1), F32)
    for got in (same, other):
        for i in range(8):
            x = got[i].astype(F32)
            squares = squares + jnp.sum(x * x, axis=-1, keepdims=True)
    scale = lax.rsqrt(squares * (1.0 / D) + 1e-05)
    for i in range(8):
        one, two = same[i].astype(F32), other[i].astype(F32)
        for k, x in enumerate((jnp.where(low, one, two), jnp.where(low, two, one))):
            z = 2 * i + k
            out[i, :, k * BAND : (k + 1) * BAND] = (x * scale * gain[:, z * BAND : (z + 1) * BAND]).astype(BF)


def near_kernel(at, same, other, gain, out):
    renorm(at, same, other, gain, out)


def multiply(at, near, far, pair, side, totals):
    for x in range(4):
        g = jnp.bitwise_xor(at[6], side) * 4 + x
        rows = jnp.concatenate([near[g], far[g]], axis=0)
        for i, w in enumerate(pair):
            totals[2 * i] = totals[2 * i] + nt(rows, w[x, 0:FC, :])
            totals[2 * i + 1] = totals[2 * i + 1] + nt(rows, w[x, FC : 2 * FC, :])


def own_rows_kernel(at, near, same, far_same, far_other, gain, mine, core, out, kept, normed):
    low = at[1] == 0
    lanes = pl.ds(pl.multiple_of(at[1] * 128, 128), 128)
    near_kept, far_kept = same[at[4], :, lanes], far_same[at[4], :, lanes]
    kept[0:HALF, :] = jnp.where(low, near_kept, far_kept)
    kept[HALF : 2 * HALF, :] = jnp.where(low, far_kept, near_kept)
    renorm(at, far_same, far_other, gain, normed)
    totals = [jnp.zeros((2 * HALF, FC), F32) for _ in range(4)]
    multiply(at, near, normed, (mine, core), 0, totals)
    for i in range(4):
        out[i] = totals[i]


def partner_rows_kernel(at, near, far, before, mine, core, out):
    totals = [before[i] for i in range(4)]
    multiply(at, near, far, (mine, core), 1, totals)
    low = at[1] == 0
    for i in range(2):
        gate = totals[2 * i]
        units = (gate / (1.0 + jnp.exp(-gate)) * totals[2 * i + 1]).astype(BF)
        first, second = units[0:HALF, :], units[HALF : 2 * HALF, :]
        out[i, 0:HALF, :] = jnp.where(low, first, second)
        out[i, HALF : 2 * HALF, :] = jnp.where(low, second, first)


def down_kernel(at, units, far_units, mine, mine_lo, core, core_lo, keep, give):
    low = at[3] == 0
    for x in range(4):
        for side, pair in enumerate(((mine, core), (mine_lo, core_lo))):
            total = jnp.zeros((128, BAND), F32)
            for i, w in enumerate(pair):
                total = total + jnp.dot(units[i], w[x, 2 * FC : 3 * FC, 0:BAND], preferred_element_type=F32)
                total = total + jnp.dot(far_units[i], w[x, 2 * FC : 3 * FC, BAND:RUN], preferred_element_type=F32)
            g = jnp.bitwise_xor(at[6], side) * 4 + x
            even, odd = total[:, 0:128], total[:, 128:256]
            keep[g] = jnp.where(low, even, odd)
            give[g] = jnp.where(low, odd, even).astype(BF)


def add_kernel(keep, got, out):
    for i in range(8):
        out[i] = (keep[i] + got[i].astype(F32)).astype(BF)


def finish_kernel(at, got, kept, keep, give):
    total = kept[...].astype(F32)
    for i in range(8):
        total = total + got[i].astype(F32)
    result = total.T
    head, tail = result[0:QC, :], result[QC : 2 * QC, :]
    keep[...] = jnp.where(at[0] == 0, head, tail).astype(BF)
    give[...] = jnp.where(at[0] == 0, tail, head).astype(BF)


def pack_kernel(query, key, value, out_part, out, token, held, sems):
    token[...] = jnp.zeros_like(token)
    spans = ((query, 0, QC), (key, QC, KC), (value, QC + KC, KC), (out_part, 96, QC))
    reads = [
        pltpu.make_async_copy(ref, held.at[pl.ds(start, rows), :], sems.at[i])
        for i, (ref, start, rows) in enumerate(spans)
    ]
    for copy in reads:
        copy.start()
    for copy in reads:
        copy.wait()
    writes = [pltpu.make_async_copy(held, out.at[g], sems.at[4 + g]) for g in range(GROUPS)]
    for copy in writes:
        copy.start()
    for copy in writes:
        copy.wait()


def norm_kernel(at, after, tables, stream, gain, normed, own, held, gains, sems):
    copies = [
        pltpu.make_async_copy(stream, held, sems.at[0]),
        pltpu.make_async_copy(gain, gains, sems.at[1]),
    ]
    for copy in copies:
        copy.start()
    for copy in copies:
        copy.wait()
    x = held[...].astype(F32)
    scale = lax.rsqrt(jnp.mean(x * x, axis=-1, keepdims=True) + 1e-05)
    for g in range(GROUPS):
        cols = pl.ds(g * RUN, RUN)
        normed[g] = (held[:, cols].astype(F32) * scale * gains[:, cols]).astype(BF)
    rows = pl.ds(pl.multiple_of(at[0] * 128 + at[1] * HALF, HALF), HALF)
    own[...] = held[rows, pl.ds(pl.multiple_of(at[2] * BAND, BAND), BAND)]


def norm(at, after, tables, stream, gain):
    return pl.pallas_call(
        norm_kernel,
        out_shape=(jax.ShapeDtypeStruct((GROUPS, 256, RUN), BF), jax.ShapeDtypeStruct((HALF, BAND), BF)),
        in_specs=[SMEM, ANY, ANY, HBM, HBM],
        out_specs=(VMEM,) * 2,
        scratch_shapes=[pltpu.VMEM((256, D), BF), pltpu.VMEM((1, D), F32), pltpu.SemaphoreType.DMA((2,))],
        compiler_params=params(50),
        name="norm",
    )(at, after, tables, stream, gain)


def join_kernel(at, after, gate, up, narrow, got, out, held, sems):
    copies = [
        pltpu.make_async_copy(narrow, held, sems.at[0]),
        pltpu.make_async_copy(gate, out.at[pl.ds(0, FC), :], sems.at[1]),
        pltpu.make_async_copy(up, out.at[pl.ds(FC, FC), :], sems.at[2]),
    ]
    for copy in copies:
        copy.start()
    low = at[1] == 0
    for k, source in ((1, got), (0, held)):
        if k == 0:
            copies[0].wait()
        for i in range(2):
            even = source[:, 2 * i * 128 : (2 * i + 1) * 128]
            odd = source[:, (2 * i + 1) * 128 : (2 * i + 2) * 128]
            out[2 * FC : 3 * FC, k * BAND + i * 128 : k * BAND + (i + 1) * 128] = jnp.where(low, even, odd)
    copies[1].wait()
    copies[2].wait()


def join(at, after, gate, up, narrow, got):
    return pl.pallas_call(
        join_kernel,
        out_shape=jax.ShapeDtypeStruct((3 * FC, RUN), BF),
        in_specs=[SMEM, ANY, HBM, HBM, HBM, VMEM],
        out_specs=VMEM,
        scratch_shapes=[pltpu.VMEM((FC, RUN), BF), pltpu.SemaphoreType.DMA((3,))],
        compiler_params=params(48),
        name="join",
    )(at, after, gate, up, narrow, got)


def pack(*parts):
    return pl.pallas_call(
        pack_kernel,
        out_shape=(jax.ShapeDtypeStruct((GROUPS, 160, RUN), BF), jax.ShapeDtypeStruct((8, 128), F32)),
        in_specs=[HBM] * 4,
        out_specs=(HBM, VMEM),
        scratch_shapes=[pltpu.VMEM((160, RUN), BF), pltpu.SemaphoreType.DMA((4 + GROUPS,))],
        compiler_params=params(60),
        name="pack",
    )(*parts)


def project(normed, weights, cos, sin):
    return pl.pallas_call(
        project_kernel,
        out_shape=(
            jax.ShapeDtypeStruct((8, HALF, 128), BF),
            jax.ShapeDtypeStruct((KC, 256), BF),
            jax.ShapeDtypeStruct((KC, 256), BF),
        ),
        in_specs=[VMEM] * 4,
        out_specs=(VMEM,) * 3,
        compiler_params=params(24),
        name="project",
    )(normed, weights, cos, sin)


def attend(at, lengths, got):
    return pl.pallas_call(
        attend_kernel,
        out_shape=jax.ShapeDtypeStruct((HALF, BAND), BF),
        in_specs=[SMEM, SMEM, VMEM],
        out_specs=VMEM,
        compiler_params=params(16),
        name="attend",
    )(at, lengths, got)


def output(at, got, weights, own):
    return pl.pallas_call(
        output_kernel,
        out_shape=jax.ShapeDtypeStruct((8, HALF, BAND), BF),
        in_specs=[SMEM] + [VMEM] * 6,
        out_specs=VMEM,
        compiler_params=params(24),
        name="output",
    )(at, got, *weights, own)


def near_half(at, same, other, gain):
    return pl.pallas_call(
        near_kernel,
        out_shape=jax.ShapeDtypeStruct((GROUPS, HALF, RUN), BF),
        in_specs=[SMEM] + [VMEM] * 3,
        out_specs=VMEM,
        compiler_params=params(16),
        name="near_half",
    )(at, same, other, gain)


def own_rows(at, near, same, far_same, far_other, gain, mine, core):
    return pl.pallas_call(
        own_rows_kernel,
        out_shape=(
            jax.ShapeDtypeStruct((4, 128, FC), F32),
            jax.ShapeDtypeStruct((128, 128), BF),
            jax.ShapeDtypeStruct((GROUPS, HALF, RUN), BF),
        ),
        in_specs=[SMEM] + [VMEM] * 7,
        out_specs=(VMEM,) * 3,
        compiler_params=params(16),
        cost_estimate=cost(2 * HALF * D * 4 * FC, 4 * 2**20),
        name="own_rows",
    )(at, near, same, far_same, far_other, gain, mine, core)


def partner_rows(at, near, far, before, mine, core):
    return pl.pallas_call(
        partner_rows_kernel,
        out_shape=jax.ShapeDtypeStruct((2, 128, FC), BF),
        in_specs=[SMEM] + [VMEM] * 5,
        out_specs=VMEM,
        compiler_params=params(16),
        cost_estimate=cost(2 * HALF * D * 4 * FC, 4 * 2**20),
        name="partner_rows",
    )(at, near, far, before, mine, core)


def down(at, units, far_units, weights):
    return pl.pallas_call(
        down_kernel,
        out_shape=(jax.ShapeDtypeStruct((8, 128, 128), F32), jax.ShapeDtypeStruct((8, 128, 128), BF)),
        in_specs=[SMEM] + [VMEM] * 6,
        out_specs=(VMEM, VMEM),
        compiler_params=params(16),
        cost_estimate=cost(4 * HALF * D * 2 * FC, 5 * 2**20),
        name="down",
    )(at, units, far_units, *weights)


def add(keep, got):
    return pl.pallas_call(
        add_kernel,
        out_shape=jax.ShapeDtypeStruct((8, 128, 128), BF),
        in_specs=[VMEM] * 2,
        out_specs=VMEM,
        compiler_params=params(16),
        name="add",
    )(keep, got)


def finish(at, got, kept):
    return pl.pallas_call(
        finish_kernel,
        out_shape=(jax.ShapeDtypeStruct((QC, 128), BF),) * 2,
        in_specs=[SMEM] + [VMEM] * 2,
        out_specs=(VMEM, VMEM),
        compiler_params=params(16),
        name="finish",
    )(at, got, kept)


def swap(x, bits):
    return lax.ppermute(x, "dev", [(d, d ^ bits) for d in range(MEMBERS)])


def swap_groups(x):
    return lax.ppermute(x, "grp", [(g, g ^ 4) for g in range(GROUPS)])


def collect_x(x):
    return lax.all_gather(x, "grp", axis=0, axis_index_groups=[[0, 1, 2, 3], [4, 5, 6, 7]])


def trade(x, groups):
    return lax.all_to_all(x, "dev", 0, 0, axis_index_groups=groups, tiled=True)


def collect(x):
    return lax.all_gather(x, "dev", axis=0, axis_index_groups=COLUMNS)


def after(x, other):
    return lax.optimization_barrier((x, other))[0]


def on_device(
    stream,
    row_length,
    row_start,
    attn_gain,
    w_query,
    w_key,
    w_value,
    w_out,
    ffn_gain,
    w_gate,
    w_up,
    w_down,
):
    member = lax.axis_index("dev")
    core, yhi, z, quad = member % 2, member // 2 % 2, member // 4, member % 4
    ylo = lax.axis_index("grp") // 4
    at = jnp.stack([core, yhi, z, z % 2, z // 2, quad, ylo]).astype(jnp.int32)

    packed, token = pack(w_query.T, w_key.T, w_value.T, w_out.T)
    first = lax.all_to_all(packed, "grp", 0, 0, tiled=True)

    lane = jnp.arange(128, dtype=jnp.int32)
    column = jnp.where(lane < QC, member * QC + lane, member * KC + lane - QC)
    pair = (column % HEAD_DIM // 2).astype(F32)
    freq = jnp.exp(-(2.0 * pair / HEAD_DIM) * math.log(ROPE_BASE))
    positions = (row_start[:, None] + jnp.arange(ROW_LEN, dtype=jnp.int32)[None, :]).reshape(-1)
    angle = positions.astype(F32)[:, None] * freq[None, :]
    cos, sin = jnp.cos(angle), jnp.sin(angle)

    normed, own = norm(at, token, cos, stream, attn_gain.reshape(1, D))
    narrow = after(w_down.T, token)
    other = swap(narrow, 2)

    send, keys, values = project(normed, first, cos, sin)
    got = trade(send, OCTETS)
    mine = join(at, send, w_gate.T, w_up.T, narrow, other)
    mine_lo = swap_groups(after(mine, got))
    out_own = first[:, 96:160, :]
    out_weights = (out_own, swap(out_own, 1), swap(out_own, 2), swap(out_own, 3))
    mixed = collect(attend(at, row_length, got))
    attended = output(at, mixed, out_weights, own)
    mine, mine_lo = collect_x(mine), collect_x(after(mine_lo, attended))
    mine = after(mine, attended)
    core_mine = swap(mine, 1)
    same = trade(attended, PARITIES)
    other, far_same, far_other = swap(same, 4), swap(same, 2), swap(same, 6)
    gain = ffn_gain.reshape(1, D)
    near = near_half(at, same, other, gain)
    mine_lo = after(mine_lo, (far_same, far_other, near))
    core_lo = swap(mine_lo, 1)
    totals, kept, far_normed = own_rows(at, near, same, far_same, far_other, gain, mine, core_mine)
    units = partner_rows(at, near, far_normed, totals, mine_lo, core_lo)
    weights = (mine, mine_lo, core_mine, core_lo)
    keep, give = down(at, units, swap(units, 2), weights)
    sums = trade(add(keep, swap(give, 4)), PARITIES)
    keep, give = finish(at, sums, kept)
    give = swap(give, 1)
    rows = jnp.where(core == 0, jnp.concatenate([keep, give], axis=1), jnp.concatenate([give, keep], axis=1))
    return (keys.T, values.T, rows.T)


def solution(mesh):
    placed = (
        P("grp", None),
        P("grp"),
        P("grp"),
        P(),
        P("grp", "dev"),
        P("grp", "dev"),
        P("grp", "dev"),
        P("grp", "dev"),
        P(),
        P("grp", "dev"),
        P("grp", "dev"),
        P("grp", "dev"),
    )
    return jax.shard_map(
        on_device,
        mesh=mesh,
        in_specs=placed,
        out_specs=(P("grp", "dev"), P("grp", "dev"), P("grp", "dev")),
        check_vma=False,
    )
```

```python
import math

import jax
import jax.numpy as jnp
from jax import lax
from jax.experimental import pallas as pl
from jax.experimental.pallas import tpu as pltpu
from jax.sharding import PartitionSpec as P

HEADS = 32
KV_HEADS = 8
HEAD_DIM = 128
ROW_LEN = 128
D = 4096
ROPE_BASE = 500000.0

GROUPS = 8
MEMBERS = 64
DEPTH = 16
HALF = 64
QC = 64
KC = 16
FC = 224
BAND = 256
RUN = 512

COLUMNS = [[4 * z + q for z in range(DEPTH)] for q in range(4)]
PARITIES = [[4 * (2 * i + p) + q for i in range(8)] for p in range(2) for q in range(4)]
OCTETS = [[8 * z + m for m in range(8)] for z in range(8)]

BF = jnp.bfloat16
F32 = jnp.float32
VMEM = pl.BlockSpec(memory_space=pltpu.VMEM)
HBM = pl.BlockSpec(memory_space=pltpu.HBM)
ANY = pl.BlockSpec(memory_space=pl.ANY)
SMEM = pl.BlockSpec(memory_space=pltpu.SMEM)


def place():
    d = lax.axis_index("dev")
    return (d % 2, d // 2 % 2, d // 4, d // 4 % 2, d // 8, d % 4, lax.axis_index("grp") // 4)


def nt(a, b):
    return lax.dot_general(a, b, (((1,), (1,)), ((), ())), preferred_element_type=F32)


def whole(*shape):
    return pl.BlockSpec(shape, lambda i: (0,) * len(shape))


def params(mib):
    return pltpu.CompilerParams(vmem_limit_bytes=mib * 2**20)


def cost(flops, nbytes):
    return pl.CostEstimate(flops=flops, bytes_accessed=nbytes, transcendentals=0)


def project_kernel(normed, weights, cos, sin, send, keys, values, tables, sems):
    copies = [pltpu.make_async_copy(ref, tables.at[i], sems.at[i]) for i, ref in enumerate((cos, sin))]
    for copy in copies:
        copy.start()
    total = jnp.zeros((256, 96), F32)
    for g in range(GROUPS):
        total = total + nt(normed[g], weights[g, 0:96, :])
    total = jnp.concatenate([total, jnp.zeros((256, 32), F32)], axis=1)
    lane = lax.broadcasted_iota(jnp.int32, (256, 128), 1)
    partner = jnp.where(lane % 2 == 0, -pltpu.roll(total, 127, 1), pltpu.roll(total, 1, 1))
    for copy in copies:
        copy.wait()
    turned = jnp.where(lane < QC + KC, total * tables[0] + partner * tables[1], total)
    turned = turned.astype(BF).astype(F32)
    flipped = turned.T
    keys[...] = flipped[QC : QC + KC, :].astype(BF)
    values[...] = flipped[QC + KC : QC + 2 * KC, :].astype(BF)
    lane = lax.broadcasted_iota(jnp.int32, (HALF, 128), 1)
    for zl in range(2):
        for yhi in range(2):
            for c in range(2):
                first = turned[c * 128 : c * 128 + HALF, :]
                second = turned[c * 128 + HALF : c * 128 + 128, :]
                mine = second if yhi else first
                chunk = jnp.where(lane < QC, mine, jnp.where(lane < 96, first, pltpu.roll(second, 32, 1)))
                send[zl * 4 + yhi * 2 + c] = chunk.astype(BF)


def attend_kernel(lengths, got, out):
    at = place()
    lane = lax.broadcasted_iota(jnp.int32, (HALF, 128), 1)
    pieces = [got[m].astype(F32) for m in range(8)]

    def gather(start):
        full = jnp.zeros((HALF, 128), F32)
        for m in range(8):
            full = jnp.where(lane // KC == m, pltpu.roll(pieces[m], (KC * m - start) % 128, 1), full)
        return full.astype(BF)

    keys = jnp.concatenate([gather(QC), gather(96)], axis=0)
    values = jnp.concatenate([gather(QC + KC), gather(96 + KC)], axis=0)
    slot = lax.broadcasted_iota(jnp.int32, (HALF, 128), 0) + at[1] * HALF
    allowed = (lane <= slot) & (lane < lengths[at[0]])
    for a in range(2):
        low = got[at[3] * 4 + a * 2].astype(F32)
        high = got[at[3] * 4 + a * 2 + 1].astype(F32)
        queries = jnp.where(lane < QC, low, pltpu.roll(high, QC, 1)).astype(BF)
        scores = nt(queries, keys) / math.sqrt(HEAD_DIM)
        scores = jnp.where(allowed, scores, -jnp.inf)
        expo = jnp.exp(scores - jnp.max(scores, axis=-1, keepdims=True))
        probs = (expo / jnp.sum(expo, axis=-1, keepdims=True)).astype(BF)
        mixed = jnp.dot(probs, values, preferred_element_type=F32).astype(BF)
        out[:, a * 128 : a * 128 + 128] = mixed


def output_kernel(got, mine, core, far, cross, own, out):
    at = place()
    parts = []
    for w in (mine, core, far, cross):
        total = jnp.zeros((HALF, QC), F32)
        for g in range(GROUPS):
            total = total + nt(got[2 * g], w[g, :, 0:BAND]) + nt(got[2 * g + 1], w[g, :, BAND:RUN])
        parts.append(total)
    blocks = []
    for j in range(4):
        picked = parts[0]
        for k in range(1, 4):
            picked = jnp.where(jnp.bitwise_xor(at[5], j) == k, parts[k], picked)
        blocks.append(picked)
    projected = jnp.concatenate(blocks, axis=1)
    attended = (own[...].astype(F32) + projected).astype(BF)
    for i in range(8):
        out[i] = attended


def renorm(at, same, other, gain, out):
    low = at[3] == 0
    squares = jnp.zeros((HALF, 1), F32)
    for got in (same, other):
        for i in range(8):
            x = got[i].astype(F32)
            squares = squares + jnp.sum(x * x, axis=-1, keepdims=True)
    scale = lax.rsqrt(squares * (1.0 / D) + 1e-05)
    for i in range(8):
        one, two = same[i].astype(F32), other[i].astype(F32)
        for k, x in enumerate((jnp.where(low, one, two), jnp.where(low, two, one))):
            z = 2 * i + k
            out[i, :, k * BAND : (k + 1) * BAND] = (x * scale * gain[:, z * BAND : (z + 1) * BAND]).astype(BF)


def near_kernel(same, other, gain, out):
    at = place()
    renorm(at, same, other, gain, out)


def multiply(at, near, far, pair, side, totals):
    for x in range(4):
        g = jnp.bitwise_xor(at[6], side) * 4 + x
        rows = jnp.concatenate([near[g], far[g]], axis=0)
        for i, w in enumerate(pair):
            totals[2 * i] = totals[2 * i] + nt(rows, w[x, 0:FC, :])
            totals[2 * i + 1] = totals[2 * i + 1] + nt(rows, w[x, FC : 2 * FC, :])


def own_rows_kernel(near, same, far_same, far_other, gain, mine, core, out, kept, normed):
    at = place()
    low = at[1] == 0
    lanes = pl.ds(pl.multiple_of(at[1] * 128, 128), 128)
    near_kept, far_kept = same[at[4], :, lanes], far_same[at[4], :, lanes]
    kept[0:HALF, :] = jnp.where(low, near_kept, far_kept)
    kept[HALF : 2 * HALF, :] = jnp.where(low, far_kept, near_kept)
    renorm(at, far_same, far_other, gain, normed)
    totals = [jnp.zeros((2 * HALF, FC), F32) for _ in range(4)]
    multiply(at, near, normed, (mine, core), 0, totals)
    for i in range(4):
        out[i] = totals[i]


def partner_rows_kernel(near, far, before, mine, core, out):
    at = place()
    totals = [before[i] for i in range(4)]
    multiply(at, near, far, (mine, core), 1, totals)
    low = at[1] == 0
    for i in range(2):
        gate = totals[2 * i]
        units = (gate / (1.0 + jnp.exp(-gate)) * totals[2 * i + 1]).astype(BF)
        first, second = units[0:HALF, :], units[HALF : 2 * HALF, :]
        out[i, 0:HALF, :] = jnp.where(low, first, second)
        out[i, HALF : 2 * HALF, :] = jnp.where(low, second, first)


def down_kernel(units, far_units, mine, mine_lo, core, core_lo, keep, give):
    at = place()
    low = at[3] == 0
    for x in range(4):
        for side, pair in enumerate(((mine, core), (mine_lo, core_lo))):
            total = jnp.zeros((128, BAND), F32)
            for i, w in enumerate(pair):
                total = total + jnp.dot(units[i], w[x, 2 * FC : 3 * FC, 0:BAND], preferred_element_type=F32)
                total = total + jnp.dot(far_units[i], w[x, 2 * FC : 3 * FC, BAND:RUN], preferred_element_type=F32)
            g = jnp.bitwise_xor(at[6], side) * 4 + x
            even, odd = total[:, 0:128], total[:, 128:256]
            keep[g] = jnp.where(low, even, odd)
            give[g] = jnp.where(low, odd, even).astype(BF)


def add_kernel(keep, got, out):
    for i in range(8):
        out[i] = (keep[i] + got[i].astype(F32)).astype(BF)


def finish_kernel(got, kept, keep, give):
    at = place()
    total = kept[...].astype(F32)
    for i in range(8):
        total = total + got[i].astype(F32)
    result = total.T
    head, tail = result[0:QC, :], result[QC : 2 * QC, :]
    keep[...] = jnp.where(at[0] == 0, head, tail).astype(BF)
    give[...] = jnp.where(at[0] == 0, tail, head).astype(BF)


def pack_kernel(query, key, value, out_part, out, token, held, sems):
    token[...] = jnp.zeros_like(token)
    spans = ((query, 0, QC), (key, QC, KC), (value, QC + KC, KC), (out_part, 96, QC))
    reads = [
        pltpu.make_async_copy(ref, held.at[pl.ds(start, rows), :], sems.at[i])
        for i, (ref, start, rows) in enumerate(spans)
    ]
    for copy in reads:
        copy.start()
    for copy in reads:
        copy.wait()
    writes = [pltpu.make_async_copy(held, out.at[g], sems.at[4 + g]) for g in range(GROUPS)]
    for copy in writes:
        copy.start()
    for copy in writes:
        copy.wait()


def norm_kernel(after, tables, stream, gain, normed, own, held, gains, sems):
    at = place()
    copies = [
        pltpu.make_async_copy(stream, held, sems.at[0]),
        pltpu.make_async_copy(gain, gains, sems.at[1]),
    ]
    for copy in copies:
        copy.start()
    for copy in copies:
        copy.wait()
    x = held[...].astype(F32)
    scale = lax.rsqrt(jnp.mean(x * x, axis=-1, keepdims=True) + 1e-05)
    for g in range(GROUPS):
        cols = pl.ds(g * RUN, RUN)
        normed[g] = (held[:, cols].astype(F32) * scale * gains[:, cols]).astype(BF)
    rows = pl.ds(pl.multiple_of(at[0] * 128 + at[1] * HALF, HALF), HALF)
    own[...] = held[rows, pl.ds(pl.multiple_of(at[2] * BAND, BAND), BAND)]


def norm(after, tables, stream, gain):
    return pl.pallas_call(
        norm_kernel,
        out_shape=(jax.ShapeDtypeStruct((GROUPS, 256, RUN), BF), jax.ShapeDtypeStruct((HALF, BAND), BF)),
        in_specs=[ANY, ANY, HBM, HBM],
        out_specs=(VMEM,) * 2,
        scratch_shapes=[pltpu.VMEM((256, D), BF), pltpu.VMEM((1, D), F32), pltpu.SemaphoreType.DMA((2,))],
        compiler_params=params(44),
        name="norm",
    )(after, tables, stream, gain)


def join_kernel(after, gate, up, narrow, got, out, held, sems):
    at = place()
    copies = [
        pltpu.make_async_copy(narrow, held, sems.at[0]),
        pltpu.make_async_copy(gate, out.at[pl.ds(0, FC), :], sems.at[1]),
        pltpu.make_async_copy(up, out.at[pl.ds(FC, FC), :], sems.at[2]),
    ]
    for copy in copies:
        copy.start()
    low = at[1] == 0
    for k, source in ((1, got), (0, held)):
        if k == 0:
            copies[0].wait()
        for i in range(2):
            even = source[:, 2 * i * 128 : (2 * i + 1) * 128]
            odd = source[:, (2 * i + 1) * 128 : (2 * i + 2) * 128]
            out[2 * FC : 3 * FC, k * BAND + i * 128 : k * BAND + (i + 1) * 128] = jnp.where(low, even, odd)
    copies[1].wait()
    copies[2].wait()


def join(after, gate, up, narrow, got):
    return pl.pallas_call(
        join_kernel,
        out_shape=jax.ShapeDtypeStruct((3 * FC, RUN), BF),
        in_specs=[ANY, HBM, HBM, HBM, VMEM],
        out_specs=VMEM,
        scratch_shapes=[pltpu.VMEM((FC, RUN), BF), pltpu.SemaphoreType.DMA((3,))],
        compiler_params=params(48),
        name="join",
    )(after, gate, up, narrow, got)


def pack(*parts):
    return pl.pallas_call(
        pack_kernel,
        out_shape=(jax.ShapeDtypeStruct((GROUPS, 160, RUN), BF), jax.ShapeDtypeStruct((8, 128), F32)),
        in_specs=[HBM] * 4,
        out_specs=(HBM, VMEM),
        scratch_shapes=[pltpu.VMEM((160, RUN), BF), pltpu.SemaphoreType.DMA((4 + GROUPS,))],
        compiler_params=params(60),
        name="pack",
    )(*parts)


def project(normed, weights, cos, sin):
    return pl.pallas_call(
        project_kernel,
        out_shape=(
            jax.ShapeDtypeStruct((8, HALF, 128), BF),
            jax.ShapeDtypeStruct((KC, 256), BF),
            jax.ShapeDtypeStruct((KC, 256), BF),
        ),
        in_specs=[VMEM] * 2 + [HBM] * 2,
        out_specs=(VMEM,) * 3,
        scratch_shapes=[pltpu.VMEM((2, 256, 128), F32), pltpu.SemaphoreType.DMA((2,))],
        compiler_params=params(24),
        name="project",
    )(normed, weights, cos, sin)


def attend(lengths, got):
    return pl.pallas_call(
        attend_kernel,
        out_shape=jax.ShapeDtypeStruct((HALF, BAND), BF),
        in_specs=[SMEM, VMEM],
        out_specs=VMEM,
        compiler_params=params(16),
        name="attend",
    )(lengths, got)


def output(got, weights, own):
    return pl.pallas_call(
        output_kernel,
        out_shape=jax.ShapeDtypeStruct((8, HALF, BAND), BF),
        in_specs=[VMEM] * 6,
        out_specs=VMEM,
        compiler_params=params(24),
        name="output",
    )(got, *weights, own)


def near_half(same, other, gain):
    return pl.pallas_call(
        near_kernel,
        out_shape=jax.ShapeDtypeStruct((GROUPS, HALF, RUN), BF),
        in_specs=[VMEM] * 3,
        out_specs=VMEM,
        compiler_params=params(16),
        name="near_half",
    )(same, other, gain)


def own_rows(near, same, far_same, far_other, gain, mine, core):
    return pl.pallas_call(
        own_rows_kernel,
        out_shape=(
            jax.ShapeDtypeStruct((4, 128, FC), F32),
            jax.ShapeDtypeStruct((128, 128), BF),
            jax.ShapeDtypeStruct((GROUPS, HALF, RUN), BF),
        ),
        in_specs=[VMEM] * 7,
        out_specs=(VMEM,) * 3,
        compiler_params=params(16),
        cost_estimate=cost(2 * HALF * D * 4 * FC, 4 * 2**20),
        name="own_rows",
    )(near, same, far_same, far_other, gain, mine, core)


def partner_rows(near, far, before, mine, core):
    return pl.pallas_call(
        partner_rows_kernel,
        out_shape=jax.ShapeDtypeStruct((2, 128, FC), BF),
        in_specs=[VMEM] * 5,
        out_specs=VMEM,
        compiler_params=params(16),
        cost_estimate=cost(2 * HALF * D * 4 * FC, 4 * 2**20),
        name="partner_rows",
    )(near, far, before, mine, core)


def down(units, far_units, weights):
    return pl.pallas_call(
        down_kernel,
        out_shape=(jax.ShapeDtypeStruct((8, 128, 128), F32), jax.ShapeDtypeStruct((8, 128, 128), BF)),
        in_specs=[VMEM] * 6,
        out_specs=(VMEM, VMEM),
        compiler_params=params(16),
        cost_estimate=cost(4 * HALF * D * 2 * FC, 5 * 2**20),
        name="down",
    )(units, far_units, *weights)


def add(keep, got):
    return pl.pallas_call(
        add_kernel,
        out_shape=jax.ShapeDtypeStruct((8, 128, 128), BF),
        in_specs=[VMEM] * 2,
        out_specs=VMEM,
        compiler_params=params(16),
        name="add",
    )(keep, got)


def finish(got, kept):
    return pl.pallas_call(
        finish_kernel,
        out_shape=(jax.ShapeDtypeStruct((QC, 128), BF),) * 2,
        in_specs=[VMEM] * 2,
        out_specs=(VMEM, VMEM),
        compiler_params=params(16),
        name="finish",
    )(got, kept)


def swap(x, bits):
    return lax.ppermute(x, "dev", [(d, d ^ bits) for d in range(MEMBERS)])


def swap_groups(x):
    return lax.ppermute(x, "grp", [(g, g ^ 4) for g in range(GROUPS)])


def collect_x(x):
    return lax.all_gather(x, "grp", axis=0, axis_index_groups=[[0, 1, 2, 3], [4, 5, 6, 7]])


def trade(x, groups):
    return lax.all_to_all(x, "dev", 0, 0, axis_index_groups=groups, tiled=True)


def collect(x):
    return lax.all_gather(x, "dev", axis=0, axis_index_groups=COLUMNS)


def after(x, other):
    return lax.optimization_barrier((x, other))[0]


def on_device(
    stream,
    row_length,
    row_start,
    attn_gain,
    w_query,
    w_key,
    w_value,
    w_out,
    ffn_gain,
    w_gate,
    w_up,
    w_down,
):
    member = lax.axis_index("dev")
    core = member % 2

    packed, token = pack(w_query.T, w_key.T, w_value.T, w_out.T)
    first = lax.all_to_all(packed, "grp", 0, 0, tiled=True)

    lane = jnp.arange(128, dtype=jnp.int32)
    column = jnp.where(lane < QC, member * QC + lane, member * KC + lane - QC)
    pair = (column % HEAD_DIM // 2).astype(F32)
    freq = jnp.exp(-(2.0 * pair / HEAD_DIM) * math.log(ROPE_BASE))
    positions = (row_start[:, None] + jnp.arange(ROW_LEN, dtype=jnp.int32)[None, :]).reshape(-1)
    angle = positions.astype(F32)[:, None] * freq[None, :]
    cos, sin = jnp.cos(angle), jnp.sin(angle)

    normed, own = norm(token, cos, stream, attn_gain.reshape(1, D))
    narrow = after(w_down.T, token)
    other = swap(narrow, 2)

    send, keys, values = project(normed, first, cos, sin)
    got = trade(send, OCTETS)
    mine = join(send, w_gate.T, w_up.T, narrow, other)
    mine_lo = swap_groups(after(mine, got))
    out_own = first[:, 96:160, :]
    out_weights = (out_own, swap(out_own, 1), swap(out_own, 2), swap(out_own, 3))
    mixed = collect(attend(row_length, got))
    attended = output(mixed, out_weights, own)
    mine, mine_lo = collect_x(mine), collect_x(after(mine_lo, attended))
    mine = after(mine, attended)
    core_mine = swap(mine, 1)
    same = trade(attended, PARITIES)
    other, far_same, far_other = swap(same, 4), swap(same, 2), swap(same, 6)
    gain = ffn_gain.reshape(1, D)
    near = near_half(same, other, gain)
    mine_lo = after(mine_lo, (far_same, far_other, near))
    core_lo = swap(mine_lo, 1)
    totals, kept, far_normed = own_rows(near, same, far_same, far_other, gain, mine, core_mine)
    units = partner_rows(near, far_normed, totals, mine_lo, core_lo)
    weights = (mine, mine_lo, core_mine, core_lo)
    keep, give = down(units, swap(units, 2), weights)
    sums = trade(add(keep, swap(give, 4)), PARITIES)
    keep, give = finish(sums, kept)
    give = swap(give, 1)
    rows = jnp.where(core == 0, jnp.concatenate([keep, give], axis=1), jnp.concatenate([give, keep], axis=1))
    return (keys.T, values.T, rows.T)


def solution(mesh):
    placed = (
        P("grp", None),
        P("grp"),
        P("grp"),
        P(),
        P("grp", "dev"),
        P("grp", "dev"),
        P("grp", "dev"),
        P("grp", "dev"),
        P(),
        P("grp", "dev"),
        P("grp", "dev"),
        P("grp", "dev"),
    )
    return jax.shard_map(
        on_device,
        mesh=mesh,
        in_specs=placed,
        out_specs=(P("grp", "dev"), P("grp", "dev"), P("grp", "dev")),
        check_vma=False,
    )
```

```python
import math

import jax
import jax.numpy as jnp
from jax import lax
from jax.experimental import pallas as pl
from jax.experimental.pallas import tpu as pltpu
from jax.sharding import PartitionSpec as P

HEADS = 32
KV_HEADS = 8
HEAD_DIM = 128
ROW_LEN = 128
D = 4096
ROPE_BASE = 500000.0

GROUPS = 8
MEMBERS = 64
DEPTH = 16
HALF = 64
QC = 64
KC = 16
FC = 224
BAND = 256
RUN = 512

COLUMNS = [[4 * z + q for z in range(DEPTH)] for q in range(4)]
PARITIES = [[4 * (2 * i + p) + q for i in range(8)] for p in range(2) for q in range(4)]
OCTETS = [[8 * z + m for m in range(8)] for z in range(8)]

BF = jnp.bfloat16
F32 = jnp.float32
VMEM = pl.BlockSpec(memory_space=pltpu.VMEM)
HBM = pl.BlockSpec(memory_space=pltpu.HBM)
ANY = pl.BlockSpec(memory_space=pl.ANY)
SMEM = pl.BlockSpec(memory_space=pltpu.SMEM)


def place():
    d = lax.axis_index("dev")
    return (d % 2, d // 2 % 2, d // 4, d // 4 % 2, d // 8, d % 4, lax.axis_index("grp") // 4)


def nt(a, b):
    return lax.dot_general(a, b, (((1,), (1,)), ((), ())), preferred_element_type=F32)


def whole(*shape):
    return pl.BlockSpec(shape, lambda i: (0,) * len(shape))


def params(mib):
    return pltpu.CompilerParams(vmem_limit_bytes=mib * 2**20)


def cost(flops, nbytes):
    return pl.CostEstimate(flops=flops, bytes_accessed=nbytes, transcendentals=0)


def project_kernel(after, normed, weights, cos, sin, send, keys, values, tables, sems):
    copies = [pltpu.make_async_copy(ref, tables.at[i], sems.at[i]) for i, ref in enumerate((cos, sin))]
    for copy in copies:
        copy.start()
    total = jnp.zeros((256, 96), F32)
    for g in range(GROUPS):
        total = total + nt(normed[g], weights[g, 0:96, :])
    total = jnp.concatenate([total, jnp.zeros((256, 32), F32)], axis=1)
    lane = lax.broadcasted_iota(jnp.int32, (256, 128), 1)
    partner = jnp.where(lane % 2 == 0, -pltpu.roll(total, 127, 1), pltpu.roll(total, 1, 1))
    for copy in copies:
        copy.wait()
    turned = jnp.where(lane < QC + KC, total * tables[0] + partner * tables[1], total)
    turned = turned.astype(BF).astype(F32)
    flipped = turned.T
    keys[...] = flipped[QC : QC + KC, :].astype(BF)
    values[...] = flipped[QC + KC : QC + 2 * KC, :].astype(BF)
    lane = lax.broadcasted_iota(jnp.int32, (HALF, 128), 1)
    for zl in range(2):
        for yhi in range(2):
            for c in range(2):
                first = turned[c * 128 : c * 128 + HALF, :]
                second = turned[c * 128 + HALF : c * 128 + 128, :]
                mine = second if yhi else first
                chunk = jnp.where(lane < QC, mine, jnp.where(lane < 96, first, pltpu.roll(second, 32, 1)))
                send[zl * 4 + yhi * 2 + c] = chunk.astype(BF)


def attend_kernel(lengths, got, out):
    at = place()
    lane = lax.broadcasted_iota(jnp.int32, (HALF, 128), 1)
    pieces = [got[m].astype(F32) for m in range(8)]

    def gather(start):
        full = jnp.zeros((HALF, 128), F32)
        for m in range(8):
            full = jnp.where(lane // KC == m, pltpu.roll(pieces[m], (KC * m - start) % 128, 1), full)
        return full.astype(BF)

    keys = jnp.concatenate([gather(QC), gather(96)], axis=0)
    values = jnp.concatenate([gather(QC + KC), gather(96 + KC)], axis=0)
    slot = lax.broadcasted_iota(jnp.int32, (HALF, 128), 0) + at[1] * HALF
    allowed = (lane <= slot) & (lane < lengths[at[0]])
    for a in range(2):
        low = got[at[3] * 4 + a * 2].astype(F32)
        high = got[at[3] * 4 + a * 2 + 1].astype(F32)
        queries = jnp.where(lane < QC, low, pltpu.roll(high, QC, 1)).astype(BF)
        scores = nt(queries, keys) / math.sqrt(HEAD_DIM)
        scores = jnp.where(allowed, scores, -jnp.inf)
        expo = jnp.exp(scores - jnp.max(scores, axis=-1, keepdims=True))
        probs = (expo / jnp.sum(expo, axis=-1, keepdims=True)).astype(BF)
        mixed = jnp.dot(probs, values, preferred_element_type=F32).astype(BF)
        out[:, a * 128 : a * 128 + 128] = mixed


def output_kernel(got, mine, core, far, cross, own, out):
    at = place()
    parts = []
    for w in (mine, core, far, cross):
        total = jnp.zeros((HALF, QC), F32)
        for g in range(GROUPS):
            total = total + nt(got[2 * g], w[g, :, 0:BAND]) + nt(got[2 * g + 1], w[g, :, BAND:RUN])
        parts.append(total)
    blocks = []
    for j in range(4):
        picked = parts[0]
        for k in range(1, 4):
            picked = jnp.where(jnp.bitwise_xor(at[5], j) == k, parts[k], picked)
        blocks.append(picked)
    projected = jnp.concatenate(blocks, axis=1)
    attended = (own[...].astype(F32) + projected).astype(BF)
    for i in range(8):
        out[i] = attended


def renorm(at, same, other, gain, out):
    low = at[3] == 0
    squares = jnp.zeros((HALF, 1), F32)
    for got in (same, other):
        for i in range(8):
            x = got[i].astype(F32)
            squares = squares + jnp.sum(x * x, axis=-1, keepdims=True)
    scale = lax.rsqrt(squares * (1.0 / D) + 1e-05)
    for i in range(8):
        one, two = same[i].astype(F32), other[i].astype(F32)
        for k, x in enumerate((jnp.where(low, one, two), jnp.where(low, two, one))):
            z = 2 * i + k
            out[i, :, k * BAND : (k + 1) * BAND] = (x * scale * gain[:, z * BAND : (z + 1) * BAND]).astype(BF)


def near_kernel(same, other, gain, out):
    at = place()
    renorm(at, same, other, gain, out)


def multiply(at, near, far, pair, side, totals):
    for x in range(4):
        g = jnp.bitwise_xor(at[6], side) * 4 + x
        rows = jnp.concatenate([near[g], far[g]], axis=0)
        for i, w in enumerate(pair):
            totals[2 * i] = totals[2 * i] + nt(rows, w[x, 0:FC, :])
            totals[2 * i + 1] = totals[2 * i + 1] + nt(rows, w[x, FC : 2 * FC, :])


def own_rows_kernel(near, same, far_same, far_other, gain, mine, core, out, kept, normed):
    at = place()
    low = at[1] == 0
    lanes = pl.ds(pl.multiple_of(at[1] * 128, 128), 128)
    near_kept, far_kept = same[at[4], :, lanes], far_same[at[4], :, lanes]
    kept[0:HALF, :] = jnp.where(low, near_kept, far_kept)
    kept[HALF : 2 * HALF, :] = jnp.where(low, far_kept, near_kept)
    renorm(at, far_same, far_other, gain, normed)
    totals = [jnp.zeros((2 * HALF, FC), F32) for _ in range(4)]
    multiply(at, near, normed, (mine, core), 0, totals)
    for i in range(4):
        out[i] = totals[i]


def down_kernel(near, far, before, mine, mine_lo, core, core_lo, keep, to_y, to_z, to_both, held, sems):
    at = place()
    copies = [
        pltpu.make_async_copy(w.at[x, pl.ds(2 * FC, FC), :], held.at[i, x], sems.at[i, x])
        for i, w in enumerate((mine, core))
        for x in range(4)
    ]
    for copy in copies:
        copy.start()
    low_y, low_z = at[1] == 0, at[3] == 0
    totals = [before[i] for i in range(4)]
    multiply(at, near, far, (mine_lo, core_lo), 1, totals)
    units = []
    for i in range(2):
        gate = totals[2 * i]
        part = (gate / (1.0 + jnp.exp(-gate)) * totals[2 * i + 1]).astype(BF)
        first, second = part[0:HALF, :], part[HALF : 2 * HALF, :]
        units.append(jnp.concatenate([jnp.where(low_y, first, second), jnp.where(low_y, second, first)], axis=0))
    for copy in copies:
        copy.wait()
    for x in range(4):
        for side in range(2):
            total = jnp.zeros((128, RUN), F32)
            for i, w in enumerate((mine_lo, core_lo)):
                block = w[x, 2 * FC : 3 * FC, :] if side else held[i, x]
                total = total + jnp.dot(units[i], block, preferred_element_type=F32)
            g = jnp.bitwise_xor(at[6], side) * 4 + x
            blocks = [total[:, k * 128 : (k + 1) * 128] for k in range(4)]
            same = [jnp.where(low_z, blocks[k], blocks[2 + k]) for k in range(2)]
            other = [jnp.where(low_z, blocks[2 + k], blocks[k]) for k in range(2)]
            keep[g] = jnp.where(low_y, same[0], same[1])
            to_y[g] = jnp.where(low_y, same[1], same[0]).astype(BF)
            to_z[g] = jnp.where(low_y, other[0], other[1]).astype(BF)
            to_both[g] = jnp.where(low_y, other[1], other[0]).astype(BF)


def add_kernel(keep, *refs):
    out = refs[-1]
    for i in range(8):
        total = keep[i]
        for got in refs[:-1]:
            total = total + got[i].astype(F32)
        out[i] = total.astype(BF)


def finish_kernel(got, kept, keep, give):
    at = place()
    total = kept[...].astype(F32)
    for i in range(8):
        total = total + got[i].astype(F32)
    result = total.T
    head, tail = result[0:QC, :], result[QC : 2 * QC, :]
    keep[...] = jnp.where(at[0] == 0, head, tail).astype(BF)
    give[...] = jnp.where(at[0] == 0, tail, head).astype(BF)


def pack_kernel(query, key, value, out_part, out, token, held, sems):
    token[...] = jnp.zeros_like(token)
    spans = ((query, 0, QC), (key, QC, KC), (value, QC + KC, KC), (out_part, 96, QC))
    reads = [
        pltpu.make_async_copy(ref, held.at[pl.ds(start, rows), :], sems.at[i])
        for i, (ref, start, rows) in enumerate(spans)
    ]
    for copy in reads:
        copy.start()
    for copy in reads:
        copy.wait()
    writes = [pltpu.make_async_copy(held, out.at[g], sems.at[4 + g]) for g in range(GROUPS)]
    for copy in writes:
        copy.start()
    for copy in writes:
        copy.wait()


def norm_kernel(after, tables, stream, gain, normed, own, held, gains, sems):
    at = place()
    copies = [
        pltpu.make_async_copy(stream, held, sems.at[0]),
        pltpu.make_async_copy(gain, gains, sems.at[1]),
    ]
    for copy in copies:
        copy.start()
    for copy in copies:
        copy.wait()
    x = held[...].astype(F32)
    scale = lax.rsqrt(jnp.mean(x * x, axis=-1, keepdims=True) + 1e-05)
    for g in range(GROUPS):
        cols = pl.ds(g * RUN, RUN)
        normed[g] = (held[:, cols].astype(F32) * scale * gains[:, cols]).astype(BF)
    rows = pl.ds(pl.multiple_of(at[0] * 128 + at[1] * HALF, HALF), HALF)
    own[...] = held[rows, pl.ds(pl.multiple_of(at[2] * BAND, BAND), BAND)]


def norm(after, tables, stream, gain):
    return pl.pallas_call(
        norm_kernel,
        out_shape=(jax.ShapeDtypeStruct((GROUPS, 256, RUN), BF), jax.ShapeDtypeStruct((HALF, BAND), BF)),
        in_specs=[ANY, ANY, HBM, HBM],
        out_specs=(VMEM,) * 2,
        scratch_shapes=[pltpu.VMEM((256, D), BF), pltpu.VMEM((1, D), F32), pltpu.SemaphoreType.DMA((2,))],
        compiler_params=params(24),
        name="norm",
    )(after, tables, stream, gain)


def join_kernel(after, gate, up, narrow, out, token, held, sems):
    token[...] = jnp.zeros_like(token)
    copies = [
        pltpu.make_async_copy(part, held.at[pl.ds(i * FC, FC), :], sems.at[i])
        for i, part in enumerate((gate, up, narrow))
    ]
    for copy in copies:
        copy.start()
    for copy in copies:
        copy.wait()
    whole_copy = pltpu.make_async_copy(held, out, sems.at[3])
    whole_copy.start()
    whole_copy.wait()


def join(after, *parts):
    return pl.pallas_call(
        join_kernel,
        out_shape=(jax.ShapeDtypeStruct((3 * FC, RUN), BF), jax.ShapeDtypeStruct((8, 128), F32)),
        in_specs=[ANY, HBM, HBM, HBM],
        out_specs=(HBM, VMEM),
        scratch_shapes=[pltpu.VMEM((3 * FC, RUN), BF), pltpu.SemaphoreType.DMA((4,))],
        compiler_params=params(60),
        name="join",
    )(after, *parts)


def pack(*parts):
    return pl.pallas_call(
        pack_kernel,
        out_shape=(jax.ShapeDtypeStruct((GROUPS, 160, RUN), BF), jax.ShapeDtypeStruct((8, 128), F32)),
        in_specs=[HBM] * 4,
        out_specs=(HBM, VMEM),
        scratch_shapes=[pltpu.VMEM((160, RUN), BF), pltpu.SemaphoreType.DMA((4 + GROUPS,))],
        compiler_params=params(60),
        name="pack",
    )(*parts)


def project(after, normed, weights, cos, sin):
    return pl.pallas_call(
        project_kernel,
        out_shape=(
            jax.ShapeDtypeStruct((8, HALF, 128), BF),
            jax.ShapeDtypeStruct((KC, 256), BF),
            jax.ShapeDtypeStruct((KC, 256), BF),
        ),
        in_specs=[ANY] + [VMEM] * 2 + [HBM] * 2,
        out_specs=(VMEM,) * 3,
        scratch_shapes=[pltpu.VMEM((2, 256, 128), F32), pltpu.SemaphoreType.DMA((2,))],
        compiler_params=params(24),
        name="project",
    )(after, normed, weights, cos, sin)


def attend(lengths, got):
    return pl.pallas_call(
        attend_kernel,
        out_shape=jax.ShapeDtypeStruct((HALF, BAND), BF),
        in_specs=[SMEM, VMEM],
        out_specs=VMEM,
        compiler_params=params(16),
        name="attend",
    )(lengths, got)


def output(got, weights, own):
    return pl.pallas_call(
        output_kernel,
        out_shape=jax.ShapeDtypeStruct((8, HALF, BAND), BF),
        in_specs=[VMEM] * 6,
        out_specs=VMEM,
        compiler_params=params(24),
        name="output",
    )(got, *weights, own)


def near_half(same, other, gain):
    return pl.pallas_call(
        near_kernel,
        out_shape=jax.ShapeDtypeStruct((GROUPS, HALF, RUN), BF),
        in_specs=[VMEM] * 3,
        out_specs=VMEM,
        compiler_params=params(16),
        name="near_half",
    )(same, other, gain)


def own_rows(near, same, far_same, far_other, gain, mine, core):
    return pl.pallas_call(
        own_rows_kernel,
        out_shape=(
            jax.ShapeDtypeStruct((4, 128, FC), F32),
            jax.ShapeDtypeStruct((128, 128), BF),
            jax.ShapeDtypeStruct((GROUPS, HALF, RUN), BF),
        ),
        in_specs=[VMEM] * 7,
        out_specs=(VMEM,) * 3,
        compiler_params=params(16),
        cost_estimate=cost(2 * HALF * D * 4 * FC, 4 * 2**20),
        name="own_rows",
    )(near, same, far_same, far_other, gain, mine, core)


def down(near, far, before, weights):
    part = jax.ShapeDtypeStruct((8, 128, 128), BF)
    return pl.pallas_call(
        down_kernel,
        out_shape=(jax.ShapeDtypeStruct((8, 128, 128), F32), part, part, part),
        in_specs=[VMEM] * 3 + [HBM, VMEM, ANY, VMEM],
        out_specs=(VMEM,) * 4,
        scratch_shapes=[pltpu.VMEM((2, 4, FC, RUN), BF), pltpu.SemaphoreType.DMA((2, 4))],
        compiler_params=params(16),
        cost_estimate=cost(4 * HALF * D * 4 * FC, 9 * 2**20),
        name="down",
    )(near, far, before, *weights)


def add(*parts):
    return pl.pallas_call(
        add_kernel,
        out_shape=jax.ShapeDtypeStruct((8, 128, 128), BF),
        in_specs=[VMEM] * 4,
        out_specs=VMEM,
        compiler_params=params(16),
        name="add",
    )(*parts)


def finish(got, kept):
    return pl.pallas_call(
        finish_kernel,
        out_shape=(jax.ShapeDtypeStruct((QC, 128), BF),) * 2,
        in_specs=[VMEM] * 2,
        out_specs=(VMEM, VMEM),
        compiler_params=params(16),
        name="finish",
    )(got, kept)


def swap(x, bits):
    return lax.ppermute(x, "dev", [(d, d ^ bits) for d in range(MEMBERS)])


def swap_groups(x):
    return lax.ppermute(x, "grp", [(g, g ^ 4) for g in range(GROUPS)])


def collect_x(x):
    return lax.all_gather(x, "grp", axis=0, axis_index_groups=[[0, 1, 2, 3], [4, 5, 6, 7]])


def trade(x, groups):
    return lax.all_to_all(x, "dev", 0, 0, axis_index_groups=groups, tiled=True)


def collect(x):
    return lax.all_gather(x, "dev", axis=0, axis_index_groups=COLUMNS)


def after(x, other):
    return lax.optimization_barrier((x, other))[0]


def on_device(
    stream,
    row_length,
    row_start,
    attn_gain,
    w_query,
    w_key,
    w_value,
    w_out,
    ffn_gain,
    w_gate,
    w_up,
    w_down,
):
    member = lax.axis_index("dev")
    core = member % 2

    packed, token = pack(w_query.T, w_key.T, w_value.T, w_out.T)
    first = lax.all_to_all(packed, "grp", 0, 0, tiled=True)

    lane = jnp.arange(128, dtype=jnp.int32)
    column = jnp.where(lane < QC, member * QC + lane, member * KC + lane - QC)
    pair = (column % HEAD_DIM // 2).astype(F32)
    freq = jnp.exp(-(2.0 * pair / HEAD_DIM) * math.log(ROPE_BASE))
    positions = (row_start[:, None] + jnp.arange(ROW_LEN, dtype=jnp.int32)[None, :]).reshape(-1)
    angle = positions.astype(F32)[:, None] * freq[None, :]
    cos, sin = jnp.cos(angle), jnp.sin(angle)

    normed, own = norm(token, cos, stream, attn_gain.reshape(1, D))
    mine, token = join(token, w_gate.T, w_up.T, w_down.T)
    send, keys, values = project(token, normed, first, cos, sin)
    got = trade(send, OCTETS)
    mine = after(mine, send)
    mine_lo = swap_groups(after(mine, got))
    out_own = first[:, 96:160, :]
    out_weights = (out_own, swap(out_own, 1), swap(out_own, 2), swap(out_own, 3))
    mixed = collect(attend(row_length, got))
    attended = output(mixed, out_weights, own)
    mine, mine_lo = collect_x(mine), collect_x(after(mine_lo, attended))
    mine = after(mine, attended)
    core_mine = swap(mine, 1)
    same = trade(attended, PARITIES)
    other, far_same, far_other = swap(same, 4), swap(same, 2), swap(same, 6)
    gain = ffn_gain.reshape(1, D)
    near = near_half(same, other, gain)
    mine_lo = after(mine_lo, (far_same, far_other, near))
    core_lo = swap(mine_lo, 1)
    totals, kept, far_normed = own_rows(near, same, far_same, far_other, gain, mine, core_mine)
    weights = (mine, mine_lo, core_mine, core_lo)
    keep, to_y, to_z, to_both = down(near, far_normed, totals, weights)
    sums = trade(add(keep, swap(to_y, 2), swap(to_z, 4), swap(to_both, 6)), PARITIES)
    keep, give = finish(sums, kept)
    give = swap(give, 1)
    rows = jnp.where(core == 0, jnp.concatenate([keep, give], axis=1), jnp.concatenate([give, keep], axis=1))
    return (keys.T, values.T, rows.T)


def solution(mesh):
    placed = (
        P("grp", None),
        P("grp"),
        P("grp"),
        P(),
        P("grp", "dev"),
        P("grp", "dev"),
        P("grp", "dev"),
        P("grp", "dev"),
        P(),
        P("grp", "dev"),
        P("grp", "dev"),
        P("grp", "dev"),
    )
    return jax.shard_map(
        on_device,
        mesh=mesh,
        in_specs=placed,
        out_specs=(P("grp", "dev"), P("grp", "dev"), P("grp", "dev")),
        check_vma=False,
    )
```

```python
import math

import jax
import jax.numpy as jnp
from jax import lax
from jax.experimental import pallas as pl
from jax.experimental.pallas import tpu as pltpu
from jax.sharding import PartitionSpec as P

HEADS = 32
KV_HEADS = 8
HEAD_DIM = 128
ROW_LEN = 128
D = 4096
ROPE_BASE = 500000.0

GROUPS = 8
MEMBERS = 64
DEPTH = 16
HALF = 64
QC = 64
KC = 16
FC = 224
BAND = 256
RUN = 512

COLUMNS = [[4 * z + q for z in range(DEPTH)] for q in range(4)]
PARITIES = [[4 * (2 * i + p) + q for i in range(8)] for p in range(2) for q in range(4)]
OCTETS = [[8 * z + m for m in range(8)] for z in range(8)]

BF = jnp.bfloat16
F32 = jnp.float32
VMEM = pl.BlockSpec(memory_space=pltpu.VMEM)
HBM = pl.BlockSpec(memory_space=pltpu.HBM)
ANY = pl.BlockSpec(memory_space=pl.ANY)
SMEM = pl.BlockSpec(memory_space=pltpu.SMEM)


def place():
    d = lax.axis_index("dev")
    return (d % 2, d // 2 % 2, d // 4, d // 4 % 2, d // 8, d % 4, lax.axis_index("grp") // 4)


def nt(a, b):
    return lax.dot_general(a, b, (((1,), (1,)), ((), ())), preferred_element_type=F32)


def whole(*shape):
    return pl.BlockSpec(shape, lambda i: (0,) * len(shape))


def params(mib):
    return pltpu.CompilerParams(vmem_limit_bytes=mib * 2**20)


def cost(flops, nbytes):
    return pl.CostEstimate(flops=flops, bytes_accessed=nbytes, transcendentals=0)


def project_kernel(after, core_out, far_out, cross_out, normed, weights, cos, sin, send, keys, values, tables, sems):
    copies = [pltpu.make_async_copy(ref, tables.at[i], sems.at[i]) for i, ref in enumerate((cos, sin))]
    for copy in copies:
        copy.start()
    total = jnp.zeros((256, 96), F32)
    for g in range(GROUPS):
        total = total + nt(normed[g], weights[g])
    total = jnp.concatenate([total, jnp.zeros((256, 32), F32)], axis=1)
    lane = lax.broadcasted_iota(jnp.int32, (256, 128), 1)
    partner = jnp.where(lane % 2 == 0, -pltpu.roll(total, 127, 1), pltpu.roll(total, 1, 1))
    for copy in copies:
        copy.wait()
    turned = jnp.where(lane < QC + KC, total * tables[0] + partner * tables[1], total)
    turned = turned.astype(BF).astype(F32)
    flipped = turned.T
    keys[...] = flipped[QC : QC + KC, :].astype(BF)
    values[...] = flipped[QC + KC : QC + 2 * KC, :].astype(BF)
    lane = lax.broadcasted_iota(jnp.int32, (HALF, 128), 1)
    for zl in range(2):
        for yhi in range(2):
            for c in range(2):
                first = turned[c * 128 : c * 128 + HALF, :]
                second = turned[c * 128 + HALF : c * 128 + 128, :]
                mine = second if yhi else first
                chunk = jnp.where(lane < QC, mine, jnp.where(lane < 96, first, pltpu.roll(second, 32, 1)))
                send[zl * 4 + yhi * 2 + c] = chunk.astype(BF)


def attend_kernel(lengths, got, out):
    at = place()
    lane = lax.broadcasted_iota(jnp.int32, (HALF, 128), 1)
    pieces = [got[m].astype(F32) for m in range(8)]

    def gather(start):
        full = jnp.zeros((HALF, 128), F32)
        for m in range(8):
            full = jnp.where(lane // KC == m, pltpu.roll(pieces[m], (KC * m - start) % 128, 1), full)
        return full.astype(BF)

    keys = jnp.concatenate([gather(QC), gather(96)], axis=0)
    values = jnp.concatenate([gather(QC + KC), gather(96 + KC)], axis=0)
    slot = lax.broadcasted_iota(jnp.int32, (HALF, 128), 0) + at[1] * HALF
    allowed = (lane <= slot) & (lane < lengths[at[0]])
    for a in range(2):
        low = got[at[3] * 4 + a * 2].astype(F32)
        high = got[at[3] * 4 + a * 2 + 1].astype(F32)
        queries = jnp.where(lane < QC, low, pltpu.roll(high, QC, 1)).astype(BF)
        scores = nt(queries, keys) / math.sqrt(HEAD_DIM)
        scores = jnp.where(allowed, scores, -jnp.inf)
        expo = jnp.exp(scores - jnp.max(scores, axis=-1, keepdims=True))
        probs = (expo / jnp.sum(expo, axis=-1, keepdims=True)).astype(BF)
        mixed = jnp.dot(probs, values, preferred_element_type=F32).astype(BF)
        out[:, a * 128 : a * 128 + 128] = mixed


def output_kernel(got, weights, own, out):
    projected = jnp.zeros((HALF, BAND), F32)
    for g in range(GROUPS):
        projected = projected + nt(got[2 * g], weights[g, :, 0:BAND]) + nt(got[2 * g + 1], weights[g, :, BAND:RUN])
    attended = (own[...].astype(F32) + projected).astype(BF)
    for i in range(8):
        out[i] = attended


def renorm(at, same, other, gain, out):
    low = at[3] == 0
    squares = jnp.zeros((HALF, 1), F32)
    for got in (same, other):
        for i in range(8):
            x = got[i].astype(F32)
            squares = squares + jnp.sum(x * x, axis=-1, keepdims=True)
    scale = lax.rsqrt(squares * (1.0 / D) + 1e-05)
    for i in range(8):
        one, two = same[i].astype(F32), other[i].astype(F32)
        for k, x in enumerate((jnp.where(low, one, two), jnp.where(low, two, one))):
            z = 2 * i + k
            out[i, :, k * BAND : (k + 1) * BAND] = (x * scale * gain[:, z * BAND : (z + 1) * BAND]).astype(BF)


def near_kernel(same, other, gain, out):
    at = place()
    renorm(at, same, other, gain, out)


def multiply(at, near, far, pair, side, totals):
    for x in range(4):
        g = jnp.bitwise_xor(at[6], side) * 4 + x
        rows = jnp.concatenate([near[g], far[g]], axis=0)
        for i, w in enumerate(pair):
            totals[2 * i] = totals[2 * i] + nt(rows, w[x, 0:FC, :])
            totals[2 * i + 1] = totals[2 * i + 1] + nt(rows, w[x, FC : 2 * FC, :])


def own_rows_kernel(near, same, far_same, far_other, gain, mine, core, out, kept, normed):
    at = place()
    low = at[1] == 0
    lanes = pl.ds(pl.multiple_of(at[1] * 128, 128), 128)
    near_kept, far_kept = same[at[4], :, lanes], far_same[at[4], :, lanes]
    kept[0:HALF, :] = jnp.where(low, near_kept, far_kept)
    kept[HALF : 2 * HALF, :] = jnp.where(low, far_kept, near_kept)
    renorm(at, far_same, far_other, gain, normed)
    totals = [jnp.zeros((2 * HALF, FC), F32) for _ in range(4)]
    multiply(at, near, normed, (mine, core), 0, totals)
    for i in range(4):
        out[i] = totals[i]


def down_kernel(near, far, before, mine, mine_lo, core, core_lo, keep, to_y, to_z, to_both):
    at = place()
    low_y, low_z = at[1] == 0, at[3] == 0
    totals = [before[i] for i in range(4)]
    multiply(at, near, far, (mine_lo, core_lo), 1, totals)
    units = []
    for i in range(2):
        gate = totals[2 * i]
        part = (gate / (1.0 + jnp.exp(-gate)) * totals[2 * i + 1]).astype(BF)
        first, second = part[0:HALF, :], part[HALF : 2 * HALF, :]
        units.append(jnp.concatenate([jnp.where(low_y, first, second), jnp.where(low_y, second, first)], axis=0))
    for x in range(4):
        for side, pair in enumerate(((mine, core), (mine_lo, core_lo))):
            total = jnp.zeros((128, RUN), F32)
            for i, w in enumerate(pair):
                total = total + jnp.dot(units[i], w[x, 2 * FC : 3 * FC, :], preferred_element_type=F32)
            g = jnp.bitwise_xor(at[6], side) * 4 + x
            blocks = [total[:, k * 128 : (k + 1) * 128] for k in range(4)]
            same = [jnp.where(low_z, blocks[k], blocks[2 + k]) for k in range(2)]
            other = [jnp.where(low_z, blocks[2 + k], blocks[k]) for k in range(2)]
            keep[g] = jnp.where(low_y, same[0], same[1])
            to_y[g] = jnp.where(low_y, same[1], same[0]).astype(BF)
            to_z[g] = jnp.where(low_y, other[0], other[1]).astype(BF)
            to_both[g] = jnp.where(low_y, other[1], other[0]).astype(BF)


def add_kernel(keep, *refs):
    out = refs[-1]
    for i in range(8):
        total = keep[i]
        for got in refs[:-1]:
            total = total + got[i].astype(F32)
        out[i] = total.astype(BF)


def finish_kernel(got, kept, keep, give):
    at = place()
    total = kept[...].astype(F32)
    for i in range(8):
        total = total + got[i].astype(F32)
    result = total.T
    head, tail = result[0:QC, :], result[QC : 2 * QC, :]
    keep[...] = jnp.where(at[0] == 0, head, tail).astype(BF)
    give[...] = jnp.where(at[0] == 0, tail, head).astype(BF)


def spread(reads, held, out, sems):
    for copy in reads:
        copy.start()
    for copy in reads:
        copy.wait()
    writes = [pltpu.make_async_copy(held, out.at[g], sems.at[len(reads) + g]) for g in range(GROUPS)]
    for copy in writes:
        copy.start()
    for copy in writes:
        copy.wait()


def pack_kernel(query, key, value, out, token, held, sems):
    token[...] = jnp.zeros_like(token)
    spans = ((query, 0, QC), (key, QC, KC), (value, QC + KC, KC))
    reads = [
        pltpu.make_async_copy(ref, held.at[pl.ds(start, rows), :], sems.at[i])
        for i, (ref, start, rows) in enumerate(spans)
    ]
    spread(reads, held, out, sems)


def pack_out_kernel(after, mine, core, far, cross, out):
    quad = place()[5]
    for k, ref in enumerate((mine, core, far, cross)):
        rows = pl.ds(pl.multiple_of(jnp.bitwise_xor(quad, k) * QC, QC), QC)
        for g in range(GROUPS):
            out[g, rows, :] = ref[...]


def pack_out(after, *parts):
    return pl.pallas_call(
        pack_out_kernel,
        out_shape=jax.ShapeDtypeStruct((GROUPS, BAND, RUN), BF),
        in_specs=[ANY] + [VMEM] * 4,
        out_specs=VMEM,
        compiler_params=params(16),
        name="pack_out",
    )(after, *parts)


def norm_kernel(after, tables, stream, gain, normed, own, held, gains, sems):
    at = place()
    copies = [
        pltpu.make_async_copy(stream, held, sems.at[0]),
        pltpu.make_async_copy(gain, gains, sems.at[1]),
    ]
    for copy in copies:
        copy.start()
    for copy in copies:
        copy.wait()
    x = held[...].astype(F32)
    scale = lax.rsqrt(jnp.mean(x * x, axis=-1, keepdims=True) + 1e-05)
    for g in range(GROUPS):
        cols = pl.ds(g * RUN, RUN)
        normed[g] = (held[:, cols].astype(F32) * scale * gains[:, cols]).astype(BF)
    rows = pl.ds(pl.multiple_of(at[0] * 128 + at[1] * HALF, HALF), HALF)
    own[...] = held[rows, pl.ds(pl.multiple_of(at[2] * BAND, BAND), BAND)]


def norm(after, tables, stream, gain):
    return pl.pallas_call(
        norm_kernel,
        out_shape=(jax.ShapeDtypeStruct((GROUPS, 256, RUN), BF), jax.ShapeDtypeStruct((HALF, BAND), BF)),
        in_specs=[ANY, ANY, HBM, HBM],
        out_specs=(VMEM,) * 2,
        scratch_shapes=[pltpu.VMEM((256, D), BF), pltpu.VMEM((1, D), F32), pltpu.SemaphoreType.DMA((2,))],
        compiler_params=params(24),
        name="norm",
    )(after, tables, stream, gain)


def join_kernel(after, gate, up, narrow, out, token, held, sems):
    token[...] = jnp.zeros_like(token)
    copies = [
        pltpu.make_async_copy(part, held.at[pl.ds(i * FC, FC), :], sems.at[i])
        for i, part in enumerate((gate, up, narrow))
    ]
    for copy in copies:
        copy.start()
    for copy in copies:
        copy.wait()
    whole_copy = pltpu.make_async_copy(held, out, sems.at[3])
    whole_copy.start()
    whole_copy.wait()


def join(after, *parts):
    return pl.pallas_call(
        join_kernel,
        out_shape=(jax.ShapeDtypeStruct((3 * FC, RUN), BF), jax.ShapeDtypeStruct((8, 128), F32)),
        in_specs=[ANY, HBM, HBM, HBM],
        out_specs=(HBM, VMEM),
        scratch_shapes=[pltpu.VMEM((3 * FC, RUN), BF), pltpu.SemaphoreType.DMA((4,))],
        compiler_params=params(60),
        name="join",
    )(after, *parts)


def pack(*parts):
    return pl.pallas_call(
        pack_kernel,
        out_shape=(jax.ShapeDtypeStruct((GROUPS, 96, RUN), BF), jax.ShapeDtypeStruct((8, 128), F32)),
        in_specs=[HBM] * 3,
        out_specs=(HBM, VMEM),
        scratch_shapes=[pltpu.VMEM((96, RUN), BF), pltpu.SemaphoreType.DMA((3 + GROUPS,))],
        compiler_params=params(60),
        name="pack",
    )(*parts)


def project(after, traded, normed, weights, cos, sin):
    return pl.pallas_call(
        project_kernel,
        out_shape=(
            jax.ShapeDtypeStruct((8, HALF, 128), BF),
            jax.ShapeDtypeStruct((KC, 256), BF),
            jax.ShapeDtypeStruct((KC, 256), BF),
        ),
        in_specs=[ANY] * 4 + [VMEM] * 2 + [HBM] * 2,
        out_specs=(VMEM,) * 3,
        scratch_shapes=[pltpu.VMEM((2, 256, 128), F32), pltpu.SemaphoreType.DMA((2,))],
        compiler_params=params(24),
        name="project",
    )(after, *traded, normed, weights, cos, sin)


def attend(lengths, got):
    return pl.pallas_call(
        attend_kernel,
        out_shape=jax.ShapeDtypeStruct((HALF, BAND), BF),
        in_specs=[SMEM, VMEM],
        out_specs=VMEM,
        compiler_params=params(16),
        name="attend",
    )(lengths, got)


def output(got, weights, own):
    return pl.pallas_call(
        output_kernel,
        out_shape=jax.ShapeDtypeStruct((8, HALF, BAND), BF),
        in_specs=[VMEM] * 3,
        out_specs=VMEM,
        compiler_params=params(24),
        name="output",
    )(got, weights, own)


def near_half(same, other, gain):
    return pl.pallas_call(
        near_kernel,
        out_shape=jax.ShapeDtypeStruct((GROUPS, HALF, RUN), BF),
        in_specs=[VMEM] * 3,
        out_specs=VMEM,
        compiler_params=params(16),
        name="near_half",
    )(same, other, gain)


def own_rows(near, same, far_same, far_other, gain, mine, core):
    return pl.pallas_call(
        own_rows_kernel,
        out_shape=(
            jax.ShapeDtypeStruct((4, 128, FC), F32),
            jax.ShapeDtypeStruct((128, 128), BF),
            jax.ShapeDtypeStruct((GROUPS, HALF, RUN), BF),
        ),
        in_specs=[VMEM] * 7,
        out_specs=(VMEM,) * 3,
        compiler_params=params(16),
        cost_estimate=cost(2 * HALF * D * 4 * FC, 4 * 2**20),
        name="own_rows",
    )(near, same, far_same, far_other, gain, mine, core)


def down(near, far, before, weights):
    part = jax.ShapeDtypeStruct((8, 128, 128), BF)
    return pl.pallas_call(
        down_kernel,
        out_shape=(jax.ShapeDtypeStruct((8, 128, 128), F32), part, part, part),
        in_specs=[VMEM] * 7,
        out_specs=(VMEM,) * 4,
        compiler_params=params(16),
        cost_estimate=cost(4 * HALF * D * 4 * FC, 9 * 2**20),
        name="down",
    )(near, far, before, *weights)


def add(*parts):
    return pl.pallas_call(
        add_kernel,
        out_shape=jax.ShapeDtypeStruct((8, 128, 128), BF),
        in_specs=[VMEM] * 4,
        out_specs=VMEM,
        compiler_params=params(16),
        name="add",
    )(*parts)


def finish(got, kept):
    return pl.pallas_call(
        finish_kernel,
        out_shape=(jax.ShapeDtypeStruct((QC, 128), BF),) * 2,
        in_specs=[VMEM] * 2,
        out_specs=(VMEM, VMEM),
        compiler_params=params(16),
        name="finish",
    )(got, kept)


def swap(x, bits):
    return lax.ppermute(x, "dev", [(d, d ^ bits) for d in range(MEMBERS)])


def swap_groups(x):
    return lax.ppermute(x, "grp", [(g, g ^ 4) for g in range(GROUPS)])


def collect_x(x):
    return lax.all_gather(x, "grp", axis=0, axis_index_groups=[[0, 1, 2, 3], [4, 5, 6, 7]])


def trade(x, groups):
    return lax.all_to_all(x, "dev", 0, 0, axis_index_groups=groups, tiled=True)


def collect(x):
    return lax.all_gather(x, "dev", axis=0, axis_index_groups=COLUMNS)


def after(x, other):
    return lax.optimization_barrier((x, other))[0]


def on_device(
    stream,
    row_length,
    row_start,
    attn_gain,
    w_query,
    w_key,
    w_value,
    w_out,
    ffn_gain,
    w_gate,
    w_up,
    w_down,
):
    member = lax.axis_index("dev")
    core = member % 2

    packed, token = pack(w_query.T, w_key.T, w_value.T)
    first = lax.all_to_all(packed, "grp", 0, 0, tiled=True)

    lane = jnp.arange(128, dtype=jnp.int32)
    column = jnp.where(lane < QC, member * QC + lane, member * KC + lane - QC)
    pair = (column % HEAD_DIM // 2).astype(F32)
    freq = jnp.exp(-(2.0 * pair / HEAD_DIM) * math.log(ROPE_BASE))
    positions = (row_start[:, None] + jnp.arange(ROW_LEN, dtype=jnp.int32)[None, :]).reshape(-1)
    angle = positions.astype(F32)[:, None] * freq[None, :]
    cos, sin = jnp.cos(angle), jnp.sin(angle)

    normed, own = norm(token, cos, stream, attn_gain.reshape(1, D))
    own_out = after(w_out.T, token)
    traded = (swap(own_out, 1), swap(own_out, 2), swap(own_out, 3))
    mine, token = join(token, w_gate.T, w_up.T, w_down.T)
    send, keys, values = project(token, traded, normed, first, cos, sin)
    got = trade(send, OCTETS)
    mine = after(mine, send)
    out_weights = pack_out(got, own_out, *traded)
    out_weights = lax.all_to_all(out_weights, "grp", 0, 0, tiled=True)
    mine_lo = swap_groups(after(mine, got))
    mixed = collect(attend(row_length, got))
    attended = output(mixed, out_weights, own)
    mine, mine_lo = collect_x(mine), collect_x(after(mine_lo, attended))
    mine = after(mine, attended)
    core_mine = swap(mine, 1)
    same = trade(attended, PARITIES)
    other, far_same, far_other = swap(same, 4), swap(same, 2), swap(same, 6)
    gain = ffn_gain.reshape(1, D)
    near = near_half(same, other, gain)
    mine_lo = after(mine_lo, (far_same, far_other, near))
    core_lo = swap(mine_lo, 1)
    totals, kept, far_normed = own_rows(near, same, far_same, far_other, gain, mine, core_mine)
    weights = (mine, mine_lo, core_mine, core_lo)
    keep, to_y, to_z, to_both = down(near, far_normed, totals, weights)
    sums = trade(add(keep, swap(to_y, 2), swap(to_z, 4), swap(to_both, 6)), PARITIES)
    keep, give = finish(sums, kept)
    give = swap(give, 1)
    rows = jnp.where(core == 0, jnp.concatenate([keep, give], axis=1), jnp.concatenate([give, keep], axis=1))
    return (keys.T, values.T, rows.T)


def solution(mesh):
    placed = (
        P("grp", None),
        P("grp"),
        P("grp"),
        P(),
        P("grp", "dev"),
        P("grp", "dev"),
        P("grp", "dev"),
        P("grp", "dev"),
        P(),
        P("grp", "dev"),
        P("grp", "dev"),
        P("grp", "dev"),
    )
    return jax.shard_map(
        on_device,
        mesh=mesh,
        in_specs=placed,
        out_specs=(P("grp", "dev"), P("grp", "dev"), P("grp", "dev")),
        check_vma=False,
    )
```

```python
import math

import jax
import jax.numpy as jnp
from jax import lax
from jax.experimental import pallas as pl
from jax.experimental.pallas import tpu as pltpu
from jax.sharding import PartitionSpec as P

HEADS = 32
KV_HEADS = 8
HEAD_DIM = 128
ROW_LEN = 128
D = 4096
ROPE_BASE = 500000.0

GROUPS = 8
MEMBERS = 64
DEPTH = 16
HALF = 64
QC = 64
KC = 16
FC = 224
BAND = 256
RUN = 512

COLUMNS = [[4 * z + q for z in range(DEPTH)] for q in range(4)]
PARITIES = [[4 * (2 * i + p) + q for i in range(8)] for p in range(2) for q in range(4)]
OCTETS = [[8 * z + m for m in range(8)] for z in range(8)]

BF = jnp.bfloat16
F32 = jnp.float32
VMEM = pl.BlockSpec(memory_space=pltpu.VMEM)
HBM = pl.BlockSpec(memory_space=pltpu.HBM)
ANY = pl.BlockSpec(memory_space=pl.ANY)
SMEM = pl.BlockSpec(memory_space=pltpu.SMEM)


def place():
    d = lax.axis_index("dev")
    return (d % 2, d // 2 % 2, d // 4, d // 4 % 2, d // 8, d % 4, lax.axis_index("grp") // 4)


def nt(a, b):
    return lax.dot_general(a, b, (((1,), (1,)), ((), ())), preferred_element_type=F32)


def whole(*shape):
    return pl.BlockSpec(shape, lambda i: (0,) * len(shape))


def params(mib):
    return pltpu.CompilerParams(vmem_limit_bytes=mib * 2**20)


def cost(flops, nbytes):
    return pl.CostEstimate(flops=flops, bytes_accessed=nbytes, transcendentals=0)


def project_kernel(normed, weights, cos, sin, send, keys, values, rows, cols, tables, sems):
    copies = []
    for g in range(GROUPS):
        copies.append(pltpu.make_async_copy(normed.at[g], rows.at[g], sems.at[2 * g]))
        copies.append(pltpu.make_async_copy(weights.at[g, pl.ds(0, 96), :], cols.at[g], sems.at[2 * g + 1]))
    for i, ref in enumerate((cos, sin)):
        copies.append(pltpu.make_async_copy(ref, tables.at[i], sems.at[2 * GROUPS + i]))
    for copy in copies:
        copy.start()
    total = jnp.zeros((256, 96), F32)
    for g in range(GROUPS):
        copies[2 * g].wait()
        copies[2 * g + 1].wait()
        total = total + nt(rows[g], cols[g])
    total = jnp.concatenate([total, jnp.zeros((256, 32), F32)], axis=1)
    lane = lax.broadcasted_iota(jnp.int32, (256, 128), 1)
    partner = jnp.where(lane % 2 == 0, -pltpu.roll(total, 127, 1), pltpu.roll(total, 1, 1))
    for copy in copies[2 * GROUPS :]:
        copy.wait()
    turned = jnp.where(lane < QC + KC, total * tables[0] + partner * tables[1], total)
    turned = turned.astype(BF).astype(F32)
    flipped = turned.T
    keys[...] = flipped[QC : QC + KC, :].astype(BF)
    values[...] = flipped[QC + KC : QC + 2 * KC, :].astype(BF)
    lane = lax.broadcasted_iota(jnp.int32, (HALF, 128), 1)
    for zl in range(2):
        for yhi in range(2):
            for c in range(2):
                first = turned[c * 128 : c * 128 + HALF, :]
                second = turned[c * 128 + HALF : c * 128 + 128, :]
                mine = second if yhi else first
                chunk = jnp.where(lane < QC, mine, jnp.where(lane < 96, first, pltpu.roll(second, 32, 1)))
                send[zl * 4 + yhi * 2 + c] = chunk.astype(BF)


def attend_kernel(lengths, got, out):
    at = place()
    lane = lax.broadcasted_iota(jnp.int32, (HALF, 128), 1)
    pieces = [got[m].astype(F32) for m in range(8)]

    def gather(start):
        full = jnp.zeros((HALF, 128), F32)
        for m in range(8):
            full = jnp.where(lane // KC == m, pltpu.roll(pieces[m], (KC * m - start) % 128, 1), full)
        return full.astype(BF)

    keys = jnp.concatenate([gather(QC), gather(96)], axis=0)
    values = jnp.concatenate([gather(QC + KC), gather(96 + KC)], axis=0)
    slot = lax.broadcasted_iota(jnp.int32, (HALF, 128), 0) + at[1] * HALF
    allowed = (lane <= slot) & (lane < lengths[at[0]])
    for a in range(2):
        low = got[at[3] * 4 + a * 2].astype(F32)
        high = got[at[3] * 4 + a * 2 + 1].astype(F32)
        queries = jnp.where(lane < QC, low, pltpu.roll(high, QC, 1)).astype(BF)
        scores = nt(queries, keys) / math.sqrt(HEAD_DIM)
        scores = jnp.where(allowed, scores, -jnp.inf)
        expo = jnp.exp(scores - jnp.max(scores, axis=-1, keepdims=True))
        probs = (expo / jnp.sum(expo, axis=-1, keepdims=True)).astype(BF)
        mixed = jnp.dot(probs, values, preferred_element_type=F32).astype(BF)
        out[:, a * 128 : a * 128 + 128] = mixed


def output_kernel(got, mine, core, far, cross, own, out):
    at = place()
    parts = []
    for w in (mine, core, far, cross):
        total = jnp.zeros((HALF, QC), F32)
        for g in range(GROUPS):
            total = total + nt(got[2 * g], w[g, :, 0:BAND]) + nt(got[2 * g + 1], w[g, :, BAND:RUN])
        parts.append(total)
    blocks = []
    for j in range(4):
        picked = parts[0]
        for k in range(1, 4):
            picked = jnp.where(jnp.bitwise_xor(at[5], j) == k, parts[k], picked)
        blocks.append(picked)
    projected = jnp.concatenate(blocks, axis=1)
    attended = (own[...].astype(F32) + projected).astype(BF)
    for i in range(8):
        out[i] = attended


def renorm(at, same, other, gain, out):
    low = at[3] == 0
    squares = jnp.zeros((HALF, 1), F32)
    for got in (same, other):
        for i in range(8):
            x = got[i].astype(F32)
            squares = squares + jnp.sum(x * x, axis=-1, keepdims=True)
    scale = lax.rsqrt(squares * (1.0 / D) + 1e-05)
    for i in range(8):
        one, two = same[i].astype(F32), other[i].astype(F32)
        for k, x in enumerate((jnp.where(low, one, two), jnp.where(low, two, one))):
            z = 2 * i + k
            out[i, :, k * BAND : (k + 1) * BAND] = (x * scale * gain[:, z * BAND : (z + 1) * BAND]).astype(BF)


def near_kernel(same, other, gain, out):
    at = place()
    renorm(at, same, other, gain, out)


def multiply(at, near, far, pair, side, totals):
    for x in range(4):
        g = jnp.bitwise_xor(at[6], side) * 4 + x
        rows = jnp.concatenate([near[g], far[g]], axis=0)
        for i, w in enumerate(pair):
            totals[2 * i] = totals[2 * i] + nt(rows, w[x, 0:FC, :])
            totals[2 * i + 1] = totals[2 * i + 1] + nt(rows, w[x, FC : 2 * FC, :])


def own_rows_kernel(near, same, far_same, far_other, gain, mine, core, out, kept, normed):
    at = place()
    low = at[1] == 0
    lanes = pl.ds(pl.multiple_of(at[1] * 128, 128), 128)
    near_kept, far_kept = same[at[4], :, lanes], far_same[at[4], :, lanes]
    kept[0:HALF, :] = jnp.where(low, near_kept, far_kept)
    kept[HALF : 2 * HALF, :] = jnp.where(low, far_kept, near_kept)
    renorm(at, far_same, far_other, gain, normed)
    totals = [jnp.zeros((2 * HALF, FC), F32) for _ in range(4)]
    multiply(at, near, normed, (mine, core), 0, totals)
    for i in range(4):
        out[i] = totals[i]


def down_kernel(near, far, before, mine, mine_lo, core, core_lo, keep, to_y, to_z, to_both):
    at = place()
    low_y, low_z = at[1] == 0, at[3] == 0
    totals = [before[i] for i in range(4)]
    multiply(at, near, far, (mine_lo, core_lo), 1, totals)
    units = []
    for i in range(2):
        gate = totals[2 * i]
        part = (gate / (1.0 + jnp.exp(-gate)) * totals[2 * i + 1]).astype(BF)
        first, second = part[0:HALF, :], part[HALF : 2 * HALF, :]
        units.append(jnp.concatenate([jnp.where(low_y, first, second), jnp.where(low_y, second, first)], axis=0))
    for x in range(4):
        for side, pair in enumerate(((mine, core), (mine_lo, core_lo))):
            total = jnp.zeros((128, RUN), F32)
            for i, w in enumerate(pair):
                total = total + jnp.dot(units[i], w[x, 2 * FC : 3 * FC, :], preferred_element_type=F32)
            g = jnp.bitwise_xor(at[6], side) * 4 + x
            blocks = [total[:, k * 128 : (k + 1) * 128] for k in range(4)]
            same = [jnp.where(low_z, blocks[k], blocks[2 + k]) for k in range(2)]
            other = [jnp.where(low_z, blocks[2 + k], blocks[k]) for k in range(2)]
            keep[g] = jnp.where(low_y, same[0], same[1])
            to_y[g] = jnp.where(low_y, same[1], same[0]).astype(BF)
            to_z[g] = jnp.where(low_y, other[0], other[1]).astype(BF)
            to_both[g] = jnp.where(low_y, other[1], other[0]).astype(BF)


def add_kernel(keep, *refs):
    out = refs[-1]
    for i in range(8):
        total = keep[i]
        for got in refs[:-1]:
            total = total + got[i].astype(F32)
        out[i] = total.astype(BF)


def finish_kernel(got, kept, keep, give):
    at = place()
    total = kept[...].astype(F32)
    for i in range(8):
        total = total + got[i].astype(F32)
    result = total.T
    head, tail = result[0:QC, :], result[QC : 2 * QC, :]
    keep[...] = jnp.where(at[0] == 0, head, tail).astype(BF)
    give[...] = jnp.where(at[0] == 0, tail, head).astype(BF)


def pack_kernel(query, key, value, out_part, out, token, held, sems):
    token[...] = jnp.zeros_like(token)
    spans = ((query, 0, QC), (key, QC, KC), (value, QC + KC, KC), (out_part, 96, QC))
    reads = [
        pltpu.make_async_copy(ref, held.at[pl.ds(start, rows), :], sems.at[i])
        for i, (ref, start, rows) in enumerate(spans)
    ]
    for copy in reads:
        copy.start()
    for copy in reads:
        copy.wait()
    writes = [pltpu.make_async_copy(held, out.at[g], sems.at[4 + g]) for g in range(GROUPS)]
    for copy in writes:
        copy.start()
    for copy in writes:
        copy.wait()


def norm_kernel(after, tables, stream, gain, normed, own, held, gains, sems):
    at = place()
    copies = [
        pltpu.make_async_copy(stream, held, sems.at[0]),
        pltpu.make_async_copy(gain, gains, sems.at[1]),
    ]
    for copy in copies:
        copy.start()
    for copy in copies:
        copy.wait()
    x = held[...].astype(F32)
    scale = lax.rsqrt(jnp.mean(x * x, axis=-1, keepdims=True) + 1e-05)
    for g in range(GROUPS):
        cols = pl.ds(g * RUN, RUN)
        normed[g] = (held[:, cols].astype(F32) * scale * gains[:, cols]).astype(BF)
    rows = pl.ds(pl.multiple_of(at[0] * 128 + at[1] * HALF, HALF), HALF)
    own[...] = held[rows, pl.ds(pl.multiple_of(at[2] * BAND, BAND), BAND)]


def norm(after, tables, stream, gain):
    return pl.pallas_call(
        norm_kernel,
        out_shape=(jax.ShapeDtypeStruct((GROUPS, 256, RUN), BF), jax.ShapeDtypeStruct((HALF, BAND), BF)),
        in_specs=[ANY, ANY, HBM, HBM],
        out_specs=(VMEM,) * 2,
        scratch_shapes=[pltpu.VMEM((256, D), BF), pltpu.VMEM((1, D), F32), pltpu.SemaphoreType.DMA((2,))],
        compiler_params=params(24),
        name="norm",
    )(after, tables, stream, gain)


def join_kernel(after, gate, up, narrow, out, token, held, sems):
    token[...] = jnp.zeros_like(token)
    copies = [
        pltpu.make_async_copy(part, held.at[pl.ds(i * FC, FC), :], sems.at[i])
        for i, part in enumerate((gate, up, narrow))
    ]
    for copy in copies:
        copy.start()
    for copy in copies:
        copy.wait()
    whole_copy = pltpu.make_async_copy(held, out, sems.at[3])
    whole_copy.start()
    whole_copy.wait()


def join(after, *parts):
    return pl.pallas_call(
        join_kernel,
        out_shape=(jax.ShapeDtypeStruct((3 * FC, RUN), BF), jax.ShapeDtypeStruct((8, 128), F32)),
        in_specs=[ANY, HBM, HBM, HBM],
        out_specs=(HBM, VMEM),
        scratch_shapes=[pltpu.VMEM((3 * FC, RUN), BF), pltpu.SemaphoreType.DMA((4,))],
        compiler_params=params(60),
        name="join",
    )(after, *parts)


def pack(*parts):
    return pl.pallas_call(
        pack_kernel,
        out_shape=(jax.ShapeDtypeStruct((GROUPS, 160, RUN), BF), jax.ShapeDtypeStruct((8, 128), F32)),
        in_specs=[HBM] * 4,
        out_specs=(HBM, VMEM),
        scratch_shapes=[pltpu.VMEM((160, RUN), BF), pltpu.SemaphoreType.DMA((4 + GROUPS,))],
        compiler_params=params(60),
        name="pack",
    )(*parts)


def project(normed, weights, cos, sin):
    return pl.pallas_call(
        project_kernel,
        out_shape=(
            jax.ShapeDtypeStruct((8, HALF, 128), BF),
            jax.ShapeDtypeStruct((KC, 256), BF),
            jax.ShapeDtypeStruct((KC, 256), BF),
        ),
        in_specs=[HBM] * 4,
        out_specs=(VMEM,) * 3,
        scratch_shapes=[
            pltpu.VMEM((GROUPS, 256, RUN), BF),
            pltpu.VMEM((GROUPS, 96, RUN), BF),
            pltpu.VMEM((2, 256, 128), F32),
            pltpu.SemaphoreType.DMA((2 * GROUPS + 2,)),
        ],
        compiler_params=params(58),
        name="project",
    )(normed, weights, cos, sin)


def attend(lengths, got):
    return pl.pallas_call(
        attend_kernel,
        out_shape=jax.ShapeDtypeStruct((HALF, BAND), BF),
        in_specs=[SMEM, VMEM],
        out_specs=VMEM,
        compiler_params=params(16),
        name="attend",
    )(lengths, got)


def output(got, weights, own):
    return pl.pallas_call(
        output_kernel,
        out_shape=jax.ShapeDtypeStruct((8, HALF, BAND), BF),
        in_specs=[VMEM] * 6,
        out_specs=VMEM,
        compiler_params=params(24),
        name="output",
    )(got, *weights, own)


def near_half(same, other, gain):
    return pl.pallas_call(
        near_kernel,
        out_shape=jax.ShapeDtypeStruct((GROUPS, HALF, RUN), BF),
        in_specs=[VMEM] * 3,
        out_specs=VMEM,
        compiler_params=params(16),
        name="near_half",
    )(same, other, gain)


def own_rows(near, same, far_same, far_other, gain, mine, core):
    return pl.pallas_call(
        own_rows_kernel,
        out_shape=(
            jax.ShapeDtypeStruct((4, 128, FC), F32),
            jax.ShapeDtypeStruct((128, 128), BF),
            jax.ShapeDtypeStruct((GROUPS, HALF, RUN), BF),
        ),
        in_specs=[VMEM] * 7,
        out_specs=(VMEM,) * 3,
        compiler_params=params(16),
        cost_estimate=cost(2 * HALF * D * 4 * FC, 4 * 2**20),
        name="own_rows",
    )(near, same, far_same, far_other, gain, mine, core)


def down(near, far, before, weights):
    part = jax.ShapeDtypeStruct((8, 128, 128), BF)
    return pl.pallas_call(
        down_kernel,
        out_shape=(jax.ShapeDtypeStruct((8, 128, 128), F32), part, part, part),
        in_specs=[VMEM] * 7,
        out_specs=(VMEM,) * 4,
        compiler_params=params(16),
        cost_estimate=cost(4 * HALF * D * 4 * FC, 9 * 2**20),
        name="down",
    )(near, far, before, *weights)


def add(*parts):
    return pl.pallas_call(
        add_kernel,
        out_shape=jax.ShapeDtypeStruct((8, 128, 128), BF),
        in_specs=[VMEM] * 4,
        out_specs=VMEM,
        compiler_params=params(16),
        name="add",
    )(*parts)


def finish(got, kept):
    return pl.pallas_call(
        finish_kernel,
        out_shape=(jax.ShapeDtypeStruct((QC, 128), BF),) * 2,
        in_specs=[VMEM] * 2,
        out_specs=(VMEM, VMEM),
        compiler_params=params(16),
        name="finish",
    )(got, kept)


def swap(x, bits):
    return lax.ppermute(x, "dev", [(d, d ^ bits) for d in range(MEMBERS)])


def swap_groups(x):
    return lax.ppermute(x, "grp", [(g, g ^ 4) for g in range(GROUPS)])


def collect_x(x):
    return lax.all_gather(x, "grp", axis=0, axis_index_groups=[[0, 1, 2, 3], [4, 5, 6, 7]])


def trade(x, groups):
    return lax.all_to_all(x, "dev", 0, 0, axis_index_groups=groups, tiled=True)


def collect(x):
    return lax.all_gather(x, "dev", axis=0, axis_index_groups=COLUMNS)


def after(x, other):
    return lax.optimization_barrier((x, other))[0]


def on_device(
    stream,
    row_length,
    row_start,
    attn_gain,
    w_query,
    w_key,
    w_value,
    w_out,
    ffn_gain,
    w_gate,
    w_up,
    w_down,
):
    member = lax.axis_index("dev")
    core = member % 2

    packed, token = pack(w_query.T, w_key.T, w_value.T, w_out.T)
    first = lax.all_to_all(packed, "grp", 0, 0, tiled=True)

    lane = jnp.arange(128, dtype=jnp.int32)
    column = jnp.where(lane < QC, member * QC + lane, member * KC + lane - QC)
    pair = (column % HEAD_DIM // 2).astype(F32)
    freq = jnp.exp(-(2.0 * pair / HEAD_DIM) * math.log(ROPE_BASE))
    positions = (row_start[:, None] + jnp.arange(ROW_LEN, dtype=jnp.int32)[None, :]).reshape(-1)
    angle = positions.astype(F32)[:, None] * freq[None, :]
    cos, sin = jnp.cos(angle), jnp.sin(angle)

    mine, token = join(token, w_gate.T, w_up.T, w_down.T)
    normed, own = norm(token, cos, stream, attn_gain.reshape(1, D))
    send, keys, values = project(normed, first, cos, sin)
    got = trade(send, OCTETS)
    mine = after(mine, send)
    mine_lo = swap_groups(after(mine, got))
    out_own = first[:, 96:160, :]
    out_weights = (out_own, swap(out_own, 1), swap(out_own, 2), swap(out_own, 3))
    mixed = collect(attend(row_length, got))
    attended = output(mixed, out_weights, own)
    mine, mine_lo = collect_x(mine), collect_x(after(mine_lo, attended))
    mine = after(mine, attended)
    core_mine = swap(mine, 1)
    same = trade(attended, PARITIES)
    other, far_same, far_other = swap(same, 4), swap(same, 2), swap(same, 6)
    gain = ffn_gain.reshape(1, D)
    near = near_half(same, other, gain)
    mine_lo = after(mine_lo, (far_same, far_other, near))
    core_lo = swap(mine_lo, 1)
    totals, kept, far_normed = own_rows(near, same, far_same, far_other, gain, mine, core_mine)
    weights = (mine, mine_lo, core_mine, core_lo)
    keep, to_y, to_z, to_both = down(near, far_normed, totals, weights)
    sums = trade(add(keep, swap(to_y, 2), swap(to_z, 4), swap(to_both, 6)), PARITIES)
    keep, give = finish(sums, kept)
    give = swap(give, 1)
    rows = jnp.where(core == 0, jnp.concatenate([keep, give], axis=1), jnp.concatenate([give, keep], axis=1))
    return (keys.T, values.T, rows.T)


def solution(mesh):
    placed = (
        P("grp", None),
        P("grp"),
        P("grp"),
        P(),
        P("grp", "dev"),
        P("grp", "dev"),
        P("grp", "dev"),
        P("grp", "dev"),
        P(),
        P("grp", "dev"),
        P("grp", "dev"),
        P("grp", "dev"),
    )
    return jax.shard_map(
        on_device,
        mesh=mesh,
        in_specs=placed,
        out_specs=(P("grp", "dev"), P("grp", "dev"), P("grp", "dev")),
        check_vma=False,
    )
```

```python
import math

import jax
import jax.numpy as jnp
from jax import lax
from jax.experimental import pallas as pl
from jax.experimental.pallas import tpu as pltpu
from jax.sharding import PartitionSpec as P

HEADS = 32
KV_HEADS = 8
HEAD_DIM = 128
ROW_LEN = 128
D = 4096
ROPE_BASE = 500000.0

GROUPS = 8
MEMBERS = 64
DEPTH = 16
HALF = 64
QC = 64
KC = 16
FC = 224
BAND = 256
RUN = 512

COLUMNS = [[4 * z + q for z in range(DEPTH)] for q in range(4)]
PARITIES = [[4 * (2 * i + p) + q for i in range(8)] for p in range(2) for q in range(4)]
OCTETS = [[8 * z + m for m in range(8)] for z in range(8)]

BF = jnp.bfloat16
F32 = jnp.float32
VMEM = pl.BlockSpec(memory_space=pltpu.VMEM)
HBM = pl.BlockSpec(memory_space=pltpu.HBM)
ANY = pl.BlockSpec(memory_space=pl.ANY)
SMEM = pl.BlockSpec(memory_space=pltpu.SMEM)


def place():
    d = lax.axis_index("dev")
    return (d % 2, d // 2 % 2, d // 4, d // 4 % 2, d // 8, d % 4, lax.axis_index("grp") // 4)


def nt(a, b):
    return lax.dot_general(a, b, (((1,), (1,)), ((), ())), preferred_element_type=F32)


def whole(*shape):
    return pl.BlockSpec(shape, lambda i: (0,) * len(shape))


def params(mib):
    return pltpu.CompilerParams(vmem_limit_bytes=mib * 2**20)


def cost(flops, nbytes):
    return pl.CostEstimate(flops=flops, bytes_accessed=nbytes, transcendentals=0)


def project_kernel(normed, weights, cos, sin, send, keys, values, out_own, rows, cols, tables, sems):
    copies = []
    for g in range(GROUPS):
        copies.append(pltpu.make_async_copy(normed.at[g], rows.at[g], sems.at[2 * g]))
        copies.append(pltpu.make_async_copy(weights.at[g, pl.ds(0, 96), :], cols.at[g], sems.at[2 * g + 1]))
    for i, ref in enumerate((cos, sin)):
        copies.append(pltpu.make_async_copy(ref, tables.at[i], sems.at[2 * GROUPS + i]))
    for g in range(GROUPS):
        source = weights.at[g, pl.ds(96, QC), :]
        copies.append(pltpu.make_async_copy(source, out_own.at[g], sems.at[2 * GROUPS + 2 + g]))
    for copy in copies:
        copy.start()
    total = jnp.zeros((256, 96), F32)
    for g in range(GROUPS):
        copies[2 * g].wait()
        copies[2 * g + 1].wait()
        total = total + nt(rows[g], cols[g])
    total = jnp.concatenate([total, jnp.zeros((256, 32), F32)], axis=1)
    lane = lax.broadcasted_iota(jnp.int32, (256, 128), 1)
    partner = jnp.where(lane % 2 == 0, -pltpu.roll(total, 127, 1), pltpu.roll(total, 1, 1))
    for copy in copies[2 * GROUPS :]:
        copy.wait()
    turned = jnp.where(lane < QC + KC, total * tables[0] + partner * tables[1], total)
    turned = turned.astype(BF).astype(F32)
    flipped = turned.T
    keys[...] = flipped[QC : QC + KC, :].astype(BF)
    values[...] = flipped[QC + KC : QC + 2 * KC, :].astype(BF)
    lane = lax.broadcasted_iota(jnp.int32, (HALF, 128), 1)
    for zl in range(2):
        for yhi in range(2):
            for c in range(2):
                first = turned[c * 128 : c * 128 + HALF, :]
                second = turned[c * 128 + HALF : c * 128 + 128, :]
                mine = second if yhi else first
                chunk = jnp.where(lane < QC, mine, jnp.where(lane < 96, first, pltpu.roll(second, 32, 1)))
                send[zl * 4 + yhi * 2 + c] = chunk.astype(BF)


def attend_kernel(lengths, got, out):
    at = place()
    lane = lax.broadcasted_iota(jnp.int32, (HALF, 128), 1)
    pieces = [got[m].astype(F32) for m in range(8)]

    def gather(start):
        full = jnp.zeros((HALF, 128), F32)
        for m in range(8):
            full = jnp.where(lane // KC == m, pltpu.roll(pieces[m], (KC * m - start) % 128, 1), full)
        return full.astype(BF)

    keys = jnp.concatenate([gather(QC), gather(96)], axis=0)
    values = jnp.concatenate([gather(QC + KC), gather(96 + KC)], axis=0)
    slot = lax.broadcasted_iota(jnp.int32, (HALF, 128), 0) + at[1] * HALF
    allowed = (lane <= slot) & (lane < lengths[at[0]])
    for a in range(2):
        low = got[at[3] * 4 + a * 2].astype(F32)
        high = got[at[3] * 4 + a * 2 + 1].astype(F32)
        queries = jnp.where(lane < QC, low, pltpu.roll(high, QC, 1)).astype(BF)
        scores = nt(queries, keys) / math.sqrt(HEAD_DIM)
        scores = jnp.where(allowed, scores, -jnp.inf)
        expo = jnp.exp(scores - jnp.max(scores, axis=-1, keepdims=True))
        probs = (expo / jnp.sum(expo, axis=-1, keepdims=True)).astype(BF)
        mixed = jnp.dot(probs, values, preferred_element_type=F32).astype(BF)
        out[:, a * 128 : a * 128 + 128] = mixed


def output_kernel(got, mine, core, far, cross, own, out):
    at = place()
    parts = []
    for w in (mine, core, far, cross):
        total = jnp.zeros((HALF, QC), F32)
        for g in range(GROUPS):
            total = total + nt(got[2 * g], w[g, :, 0:BAND]) + nt(got[2 * g + 1], w[g, :, BAND:RUN])
        parts.append(total)
    blocks = []
    for j in range(4):
        picked = parts[0]
        for k in range(1, 4):
            picked = jnp.where(jnp.bitwise_xor(at[5], j) == k, parts[k], picked)
        blocks.append(picked)
    projected = jnp.concatenate(blocks, axis=1)
    attended = (own[...].astype(F32) + projected).astype(BF)
    for i in range(8):
        out[i] = attended


def renorm(at, same, other, gain, out):
    low = at[3] == 0
    squares = jnp.zeros((HALF, 1), F32)
    for got in (same, other):
        for i in range(8):
            x = got[i].astype(F32)
            squares = squares + jnp.sum(x * x, axis=-1, keepdims=True)
    scale = lax.rsqrt(squares * (1.0 / D) + 1e-05)
    for i in range(8):
        one, two = same[i].astype(F32), other[i].astype(F32)
        for k, x in enumerate((jnp.where(low, one, two), jnp.where(low, two, one))):
            z = 2 * i + k
            out[i, :, k * BAND : (k + 1) * BAND] = (x * scale * gain[:, z * BAND : (z + 1) * BAND]).astype(BF)


def near_kernel(same, other, gain, out):
    at = place()
    renorm(at, same, other, gain, out)


def multiply(at, near, far, pair, side, totals):
    for x in range(4):
        g = jnp.bitwise_xor(at[6], side) * 4 + x
        rows = jnp.concatenate([near[g], far[g]], axis=0)
        for i, w in enumerate(pair):
            totals[2 * i] = totals[2 * i] + nt(rows, w[x, 0:FC, :])
            totals[2 * i + 1] = totals[2 * i + 1] + nt(rows, w[x, FC : 2 * FC, :])


def own_rows_kernel(near, same, far_same, far_other, gain, mine, core, out, kept, normed):
    at = place()
    low = at[1] == 0
    lanes = pl.ds(pl.multiple_of(at[1] * 128, 128), 128)
    near_kept, far_kept = same[at[4], :, lanes], far_same[at[4], :, lanes]
    kept[0:HALF, :] = jnp.where(low, near_kept, far_kept)
    kept[HALF : 2 * HALF, :] = jnp.where(low, far_kept, near_kept)
    renorm(at, far_same, far_other, gain, normed)
    totals = [jnp.zeros((2 * HALF, FC), F32) for _ in range(4)]
    multiply(at, near, normed, (mine, core), 0, totals)
    for i in range(4):
        out[i] = totals[i]


def down_kernel(near, far, before, mine, mine_lo, core, core_lo, keep, to_y, to_z, to_both):
    at = place()
    low_y, low_z = at[1] == 0, at[3] == 0
    totals = [before[i] for i in range(4)]
    multiply(at, near, far, (mine_lo, core_lo), 1, totals)
    units = []
    for i in range(2):
        gate = totals[2 * i]
        part = (gate / (1.0 + jnp.exp(-gate)) * totals[2 * i + 1]).astype(BF)
        first, second = part[0:HALF, :], part[HALF : 2 * HALF, :]
        units.append(jnp.concatenate([jnp.where(low_y, first, second), jnp.where(low_y, second, first)], axis=0))
    for x in range(4):
        for side, pair in enumerate(((mine, core), (mine_lo, core_lo))):
            total = jnp.zeros((128, RUN), F32)
            for i, w in enumerate(pair):
                total = total + jnp.dot(units[i], w[x, 2 * FC : 3 * FC, :], preferred_element_type=F32)
            g = jnp.bitwise_xor(at[6], side) * 4 + x
            blocks = [total[:, k * 128 : (k + 1) * 128] for k in range(4)]
            same = [jnp.where(low_z, blocks[k], blocks[2 + k]) for k in range(2)]
            other = [jnp.where(low_z, blocks[2 + k], blocks[k]) for k in range(2)]
            keep[g] = jnp.where(low_y, same[0], same[1])
            to_y[g] = jnp.where(low_y, same[1], same[0]).astype(BF)
            to_z[g] = jnp.where(low_y, other[0], other[1]).astype(BF)
            to_both[g] = jnp.where(low_y, other[1], other[0]).astype(BF)


def add_kernel(keep, *refs):
    out = refs[-1]
    for i in range(8):
        total = keep[i]
        for got in refs[:-1]:
            total = total + got[i].astype(F32)
        out[i] = total.astype(BF)


def finish_kernel(got, kept, keep, give):
    at = place()
    total = kept[...].astype(F32)
    for i in range(8):
        total = total + got[i].astype(F32)
    result = total.T
    head, tail = result[0:QC, :], result[QC : 2 * QC, :]
    keep[...] = jnp.where(at[0] == 0, head, tail).astype(BF)
    give[...] = jnp.where(at[0] == 0, tail, head).astype(BF)


def pack_kernel(query, key, value, out_part, out, token, held, sems):
    token[...] = jnp.zeros_like(token)
    spans = ((query, 0, QC), (key, QC, KC), (value, QC + KC, KC), (out_part, 96, QC))
    reads = [
        pltpu.make_async_copy(ref, held.at[pl.ds(start, rows), :], sems.at[i])
        for i, (ref, start, rows) in enumerate(spans)
    ]
    for copy in reads:
        copy.start()
    for copy in reads:
        copy.wait()
    writes = [pltpu.make_async_copy(held, out.at[g], sems.at[4 + g]) for g in range(GROUPS)]
    for copy in writes:
        copy.start()
    for copy in writes:
        copy.wait()


def norm_kernel(after, tables, stream, gain, normed, own, held, gains, sems):
    at = place()
    copies = [
        pltpu.make_async_copy(stream, held, sems.at[0]),
        pltpu.make_async_copy(gain, gains, sems.at[1]),
    ]
    for copy in copies:
        copy.start()
    for copy in copies:
        copy.wait()
    x = held[...].astype(F32)
    scale = lax.rsqrt(jnp.mean(x * x, axis=-1, keepdims=True) + 1e-05)
    for g in range(GROUPS):
        cols = pl.ds(g * RUN, RUN)
        normed[g] = (held[:, cols].astype(F32) * scale * gains[:, cols]).astype(BF)
    rows = pl.ds(pl.multiple_of(at[0] * 128 + at[1] * HALF, HALF), HALF)
    own[...] = held[rows, pl.ds(pl.multiple_of(at[2] * BAND, BAND), BAND)]


def norm(after, tables, stream, gain):
    return pl.pallas_call(
        norm_kernel,
        out_shape=(jax.ShapeDtypeStruct((GROUPS, 256, RUN), BF), jax.ShapeDtypeStruct((HALF, BAND), BF)),
        in_specs=[ANY, ANY, HBM, HBM],
        out_specs=(VMEM,) * 2,
        scratch_shapes=[pltpu.VMEM((256, D), BF), pltpu.VMEM((1, D), F32), pltpu.SemaphoreType.DMA((2,))],
        compiler_params=params(24),
        name="norm",
    )(after, tables, stream, gain)


def join_kernel(after, gate, up, narrow, out, token, held, sems):
    token[...] = jnp.zeros_like(token)
    copies = [
        pltpu.make_async_copy(part, held.at[pl.ds(i * FC, FC), :], sems.at[i])
        for i, part in enumerate((gate, up, narrow))
    ]
    for copy in copies:
        copy.start()
    for copy in copies:
        copy.wait()
    whole_copy = pltpu.make_async_copy(held, out, sems.at[3])
    whole_copy.start()
    whole_copy.wait()


def join(after, *parts):
    return pl.pallas_call(
        join_kernel,
        out_shape=(jax.ShapeDtypeStruct((3 * FC, RUN), BF), jax.ShapeDtypeStruct((8, 128), F32)),
        in_specs=[ANY, HBM, HBM, HBM],
        out_specs=(HBM, VMEM),
        scratch_shapes=[pltpu.VMEM((3 * FC, RUN), BF), pltpu.SemaphoreType.DMA((4,))],
        compiler_params=params(60),
        name="join",
    )(after, *parts)


def pack(*parts):
    return pl.pallas_call(
        pack_kernel,
        out_shape=(jax.ShapeDtypeStruct((GROUPS, 160, RUN), BF), jax.ShapeDtypeStruct((8, 128), F32)),
        in_specs=[HBM] * 4,
        out_specs=(HBM, VMEM),
        scratch_shapes=[pltpu.VMEM((160, RUN), BF), pltpu.SemaphoreType.DMA((4 + GROUPS,))],
        compiler_params=params(60),
        name="pack",
    )(*parts)


def project(normed, weights, cos, sin):
    return pl.pallas_call(
        project_kernel,
        out_shape=(
            jax.ShapeDtypeStruct((8, HALF, 128), BF),
            jax.ShapeDtypeStruct((KC, 256), BF),
            jax.ShapeDtypeStruct((KC, 256), BF),
            jax.ShapeDtypeStruct((GROUPS, QC, RUN), BF),
        ),
        in_specs=[HBM] * 4,
        out_specs=(VMEM,) * 4,
        scratch_shapes=[
            pltpu.VMEM((GROUPS, 256, RUN), BF),
            pltpu.VMEM((GROUPS, 96, RUN), BF),
            pltpu.VMEM((2, 256, 128), F32),
            pltpu.SemaphoreType.DMA((3 * GROUPS + 2,)),
        ],
        compiler_params=params(58),
        name="project",
    )(normed, weights, cos, sin)


def attend(lengths, got):
    return pl.pallas_call(
        attend_kernel,
        out_shape=jax.ShapeDtypeStruct((HALF, BAND), BF),
        in_specs=[SMEM, VMEM],
        out_specs=VMEM,
        compiler_params=params(16),
        name="attend",
    )(lengths, got)


def output(got, weights, own):
    return pl.pallas_call(
        output_kernel,
        out_shape=jax.ShapeDtypeStruct((8, HALF, BAND), BF),
        in_specs=[VMEM] * 6,
        out_specs=VMEM,
        compiler_params=params(24),
        name="output",
    )(got, *weights, own)


def near_half(same, other, gain):
    return pl.pallas_call(
        near_kernel,
        out_shape=jax.ShapeDtypeStruct((GROUPS, HALF, RUN), BF),
        in_specs=[VMEM] * 3,
        out_specs=VMEM,
        compiler_params=params(16),
        name="near_half",
    )(same, other, gain)


def own_rows(near, same, far_same, far_other, gain, mine, core):
    return pl.pallas_call(
        own_rows_kernel,
        out_shape=(
            jax.ShapeDtypeStruct((4, 128, FC), F32),
            jax.ShapeDtypeStruct((128, 128), BF),
            jax.ShapeDtypeStruct((GROUPS, HALF, RUN), BF),
        ),
        in_specs=[VMEM] * 7,
        out_specs=(VMEM,) * 3,
        compiler_params=params(16),
        cost_estimate=cost(2 * HALF * D * 4 * FC, 4 * 2**20),
        name="own_rows",
    )(near, same, far_same, far_other, gain, mine, core)


def down(near, far, before, weights):
    part = jax.ShapeDtypeStruct((8, 128, 128), BF)
    return pl.pallas_call(
        down_kernel,
        out_shape=(jax.ShapeDtypeStruct((8, 128, 128), F32), part, part, part),
        in_specs=[VMEM] * 7,
        out_specs=(VMEM,) * 4,
        compiler_params=params(16),
        cost_estimate=cost(4 * HALF * D * 4 * FC, 9 * 2**20),
        name="down",
    )(near, far, before, *weights)


def add(*parts):
    return pl.pallas_call(
        add_kernel,
        out_shape=jax.ShapeDtypeStruct((8, 128, 128), BF),
        in_specs=[VMEM] * 4,
        out_specs=VMEM,
        compiler_params=params(16),
        name="add",
    )(*parts)


def finish(got, kept):
    return pl.pallas_call(
        finish_kernel,
        out_shape=(jax.ShapeDtypeStruct((QC, 128), BF),) * 2,
        in_specs=[VMEM] * 2,
        out_specs=(VMEM, VMEM),
        compiler_params=params(16),
        name="finish",
    )(got, kept)


def swap(x, bits):
    return lax.ppermute(x, "dev", [(d, d ^ bits) for d in range(MEMBERS)])


def swap_groups(x):
    return lax.ppermute(x, "grp", [(g, g ^ 4) for g in range(GROUPS)])


def collect_x(x):
    return lax.all_gather(x, "grp", axis=0, axis_index_groups=[[0, 1, 2, 3], [4, 5, 6, 7]])


def trade(x, groups):
    return lax.all_to_all(x, "dev", 0, 0, axis_index_groups=groups, tiled=True)


def collect(x):
    return lax.all_gather(x, "dev", axis=0, axis_index_groups=COLUMNS)


def after(x, other):
    return lax.optimization_barrier((x, other))[0]


def on_device(
    stream,
    row_length,
    row_start,
    attn_gain,
    w_query,
    w_key,
    w_value,
    w_out,
    ffn_gain,
    w_gate,
    w_up,
    w_down,
):
    member = lax.axis_index("dev")
    core = member % 2

    packed, token = pack(w_query.T, w_key.T, w_value.T, w_out.T)
    first = lax.all_to_all(packed, "grp", 0, 0, tiled=True)

    lane = jnp.arange(128, dtype=jnp.int32)
    column = jnp.where(lane < QC, member * QC + lane, member * KC + lane - QC)
    pair = (column % HEAD_DIM // 2).astype(F32)
    freq = jnp.exp(-(2.0 * pair / HEAD_DIM) * math.log(ROPE_BASE))
    positions = (row_start[:, None] + jnp.arange(ROW_LEN, dtype=jnp.int32)[None, :]).reshape(-1)
    angle = positions.astype(F32)[:, None] * freq[None, :]
    cos, sin = jnp.cos(angle), jnp.sin(angle)

    mine, token = join(token, w_gate.T, w_up.T, w_down.T)
    normed, own = norm(token, cos, stream, attn_gain.reshape(1, D))
    send, keys, values, out_own = project(normed, first, cos, sin)
    got = trade(send, OCTETS)
    mine = after(mine, send)
    mine_lo = swap_groups(after(mine, got))
    out_weights = (out_own, swap(out_own, 1), swap(out_own, 2), swap(out_own, 3))
    mixed = collect(attend(row_length, got))
    attended = output(mixed, out_weights, own)
    mine, mine_lo = collect_x(mine), collect_x(after(mine_lo, attended))
    mine = after(mine, attended)
    core_mine = swap(mine, 1)
    same = trade(attended, PARITIES)
    other, far_same, far_other = swap(same, 4), swap(same, 2), swap(same, 6)
    gain = ffn_gain.reshape(1, D)
    near = near_half(same, other, gain)
    mine_lo = after(mine_lo, (far_same, far_other, other))
    core_lo = swap(mine_lo, 1)
    totals, kept, far_normed = own_rows(near, same, far_same, far_other, gain, mine, core_mine)
    weights = (mine, mine_lo, core_mine, core_lo)
    keep, to_y, to_z, to_both = down(near, far_normed, totals, weights)
    sums = trade(add(keep, swap(to_y, 2), swap(to_z, 4), swap(to_both, 6)), PARITIES)
    keep, give = finish(sums, kept)
    give = swap(give, 1)
    rows = jnp.where(core == 0, jnp.concatenate([keep, give], axis=1), jnp.concatenate([give, keep], axis=1))
    return (keys.T, values.T, rows.T)


def solution(mesh):
    placed = (
        P("grp", None),
        P("grp"),
        P("grp"),
        P(),
        P("grp", "dev"),
        P("grp", "dev"),
        P("grp", "dev"),
        P("grp", "dev"),
        P(),
        P("grp", "dev"),
        P("grp", "dev"),
        P("grp", "dev"),
    )
    return jax.shard_map(
        on_device,
        mesh=mesh,
        in_specs=placed,
        out_specs=(P("grp", "dev"), P("grp", "dev"), P("grp", "dev")),
        check_vma=False,
    )
```

```python
import math

import jax
import jax.numpy as jnp
from jax import lax
from jax.experimental import pallas as pl
from jax.experimental.pallas import tpu as pltpu
from jax.sharding import PartitionSpec as P

HEADS = 32
KV_HEADS = 8
HEAD_DIM = 128
ROW_LEN = 128
D = 4096
ROPE_BASE = 500000.0

GROUPS = 8
MEMBERS = 64
DEPTH = 16
HALF = 64
QC = 64
KC = 16
FC = 224
BAND = 256
RUN = 512

COLUMNS = [[4 * z + q for z in range(DEPTH)] for q in range(4)]
PARITIES = [[4 * (2 * i + p) + q for i in range(8)] for p in range(2) for q in range(4)]
OCTETS = [[8 * z + m for m in range(8)] for z in range(8)]

BF = jnp.bfloat16
F32 = jnp.float32
VMEM = pl.BlockSpec(memory_space=pltpu.VMEM)
HBM = pl.BlockSpec(memory_space=pltpu.HBM)
ANY = pl.BlockSpec(memory_space=pl.ANY)
SMEM = pl.BlockSpec(memory_space=pltpu.SMEM)


def place():
    d = lax.axis_index("dev")
    return (d % 2, d // 2 % 2, d // 4, d // 4 % 2, d // 8, d % 4, lax.axis_index("grp") // 4)


def nt(a, b):
    return lax.dot_general(a, b, (((1,), (1,)), ((), ())), preferred_element_type=F32)


def whole(*shape):
    return pl.BlockSpec(shape, lambda i: (0,) * len(shape))


def params(mib):
    return pltpu.CompilerParams(vmem_limit_bytes=mib * 2**20)


def cost(flops, nbytes):
    return pl.CostEstimate(flops=flops, bytes_accessed=nbytes, transcendentals=0)


def project_kernel(normed, weights, cos, sin, send, keys, values, out_own, rows, cols, tables, sems):
    copies = []
    for g in range(GROUPS):
        copies.append(pltpu.make_async_copy(normed.at[g], rows.at[g], sems.at[2 * g]))
        copies.append(pltpu.make_async_copy(weights.at[g, pl.ds(0, 96), :], cols.at[g], sems.at[2 * g + 1]))
    for i, ref in enumerate((cos, sin)):
        copies.append(pltpu.make_async_copy(ref, tables.at[i], sems.at[2 * GROUPS + i]))
    for g in range(GROUPS):
        source = weights.at[g, pl.ds(96, QC), :]
        copies.append(pltpu.make_async_copy(source, out_own.at[g], sems.at[2 * GROUPS + 2 + g]))
    for copy in copies:
        copy.start()
    total = jnp.zeros((256, 96), F32)
    for g in range(GROUPS):
        copies[2 * g].wait()
        copies[2 * g + 1].wait()
        total = total + nt(rows[g], cols[g])
    total = jnp.concatenate([total, jnp.zeros((256, 32), F32)], axis=1)
    lane = lax.broadcasted_iota(jnp.int32, (256, 128), 1)
    partner = jnp.where(lane % 2 == 0, -pltpu.roll(total, 127, 1), pltpu.roll(total, 1, 1))
    for copy in copies[2 * GROUPS :]:
        copy.wait()
    turned = jnp.where(lane < QC + KC, total * tables[0] + partner * tables[1], total)
    turned = turned.astype(BF).astype(F32)
    flipped = turned.T
    keys[...] = flipped[QC : QC + KC, :].astype(BF)
    values[...] = flipped[QC + KC : QC + 2 * KC, :].astype(BF)
    lane = lax.broadcasted_iota(jnp.int32, (HALF, 128), 1)
    for zl in range(2):
        for yhi in range(2):
            for c in range(2):
                first = turned[c * 128 : c * 128 + HALF, :]
                second = turned[c * 128 + HALF : c * 128 + 128, :]
                mine = second if yhi else first
                chunk = jnp.where(lane < QC, mine, jnp.where(lane < 96, first, pltpu.roll(second, 32, 1)))
                send[zl * 4 + yhi * 2 + c] = chunk.astype(BF)


def attend_kernel(lengths, got, out):
    at = place()
    lane = lax.broadcasted_iota(jnp.int32, (HALF, 128), 1)
    pieces = [got[m].astype(F32) for m in range(8)]

    def gather(start):
        full = jnp.zeros((HALF, 128), F32)
        for m in range(8):
            full = jnp.where(lane // KC == m, pltpu.roll(pieces[m], (KC * m - start) % 128, 1), full)
        return full.astype(BF)

    keys = jnp.concatenate([gather(QC), gather(96)], axis=0)
    values = jnp.concatenate([gather(QC + KC), gather(96 + KC)], axis=0)
    slot = lax.broadcasted_iota(jnp.int32, (HALF, 128), 0) + at[1] * HALF
    allowed = (lane <= slot) & (lane < lengths[at[0]])
    for a in range(2):
        low = got[at[3] * 4 + a * 2].astype(F32)
        high = got[at[3] * 4 + a * 2 + 1].astype(F32)
        queries = jnp.where(lane < QC, low, pltpu.roll(high, QC, 1)).astype(BF)
        scores = nt(queries, keys) / math.sqrt(HEAD_DIM)
        scores = jnp.where(allowed, scores, -jnp.inf)
        expo = jnp.exp(scores - jnp.max(scores, axis=-1, keepdims=True))
        probs = (expo / jnp.sum(expo, axis=-1, keepdims=True)).astype(BF)
        mixed = jnp.dot(probs, values, preferred_element_type=F32).astype(BF)
        out[:, a * 128 : a * 128 + 128] = mixed


def output_kernel(got, mine, core, far, cross, own, out):
    at = place()
    parts = []
    for w in (mine, core, far, cross):
        total = jnp.zeros((HALF, QC), F32)
        for g in range(GROUPS):
            total = total + nt(got[2 * g], w[g, :, 0:BAND]) + nt(got[2 * g + 1], w[g, :, BAND:RUN])
        parts.append(total)
    blocks = []
    for j in range(4):
        picked = parts[0]
        for k in range(1, 4):
            picked = jnp.where(jnp.bitwise_xor(at[5], j) == k, parts[k], picked)
        blocks.append(picked)
    projected = jnp.concatenate(blocks, axis=1)
    attended = (own[...].astype(F32) + projected).astype(BF)
    for i in range(8):
        out[i] = attended


def renorm(at, same, other, gain, out):
    low = at[3] == 0
    squares = jnp.zeros((HALF, 1), F32)
    for got in (same, other):
        for i in range(8):
            x = got[i].astype(F32)
            squares = squares + jnp.sum(x * x, axis=-1, keepdims=True)
    scale = lax.rsqrt(squares * (1.0 / D) + 1e-05)
    for i in range(8):
        one, two = same[i].astype(F32), other[i].astype(F32)
        for k, x in enumerate((jnp.where(low, one, two), jnp.where(low, two, one))):
            z = 2 * i + k
            out[i, :, k * BAND : (k + 1) * BAND] = (x * scale * gain[:, z * BAND : (z + 1) * BAND]).astype(BF)


def near_kernel(same, other, gain, out):
    at = place()
    renorm(at, same, other, gain, out)


def multiply(at, near, far, pair, side, totals):
    for x in range(4):
        g = jnp.bitwise_xor(at[6], side) * 4 + x
        rows = jnp.concatenate([near[g], far[g]], axis=0)
        for i, w in enumerate(pair):
            totals[2 * i] = totals[2 * i] + nt(rows, w[x, 0:FC, :])
            totals[2 * i + 1] = totals[2 * i + 1] + nt(rows, w[x, FC : 2 * FC, :])


def own_rows_kernel(near, same, far_same, far_other, gain, mine, core, out, kept, normed):
    at = place()
    low = at[1] == 0
    lanes = pl.ds(pl.multiple_of(at[1] * 128, 128), 128)
    near_kept, far_kept = same[at[4], :, lanes], far_same[at[4], :, lanes]
    kept[0:HALF, :] = jnp.where(low, near_kept, far_kept)
    kept[HALF : 2 * HALF, :] = jnp.where(low, far_kept, near_kept)
    renorm(at, far_same, far_other, gain, normed)
    totals = [jnp.zeros((2 * HALF, FC), F32) for _ in range(4)]
    multiply(at, near, normed, (mine, core), 0, totals)
    for i in range(4):
        out[i] = totals[i]


def down_kernel(near, far, before, mine, mine_lo, core, core_lo, keep, to_y, to_z, to_both):
    at = place()
    low_y, low_z = at[1] == 0, at[3] == 0
    totals = [before[i] for i in range(4)]
    multiply(at, near, far, (mine_lo, core_lo), 1, totals)
    units = []
    for i in range(2):
        gate = totals[2 * i]
        part = (gate / (1.0 + jnp.exp(-gate)) * totals[2 * i + 1]).astype(BF)
        first, second = part[0:HALF, :], part[HALF : 2 * HALF, :]
        units.append(jnp.concatenate([jnp.where(low_y, first, second), jnp.where(low_y, second, first)], axis=0))
    for x in range(4):
        for side, pair in enumerate(((mine, core), (mine_lo, core_lo))):
            total = jnp.zeros((128, RUN), F32)
            for i, w in enumerate(pair):
                total = total + jnp.dot(units[i], w[x, 2 * FC : 3 * FC, :], preferred_element_type=F32)
            g = jnp.bitwise_xor(at[6], side) * 4 + x
            blocks = [total[:, k * 128 : (k + 1) * 128] for k in range(4)]
            same = [jnp.where(low_z, blocks[k], blocks[2 + k]) for k in range(2)]
            other = [jnp.where(low_z, blocks[2 + k], blocks[k]) for k in range(2)]
            keep[g] = jnp.where(low_y, same[0], same[1])
            to_y[g] = jnp.where(low_y, same[1], same[0]).astype(BF)
            to_z[g] = jnp.where(low_y, other[0], other[1]).astype(BF)
            to_both[g] = jnp.where(low_y, other[1], other[0]).astype(BF)


def add_kernel(keep, *refs):
    out = refs[-1]
    for i in range(8):
        total = keep[i]
        for got in refs[:-1]:
            total = total + got[i].astype(F32)
        out[i] = total.astype(BF)


def finish_kernel(got, kept, keep, give):
    at = place()
    total = kept[...].astype(F32)
    for i in range(8):
        total = total + got[i].astype(F32)
    result = total.T
    head, tail = result[0:QC, :], result[QC : 2 * QC, :]
    keep[...] = jnp.where(at[0] == 0, head, tail).astype(BF)
    give[...] = jnp.where(at[0] == 0, tail, head).astype(BF)


def pack_kernel(query, key, value, out_part, out, token, held, sems):
    token[...] = jnp.zeros_like(token)
    spans = ((query, 0, QC), (key, QC, KC), (value, QC + KC, KC), (out_part, 96, QC))
    reads = [
        pltpu.make_async_copy(ref, held.at[pl.ds(start, rows), :], sems.at[i])
        for i, (ref, start, rows) in enumerate(spans)
    ]
    for copy in reads:
        copy.start()
    for copy in reads:
        copy.wait()
    writes = [pltpu.make_async_copy(held, out.at[g], sems.at[4 + g]) for g in range(GROUPS)]
    for copy in writes:
        copy.start()
    for copy in writes:
        copy.wait()


def norm_kernel(after, tables, stream, gain, normed, own, held, gains, sems):
    at = place()
    copies = [
        pltpu.make_async_copy(stream, held, sems.at[0]),
        pltpu.make_async_copy(gain, gains, sems.at[1]),
    ]
    for copy in copies:
        copy.start()
    for copy in copies:
        copy.wait()
    x = held[...].astype(F32)
    scale = lax.rsqrt(jnp.mean(x * x, axis=-1, keepdims=True) + 1e-05)
    for g in range(GROUPS):
        cols = pl.ds(g * RUN, RUN)
        normed[g] = (held[:, cols].astype(F32) * scale * gains[:, cols]).astype(BF)
    rows = pl.ds(pl.multiple_of(at[0] * 128 + at[1] * HALF, HALF), HALF)
    own[...] = held[rows, pl.ds(pl.multiple_of(at[2] * BAND, BAND), BAND)]


def norm(after, tables, stream, gain):
    return pl.pallas_call(
        norm_kernel,
        out_shape=(jax.ShapeDtypeStruct((GROUPS, 256, RUN), BF), jax.ShapeDtypeStruct((HALF, BAND), BF)),
        in_specs=[ANY, ANY, HBM, HBM],
        out_specs=(VMEM,) * 2,
        scratch_shapes=[pltpu.VMEM((256, D), BF), pltpu.VMEM((1, D), F32), pltpu.SemaphoreType.DMA((2,))],
        compiler_params=params(24),
        name="norm",
    )(after, tables, stream, gain)


def join_kernel(after, gate, up, narrow, out, token, held, sems):
    token[...] = jnp.zeros_like(token)
    copies = [
        pltpu.make_async_copy(part, held.at[pl.ds(i * FC, FC), :], sems.at[i])
        for i, part in enumerate((gate, up, narrow))
    ]
    for copy in copies:
        copy.start()
    for copy in copies:
        copy.wait()
    whole_copy = pltpu.make_async_copy(held, out, sems.at[3])
    whole_copy.start()
    whole_copy.wait()


def join(after, *parts):
    return pl.pallas_call(
        join_kernel,
        out_shape=(jax.ShapeDtypeStruct((3 * FC, RUN), BF), jax.ShapeDtypeStruct((8, 128), F32)),
        in_specs=[ANY, HBM, HBM, HBM],
        out_specs=(HBM, VMEM),
        scratch_shapes=[pltpu.VMEM((3 * FC, RUN), BF), pltpu.SemaphoreType.DMA((4,))],
        compiler_params=params(60),
        name="join",
    )(after, *parts)


def pack(*parts):
    return pl.pallas_call(
        pack_kernel,
        out_shape=(jax.ShapeDtypeStruct((GROUPS, 160, RUN), BF), jax.ShapeDtypeStruct((8, 128), F32)),
        in_specs=[HBM] * 4,
        out_specs=(HBM, VMEM),
        scratch_shapes=[pltpu.VMEM((160, RUN), BF), pltpu.SemaphoreType.DMA((4 + GROUPS,))],
        compiler_params=params(60),
        name="pack",
    )(*parts)


def project(normed, weights, cos, sin):
    return pl.pallas_call(
        project_kernel,
        out_shape=(
            jax.ShapeDtypeStruct((8, HALF, 128), BF),
            jax.ShapeDtypeStruct((KC, 256), BF),
            jax.ShapeDtypeStruct((KC, 256), BF),
            jax.ShapeDtypeStruct((GROUPS, QC, RUN), BF),
        ),
        in_specs=[HBM] * 4,
        out_specs=(VMEM,) * 4,
        scratch_shapes=[
            pltpu.VMEM((GROUPS, 256, RUN), BF),
            pltpu.VMEM((GROUPS, 96, RUN), BF),
            pltpu.VMEM((2, 256, 128), F32),
            pltpu.SemaphoreType.DMA((3 * GROUPS + 2,)),
        ],
        compiler_params=params(58),
        name="project",
    )(normed, weights, cos, sin)


def attend(lengths, got):
    return pl.pallas_call(
        attend_kernel,
        out_shape=jax.ShapeDtypeStruct((HALF, BAND), BF),
        in_specs=[SMEM, VMEM],
        out_specs=VMEM,
        compiler_params=params(16),
        name="attend",
    )(lengths, got)


def output(got, weights, own):
    return pl.pallas_call(
        output_kernel,
        out_shape=jax.ShapeDtypeStruct((8, HALF, BAND), BF),
        in_specs=[VMEM] * 6,
        out_specs=VMEM,
        compiler_params=params(24),
        name="output",
    )(got, *weights, own)


def near_half(same, other, gain):
    return pl.pallas_call(
        near_kernel,
        out_shape=jax.ShapeDtypeStruct((GROUPS, HALF, RUN), BF),
        in_specs=[VMEM] * 3,
        out_specs=VMEM,
        compiler_params=params(16),
        name="near_half",
    )(same, other, gain)


def own_rows(near, same, far_same, far_other, gain, mine, core):
    return pl.pallas_call(
        own_rows_kernel,
        out_shape=(
            jax.ShapeDtypeStruct((4, 128, FC), F32),
            jax.ShapeDtypeStruct((128, 128), BF),
            jax.ShapeDtypeStruct((GROUPS, HALF, RUN), BF),
        ),
        in_specs=[VMEM] * 7,
        out_specs=(VMEM,) * 3,
        compiler_params=params(16),
        cost_estimate=cost(2 * HALF * D * 4 * FC, 4 * 2**20),
        name="own_rows",
    )(near, same, far_same, far_other, gain, mine, core)


def down(near, far, before, weights):
    part = jax.ShapeDtypeStruct((8, 128, 128), BF)
    return pl.pallas_call(
        down_kernel,
        out_shape=(jax.ShapeDtypeStruct((8, 128, 128), F32), part, part, part),
        in_specs=[VMEM] * 7,
        out_specs=(VMEM,) * 4,
        compiler_params=params(16),
        cost_estimate=cost(4 * HALF * D * 4 * FC, 9 * 2**20),
        name="down",
    )(near, far, before, *weights)


def add(*parts):
    return pl.pallas_call(
        add_kernel,
        out_shape=jax.ShapeDtypeStruct((8, 128, 128), BF),
        in_specs=[VMEM] * 4,
        out_specs=VMEM,
        compiler_params=params(16),
        name="add",
    )(*parts)


def finish(got, kept):
    return pl.pallas_call(
        finish_kernel,
        out_shape=(jax.ShapeDtypeStruct((QC, 128), BF),) * 2,
        in_specs=[VMEM] * 2,
        out_specs=(VMEM, VMEM),
        compiler_params=params(16),
        name="finish",
    )(got, kept)


def swap(x, bits):
    return lax.ppermute(x, "dev", [(d, d ^ bits) for d in range(MEMBERS)])


def swap_groups(x):
    return lax.ppermute(x, "grp", [(g, g ^ 4) for g in range(GROUPS)])


def collect_x(x):
    return lax.all_gather(x, "grp", axis=0, axis_index_groups=[[0, 1, 2, 3], [4, 5, 6, 7]])


def trade(x, groups):
    return lax.all_to_all(x, "dev", 0, 0, axis_index_groups=groups, tiled=True)


def collect(x):
    return lax.all_gather(x, "dev", axis=0, axis_index_groups=COLUMNS)


def after(x, other):
    return lax.optimization_barrier((x, other))[0]


def on_device(
    stream,
    row_length,
    row_start,
    attn_gain,
    w_query,
    w_key,
    w_value,
    w_out,
    ffn_gain,
    w_gate,
    w_up,
    w_down,
):
    member = lax.axis_index("dev")
    core = member % 2

    packed, token = pack(w_query.T, w_key.T, w_value.T, w_out.T)
    first = lax.all_to_all(packed, "grp", 0, 0, tiled=True)

    lane = jnp.arange(128, dtype=jnp.int32)
    column = jnp.where(lane < QC, member * QC + lane, member * KC + lane - QC)
    pair = (column % HEAD_DIM // 2).astype(F32)
    freq = jnp.exp(-(2.0 * pair / HEAD_DIM) * math.log(ROPE_BASE))
    positions = (row_start[:, None] + jnp.arange(ROW_LEN, dtype=jnp.int32)[None, :]).reshape(-1)
    angle = positions.astype(F32)[:, None] * freq[None, :]
    cos, sin = jnp.cos(angle), jnp.sin(angle)

    mine, token = join(token, w_gate.T, w_up.T, w_down.T)
    normed, own = norm(token, cos, stream, attn_gain.reshape(1, D))
    send, keys, values, out_own = project(normed, first, cos, sin)
    got = trade(send, OCTETS)
    mine = after(mine, send)
    mine_lo = swap_groups(after(mine, got))
    out_weights = (out_own, swap(out_own, 1), swap(out_own, 2), swap(out_own, 3))
    mixed = collect(attend(row_length, got))
    attended = output(mixed, out_weights, own)
    mine, mine_lo = collect_x(mine), collect_x(after(mine_lo, attended))
    mine = after(mine, attended)
    core_mine = swap(mine, 1)
    same = trade(attended, PARITIES)
    other, far_same, far_other = swap(same, 4), swap(same, 2), swap(same, 6)
    gain = ffn_gain.reshape(1, D)
    near = near_half(same, other, gain)
    mine_lo = after(mine_lo, (far_same, far_other, other))
    core_lo = swap(mine_lo, 1)
    totals, kept, far_normed = own_rows(near, same, far_same, far_other, gain, mine, core_mine)
    weights = (mine, mine_lo, core_mine, core_lo)
    keep, to_y, to_z, to_both = down(near, far_normed, totals, weights)
    sums = trade(add(keep, swap(to_both, 6), swap(to_y, 2), swap(to_z, 4)), PARITIES)
    keep, give = finish(sums, kept)
    give = swap(give, 1)
    rows = jnp.where(core == 0, jnp.concatenate([keep, give], axis=1), jnp.concatenate([give, keep], axis=1))
    return (keys.T, values.T, rows.T)


def solution(mesh):
    placed = (
        P("grp", None),
        P("grp"),
        P("grp"),
        P(),
        P("grp", "dev"),
        P("grp", "dev"),
        P("grp", "dev"),
        P("grp", "dev"),
        P(),
        P("grp", "dev"),
        P("grp", "dev"),
        P("grp", "dev"),
    )
    return jax.shard_map(
        on_device,
        mesh=mesh,
        in_specs=placed,
        out_specs=(P("grp", "dev"), P("grp", "dev"), P("grp", "dev")),
        check_vma=False,
    )
```
